32 devices in a mesh: atom: 16 (over z, y, x), chan: 2 (over core).
Axes of the slice: x: 2, y: 2, z: 4, core: 2. Of those that a mesh axis runs over, the one named last changes fastest.
Arguments:
- features: bfloat16 [128, 49, 4096], P('chan', None, 'atom'), may hold values from -6 to 6
- weights: bfloat16 [3, 7, 128, 128], P(None, None, None, 'chan'), may hold values from -2 to 2
- cotangent: bfloat16 [128, 49, 4096], P('chan', None, 'atom'), may hold values from -6 to 6
- edge_bias: float32 [8, 16, 4096], P('chan', None, 'atom'), may hold values from -5 to 5
- neighbours: int32 [16, 4096], P(None, 'atom'), may hold values from 0 to 4095, as said below
- valid_mask: int32 [16, 4096], P(None, 'atom'), may hold values from 0 to 1, as said below
Outputs:
- grad_features: bfloat16 [128, 49, 4096], P('chan', None, 'atom')
- grad_weights: float32 [3, 7, 128, 128], P(None, None, None, 'chan')
- grad_bias: float32 [8, 16, 4096], P('chan', None, 'atom')
The draws below stay inside these ranges and needn't reach their ends.
Inputs may be any that keep to these rules, and one draw needn't show every extreme that they name: neighbours[s, a] = (a + o) mod 4096 with -128 <= o <= 128; offsets of -128 and 128 both occur, and slot 0 always holds (a - 1) mod 4096. `valid_mask`: slot 0 of every atom is valid; the share of valid slots rises along the atom order from about a quarter to nearly all.
All inputs are finite; a program needn't handle non-finite values.
Results may differ from the reference program's by a relative error of at most 0.005.
The reference program's roundings to bfloat16 on the way (of `projected` and `grads`) count: a program that leaves them out, or rounds other values in their place, can miss the bound.
Values may be sent and summed in bfloat16 or wider, within the bound.
No kernel may reach another device: no remote copies, remote signals or barrier semaphores. Data moves between devices by JAX's collectives and lax.ppermute only.
A program may use at most 128 MiB of HBM per device.

```python
import jax
import jax.numpy as jnp
from jax import lax

LMAX = 6
M = 49
C = 128
H = 8
K = 16
HALO = 128
ATOMS = 4096


def draw_neighbours(key, part):
    atom_ids = jnp.arange(ATOMS, dtype=jnp.int32)[None, :]
    slot_ids = jnp.arange(K, dtype=jnp.int32)[:, None]
    offsets = jax.random.randint(key, (K, ATOMS), -HALO, HALO + 1).astype(jnp.int32)
    offsets = jnp.where(slot_ids == 0, -1, offsets)
    offsets = jnp.where((slot_ids == 1) & (atom_ids % 8 == 0), -HALO, offsets)
    offsets = jnp.where((slot_ids == 1) & (atom_ids % 8 == 4), HALO, offsets)
    return ((atom_ids + offsets) % ATOMS).astype(jnp.int32)


def draw_valid_mask(key, part):
    atom_ids = jnp.arange(ATOMS, dtype=jnp.int32)[None, :]
    slot_ids = jnp.arange(K, dtype=jnp.int32)[:, None]
    levels = 2 + 6 * atom_ids // ATOMS
    rolled = jax.random.randint(key, (K, ATOMS), 0, 8).astype(jnp.int32)
    live_slots = jnp.where(rolled < levels, 1, 0)
    return jnp.where(slot_ids == 0, 1, live_slots).astype(jnp.int32)


def draw_weights(key, part):
    shape = (3, LMAX + 1, C, C)
    base = jax.random.normal(key, shape, jnp.float32)
    factor = jnp.array([3.0, 3.0, 1.0], jnp.float32).reshape(3, 1, 1, 1)
    values = jnp.clip(base * factor / jnp.sqrt(jnp.float32(C)), -2.0, 2.0)
    return values.astype(jnp.bfloat16)


def block_levels(own_key, extent, split, least, high):
    def one(axis_at, blocks):
        draws = jax.random.uniform(jax.random.fold_in(jax.random.fold_in(own_key, 6), axis_at), (blocks,), jnp.float32, least / len(split), high / len(split))
        return jnp.repeat(jnp.exp(draws), extent[axis_at] // blocks).reshape((-1,) + (1,) * (len(extent) - axis_at - 1))

    level = one(*split[0])
    for cut in split[1:]:
        level = level * one(*cut)
    return level


def scatter_about(own_key, extent, deviation, reach, split=(), kind=jnp.bfloat16):
    result = deviation * jax.random.normal(own_key, extent, jnp.float32)
    if split:
        result = result * block_levels(own_key, extent, split, -0.22, 0.18)
    return jnp.clip(result, -reach, reach).astype(kind)


def setup_inputs(seed: int = 0) -> dict:
    key_of = jax.random.split(jax.random.key(seed), 7)
    return {
        "features": scatter_about(key_of[0], (C, M, ATOMS), 1.0, 6.0, ((0, 2), (2, 16))),
        "weights": draw_weights(jax.random.fold_in(key_of[6], 71), 0),
        "cotangent": scatter_about(key_of[2], (C, M, ATOMS), 1.0, 6.0, ((0, 2), (2, 16))),
        "edge_bias": scatter_about(key_of[3], (H, K, ATOMS), 1.0, 5.0, ((0, 2), (2, 16)), jnp.float32),
        "neighbours": draw_neighbours(jax.random.fold_in(key_of[6], 71), 0),
        "valid_mask": draw_valid_mask(jax.random.fold_in(key_of[6], 71), 0),
    }


soft_cap = 10.0


def degree_bounds():
    return [(degree * degree, (degree + 1) * (degree + 1)) for degree in range(LMAX + 1)]


def reference(features, weights, cotangent, edge_bias, neighbours, valid_mask):
    head_rows = (C // H) * M
    score_scale = 1.0 / (head_rows ** 0.5)
    feature_f = features.astype(jnp.float32)
    weight_f = weights.astype(jnp.float32)
    projected = jnp.concatenate(
        [jnp.einsum("cma,gcd->gdma", feature_f[:, low_comp:high_comp], weight_f[:, degree])
         for degree, (low_comp, high_comp) in enumerate(degree_bounds())], axis=2)
    projected = projected.astype(jnp.bfloat16)
    head_view = projected.reshape(3, H, head_rows, ATOMS)
    grad_out = cotangent.reshape(H, head_rows, ATOMS)
    live_slots = valid_mask > 0
    flat_index = neighbours.reshape(-1)

    def one_head(head_items):
        query_h, keys_h, values_h, grad_h, bias_h = head_items
        query_f = query_h.astype(jnp.float32)
        grad_f = grad_h.astype(jnp.float32)
        key_edges = keys_h[:, neighbours].astype(jnp.float32)
        value_edges = values_h[:, neighbours].astype(jnp.float32)
        raw_score = score_scale * jnp.einsum("fa,fka->ka", query_f, key_edges)
        squashed = jnp.tanh(raw_score / soft_cap)
        logits = soft_cap * squashed + bias_h
        exp_logit = jnp.where(live_slots, jnp.exp(logits), jnp.float32(0.0))
        attention = exp_logit / jnp.sum(exp_logit, axis=0, keepdims=True)
        grad_attn = jnp.einsum("fa,fka->ka", grad_f, value_edges)
        grad_logit = attention * (grad_attn - jnp.sum(attention * grad_attn, axis=0, keepdims=True))
        grad_raw = score_scale * grad_logit * (1.0 - squashed * squashed)
        grad_query = jnp.einsum("ka,fka->fa", grad_raw, key_edges)
        key_terms = (grad_raw[None] * query_f[:, None, :]).reshape(head_rows, -1)
        value_terms = (attention[None] * grad_f[:, None, :]).reshape(head_rows, -1)
        both_terms = jnp.stack([key_terms, value_terms])
        scattered = jnp.zeros((2, head_rows, ATOMS), jnp.float32).at[:, :, flat_index].add(both_terms)
        return grad_query, scattered, grad_logit

    grad_query, scattered, grad_logit = lax.map(
        one_head, (head_view[0], head_view[1], head_view[2], grad_out, edge_bias))
    grads = jnp.stack([grad_query, scattered[:, 0], scattered[:, 1]]).astype(jnp.bfloat16)
    grads_f = grads.reshape(3, C, M, ATOMS).astype(jnp.float32)
    grad_weights = jnp.stack(
        [jnp.einsum("cma,gdma->gcd", feature_f[:, low_comp:high_comp], grads_f[:, :, low_comp:high_comp])
         for low_comp, high_comp in degree_bounds()], axis=1)
    grad_features = jnp.concatenate(
        [jnp.einsum("gcd,gdma->cma", weight_f[:, degree], grads_f[:, :, low_comp:high_comp])
         for degree, (low_comp, high_comp) in enumerate(degree_bounds())], axis=1)
    return grad_features.astype(jnp.bfloat16), grad_weights, grad_logit
```

```python
import functools
import math

import jax
import jax.numpy as jnp
from jax import lax
from jax.experimental import pallas as pl
from jax.experimental.pallas import tpu as pltpu
from jax.sharding import PartitionSpec as P

LMAX = 6
HALO = 128
SOFT_CAP = 10.0
F32 = jnp.float32
BF16 = jnp.bfloat16


def degree_of(comp):
    return math.isqrt(comp)


def nn(lhs, rhs):
    return lax.dot_general(lhs, rhs, (((1,), (0,)), ((), ())), preferred_element_type=F32)


def nt(lhs, rhs):
    return lax.dot_general(lhs, rhs, (((1,), (1,)), ((), ())), preferred_element_type=F32)


def tn(lhs, rhs):
    return lax.dot_general(lhs, rhs, (((0,), (0,)), ((), ())), preferred_element_type=F32)


def pick(table, index):
    return jnp.take_along_axis(table, index, axis=1, mode="promise_in_bounds")


def head_rows_of(ref, first_row, rows):
    block = ref[:, first_row : first_row + rows, :]
    return block.reshape(block.shape[0] * rows, block.shape[2])


def slot_tile(window_index, tile):
    atoms, slots = window_index.shape
    lane = lax.broadcasted_iota(jnp.int32, (atoms, HALO), 1) + tile * HALO
    found = jnp.full((atoms, HALO), -1, jnp.int32)
    for slot in range(slots):
        found = jnp.where(window_index[:, slot : slot + 1] == lane, slot, found)
    return found


def spread(slot, coef, quantity, slots):
    values = pick(coef, jnp.maximum(slot, 0) + quantity * slots)
    return jnp.where(slot >= 0, values, 0.0).astype(BF16)


def own_kernel(heads, fa, fb, oa, ob, ca, cb, wp, own_index, left_index, right_index,
               qkv, scores, slot_own, slot_left, slot_right):
    comps, chan_local = fa.shape[0], fa.shape[1]
    rows = chan_local // heads
    for comp in range(comps):
        feats = jnp.concatenate(
            [
                jnp.concatenate([fa[comp], fb[comp]], axis=1),
                jnp.concatenate([oa[comp], ob[comp]], axis=1),
            ],
            axis=0,
        )
        qkv[comp] = nn(wp[degree_of(comp)], feats).astype(BF16)
    for head in range(heads):
        query = head_rows_of(qkv, head * rows, rows)
        key = head_rows_of(qkv, chan_local + head * rows, rows)
        value = head_rows_of(qkv, 2 * chan_local + head * rows, rows)
        cot = jnp.concatenate(
            [head_rows_of(ca, head * rows, rows), head_rows_of(cb, head * rows, rows)], axis=1
        )
        scores[head] = tn(query, key)
        scores[heads + head] = tn(cot, value)
    for half in range(2):
        index = own_index[half * HALO : (half + 1) * HALO, :]
        for tile in range(3):
            slot_own[half, tile] = slot_tile(index, tile)
    slot_left[...] = slot_tile(left_index[...], 2)
    slot_right[...] = slot_tile(right_index[...], 0)


def edge_kernel(heads, slots, score_scale, flm, flo, frm, fro, wp, qkv, ca, cb, scores, bias, valid,
                index_rows, index_wide, halo_qkv, grad_bias, coef):
    comps, chan_local = flm.shape[0], flm.shape[1]
    rows = chan_local // heads
    for comp in range(comps):
        feats = jnp.concatenate(
            [
                jnp.concatenate([flm[comp], frm[comp]], axis=1),
                jnp.concatenate([flo[comp], fro[comp]], axis=1),
            ],
            axis=0,
        )
        halo_qkv[comp] = nn(wp[degree_of(comp)], feats).astype(BF16)
    lane = lax.broadcasted_iota(jnp.int32, (HALO, 2 * heads * slots), 1)
    gathered = [jnp.zeros((HALO, 2 * heads * slots), F32) for _ in range(2)]
    for quantity in range(2 * heads):
        head = quantity % heads
        if quantity < heads:
            mine = head_rows_of(qkv, head * rows, rows)
            theirs = head_rows_of(halo_qkv, chan_local + head * rows, rows)
        else:
            mine = jnp.concatenate(
                [head_rows_of(ca, head * rows, rows), head_rows_of(cb, head * rows, rows)], axis=1
            )
            theirs = head_rows_of(halo_qkv, 2 * chan_local + head * rows, rows)
        left = tn(mine[:, :HALO], theirs[:, :HALO])
        right = tn(mine[:, HALO:], theirs[:, HALO:])
        for half in range(2):
            own = scores[quantity, half * HALO : (half + 1) * HALO, :]
            own = [own[:, :HALO], own[:, HALO:]]
            tiles = [left] + own if half == 0 else own + [right]
            index = index_wide[half * HALO : (half + 1) * HALO, :]
            inner, tile_of = index & (HALO - 1), index >> 7
            values = jnp.where(
                tile_of == 0,
                pick(tiles[0], inner),
                jnp.where(tile_of == 1, pick(tiles[1], inner), pick(tiles[2], inner)),
            )
            gathered[half] = jnp.where(lane // slots == quantity, values, gathered[half])
    for half in range(2):
        span = slice(half * HALO, (half + 1) * HALO)
        edges = gathered[half].T.reshape(2, heads, slots, HALO)
        squashed = jnp.tanh(edges[0] * (score_scale / SOFT_CAP))
        logits = SOFT_CAP * squashed + bias[:, :, span]
        live = valid[:, span][None] > 0
        weight = jnp.where(live, jnp.exp(logits), 0.0)
        attention = weight / jnp.sum(weight, axis=1, keepdims=True)
        grad_attn = edges[1]
        grad_logit = attention * (
            grad_attn - jnp.sum(attention * grad_attn, axis=1, keepdims=True)
        )
        grad_bias[:, :, span] = grad_logit
        grad_raw = score_scale * grad_logit * (1.0 - squashed * squashed)
        index = index_rows[:, span]
        both = jnp.stack([grad_raw, attention]).reshape(2 * heads, slots, HALO)
        merged = jnp.zeros_like(both)
        for slot in range(slots):
            same = (index == index[slot : slot + 1, :])[None]
            merged = merged + jnp.where(same, both[:, slot : slot + 1, :], 0.0)
        coef[span, :] = merged.reshape(2 * heads * slots, HALO).T.astype(BF16)


def grads_kernel(heads, slots, fa, fb, oa, ob, flm, flo, frm, fro, qkv, halo_qkv, ca, cb, slot_own,
                 coef, grad_query, own_key, own_value, weight_terms, ext):
    comps, chan_local = fa.shape[0], fa.shape[1]
    rows = chan_local // heads
    atoms = 2 * HALO
    empty = jnp.zeros((HALO, HALO), BF16)
    for head in range(heads):
        tables = []
        for quantity in (head, heads + head):
            halves = []
            for half in range(2):
                table = coef[half * HALO : (half + 1) * HALO, :].astype(F32)
                tiles = [spread(slot_own[half, tile], table, quantity, slots) for tile in range(3)]
                tiles = tiles + [empty] if half == 0 else [empty] + tiles
                halves.append(jnp.concatenate(tiles, axis=1))
            tables.append(jnp.concatenate(halves, axis=0))
        raw_table, attn_table = tables
        query = head_rows_of(qkv, head * rows, rows)
        key = head_rows_of(qkv, chan_local + head * rows, rows)
        halo_key = head_rows_of(halo_qkv, chan_local + head * rows, rows)
        cot = jnp.concatenate(
            [head_rows_of(ca, head * rows, rows), head_rows_of(cb, head * rows, rows)], axis=1
        )
        key_ext = jnp.concatenate([halo_key[:, :HALO], key, halo_key[:, HALO:]], axis=1)
        span = slice(head * rows, (head + 1) * rows)
        value_span = slice(chan_local + head * rows, chan_local + (head + 1) * rows)
        grad_query[:, span, :] = nt(key_ext, raw_table).astype(BF16).reshape(comps, rows, atoms)
        key_sums = nn(query, raw_table)
        own_key[:, span, :] = key_sums[:, HALO : HALO + atoms].reshape(comps, rows, atoms)
        ext[:, span, :] = key_sums.astype(BF16).reshape(comps, rows, atoms + 2 * HALO)
        value_sums = nn(cot, attn_table)
        own_value[:, span, :] = value_sums[:, HALO : HALO + atoms].reshape(comps, rows, atoms)
        ext[:, value_span, :] = value_sums.astype(BF16).reshape(comps, rows, atoms + 2 * HALO)
    for degree in range(LMAX + 1):
        query_total = jnp.zeros((chan_local, 2 * chan_local), F32)
        keyval_total = jnp.zeros((2 * chan_local, 2 * chan_local), F32)
        for comp in range(degree * degree, (degree + 1) * (degree + 1)):
            own = jnp.concatenate(
                [
                    jnp.concatenate([fa[comp], fb[comp]], axis=1),
                    jnp.concatenate([oa[comp], ob[comp]], axis=1),
                ],
                axis=0,
            )
            wide = jnp.concatenate(
                [
                    jnp.concatenate([flm[comp], fa[comp], fb[comp], frm[comp]], axis=1),
                    jnp.concatenate([flo[comp], oa[comp], ob[comp], fro[comp]], axis=1),
                ],
                axis=0,
            )
            query_total = query_total + nt(grad_query[comp], own)
            keyval_total = keyval_total + nt(ext[comp], wide)
        weight_terms[degree, :chan_local, :] = query_total
        weight_terms[degree, chan_local:, :] = keyval_total


def key_kernel(heads, slots, grad_query, own_key, halo_qkv, coef_left, coef_right, slot_left,
               slot_right, wc, terms, grad):
    comps, chan_local = grad_query.shape[0], grad_query.shape[1]
    rows = chan_local // heads
    grad[:, :chan_local, :] = grad_query[...]
    left, right = coef_left[...].astype(F32), coef_right[...].astype(F32)
    for head in range(heads):
        query = head_rows_of(halo_qkv, head * rows, rows)
        rim = jnp.concatenate(
            [
                nn(query[:, :HALO], spread(slot_left[...], left, head, slots)),
                nn(query[:, HALO:], spread(slot_right[...], right, head, slots)),
            ],
            axis=1,
        )
        total = head_rows_of(own_key, head * rows, rows) + rim
        span = slice(chan_local + head * rows, chan_local + (head + 1) * rows)
        grad[:, span, :] = total.astype(BF16).reshape(comps, rows, 2 * HALO)
    for comp in range(comps):
        terms[comp] = nn(wc[degree_of(comp)][:, : 2 * chan_local], grad[comp])


def value_kernel(heads, slots, own_value, cl, cr, coef_left, coef_right, slot_left, slot_right, wc,
                 terms, mine, theirs, grad):
    comps, chan_local = own_value.shape[0], own_value.shape[1]
    rows = chan_local // heads
    left, right = coef_left[...].astype(F32), coef_right[...].astype(F32)
    for head in range(heads):
        rim = jnp.concatenate(
            [
                nn(head_rows_of(cl, head * rows, rows),
                   spread(slot_left[...], left, heads + head, slots)),
                nn(head_rows_of(cr, head * rows, rows),
                   spread(slot_right[...], right, heads + head, slots)),
            ],
            axis=1,
        )
        total = head_rows_of(own_value, head * rows, rows) + rim
        span = slice(head * rows, (head + 1) * rows)
        grad[:, span, :] = total.astype(BF16).reshape(comps, rows, 2 * HALO)
    for comp in range(comps):
        total = terms[comp] + nn(wc[degree_of(comp)][:, 2 * chan_local :], grad[comp])
        mine[comp] = total[:chan_local]
        theirs[comp] = total[chan_local:].astype(BF16)


def call(kernel, args, outs, scratch=(), flops=0):
    whole = pl.BlockSpec(memory_space=pltpu.VMEM)
    moved = sum(math.prod(a.shape) * a.dtype.itemsize for a in list(args) + list(outs))
    return pl.pallas_call(
        kernel,
        out_shape=tuple(outs),
        in_specs=[whole] * len(args),
        out_specs=tuple([whole] * len(outs)),
        scratch_shapes=list(scratch),
        compiler_params=pltpu.CompilerParams(vmem_limit_bytes=56 * 1024 * 1024),
        cost_estimate=pl.CostEstimate(flops=flops, bytes_accessed=moved, transcendentals=0),
    )(*args)


def shifted(value, axis, steps):
    count = lax.axis_size(axis)
    pairs = [(source, (source + steps) % count) for source in range(count)]
    return lax.ppermute(value, axis, pairs)


def summed_over(value, axis):
    count = lax.axis_size(axis)
    if count & (count - 1):
        return lax.psum(value, axis)
    place = lax.axis_index(axis)
    bits = list(reversed(range(count.bit_length() - 1)))
    halved = []
    for at, bit in enumerate(bits):
        pairs = [(source, source ^ (1 << bit)) for source in range(count)]
        upper = (place >> bit) & 1
        half = value.shape[1] // 2
        if at < len(bits) - 1 and value.shape[1] % 16 == 0 and half >= 24:
            low, high = value[:, :half], value[:, half:]
            keep = jnp.where(upper == 1, high, low)
            send = jnp.where(upper == 1, low, high)
            if at == 0:
                send = send.astype(BF16)
            value = keep + lax.ppermute(send, axis, pairs).astype(F32)
            halved.append((bit, pairs))
        else:
            value = value + lax.ppermute(value, axis, pairs)
    value = value.astype(BF16)
    for bit, pairs in reversed(halved):
        upper = (place >> bit) & 1
        other = lax.ppermute(value, axis, pairs)
        value = jnp.concatenate(
            [jnp.where(upper == 1, other, value), jnp.where(upper == 1, value, other)], axis=1
        )
    return value.astype(F32)


def on_device(features, weights, cotangent, edge_bias, neighbours, valid_mask):
    chan_local, comps, atoms_dev = features.shape
    heads, slots = edge_bias.shape[0], edge_bias.shape[1]
    channels = weights.shape[2]
    assert atoms_dev == 2 * HALO and channels == 2 * chan_local
    score_scale = 1.0 / math.sqrt(chan_local // heads * comps)
    total_atoms = atoms_dev * lax.axis_size("atom")
    first_atom = lax.axis_index("atom") * atoms_dev
    core = lax.axis_index("chan")

    def shape(*dims, dtype=F32):
        return jax.ShapeDtypeStruct(dims, dtype)

    def halves(array):
        return (
            jnp.transpose(array[:, :, :HALO], (1, 0, 2)),
            jnp.transpose(array[:, :, HALO:], (1, 0, 2)),
        )

    fa, fb = halves(features)
    ca, cb = halves(cotangent)
    flm = shifted(fb, "atom", 1)
    frm = shifted(fa, "atom", -1)
    oa = shifted(fa, "chan", 1)
    ob = shifted(fb, "chan", 1)
    flo = shifted(flm, "chan", 1)
    fro = shifted(frm, "chan", 1)
    ca_out, cb_out, flm, frm = lax.optimization_barrier((ca, cb, flm, frm))
    cl = shifted(cb_out, "atom", 1)
    cr = shifted(ca_out, "atom", -1)

    atom_ids = first_atom + jnp.arange(atoms_dev, dtype=jnp.int32)
    half_start = atom_ids - jnp.arange(atoms_dev, dtype=jnp.int32) % HALO
    window = (neighbours - half_start[None] + HALO + total_atoms) % total_atoms
    left_index = shifted(window[:, HALO:], "atom", 1)
    right_index = shifted(window[:, :HALO], "atom", -1)
    window_t = window.T
    window_wide = jnp.tile(window_t, (1, 2 * heads))

    swapped = jnp.where(core == 0, weights, jnp.roll(weights, chan_local, axis=2))
    wp = jnp.transpose(swapped, (1, 0, 3, 2)).reshape(LMAX + 1, 3 * chan_local, channels)
    wc = jnp.transpose(swapped, (1, 2, 0, 3)).reshape(LMAX + 1, channels, 3 * chan_local)

    rows = chan_local // heads * comps
    pair_flops = 2 * heads * rows * HALO * HALO
    mix_flops = 2 * comps * channels * 3 * chan_local * atoms_dev
    qkv, scores, slot_own, slot_left, slot_right = call(
        functools.partial(own_kernel, heads),
        (fa, fb, oa, ob, ca, cb, wp, window_t, left_index.T, right_index.T),
        (
            shape(comps, 3 * chan_local, atoms_dev, dtype=BF16),
            shape(2 * heads, atoms_dev, atoms_dev),
            shape(2, 3, HALO, HALO, dtype=jnp.int32),
            shape(HALO, HALO, dtype=jnp.int32),
            shape(HALO, HALO, dtype=jnp.int32),
        ),
        flops=mix_flops + 8 * pair_flops,
    )
    halo_qkv, grad_bias, coef = call(
        functools.partial(edge_kernel, heads, slots, score_scale),
        (flm, flo, frm, fro, wp, qkv, ca, cb, scores, edge_bias, valid_mask, window, window_wide),
        (
            shape(comps, 3 * chan_local, atoms_dev, dtype=BF16),
            shape(heads, slots, atoms_dev),
            shape(atoms_dev, 2 * heads * slots, dtype=BF16),
        ),
        flops=mix_flops + 4 * pair_flops,
    )
    coef_left = shifted(coef[HALO:], "atom", 1)
    coef_right = shifted(coef[:HALO], "atom", -1)
    grad_query, own_key, own_value, weight_terms = call(
        functools.partial(grads_kernel, heads, slots),
        (fa, fb, oa, ob, flm, flo, frm, fro, qkv, halo_qkv, ca, cb, slot_own, coef),
        (
            shape(comps, chan_local, atoms_dev, dtype=BF16),
            shape(comps, chan_local, atoms_dev),
            shape(comps, chan_local, atoms_dev),
            shape(LMAX + 1, 3 * chan_local, channels),
        ),
        scratch=[pltpu.VMEM((comps, 2 * chan_local, 2 * atoms_dev), BF16)],
        flops=24 * pair_flops + 2 * mix_flops,
    )
    grad_weights = summed_over(weight_terms, "atom")
    (terms,) = call(
        functools.partial(key_kernel, heads, slots),
        (grad_query, own_key, halo_qkv, coef_left, coef_right, slot_left, slot_right, wc),
        (shape(comps, channels, atoms_dev),),
        scratch=[pltpu.VMEM((comps, 2 * chan_local, atoms_dev), BF16)],
        flops=2 * pair_flops + mix_flops,
    )
    mine, theirs = call(
        functools.partial(value_kernel, heads, slots),
        (own_value, cl, cr, coef_left, coef_right, slot_left, slot_right, wc, terms),
        (
            shape(comps, chan_local, atoms_dev),
            shape(comps, chan_local, atoms_dev, dtype=BF16),
        ),
        scratch=[pltpu.VMEM((comps, chan_local, atoms_dev), BF16)],
        flops=2 * pair_flops + mix_flops // 2,
    )
    total = mine + shifted(theirs, "chan", 1).astype(F32)
    grad_features = jnp.transpose(total.astype(BF16), (1, 0, 2))
    grad_weights = grad_weights.reshape(LMAX + 1, 3, chan_local, channels)
    grad_weights = jnp.transpose(grad_weights, (1, 0, 3, 2))
    grad_weights = jnp.where(core == 0, grad_weights, jnp.roll(grad_weights, chan_local, axis=2))
    return grad_features, grad_weights, grad_bias


def solution(mesh):
    in_specs = (
        P("chan", None, "atom"),
        P(None, None, None, "chan"),
        P("chan", None, "atom"),
        P("chan", None, "atom"),
        P(None, "atom"),
        P(None, "atom"),
    )
    out_specs = (P("chan", None, "atom"), P(None, None, None, "chan"), P("chan", None, "atom"))
    return jax.shard_map(
        on_device, mesh=mesh, in_specs=in_specs, out_specs=out_specs, check_vma=False
    )
```

```python
import functools
import math

import jax
import jax.numpy as jnp
from jax import lax
from jax.experimental import pallas as pl
from jax.experimental.pallas import tpu as pltpu
from jax.sharding import PartitionSpec as P

LMAX = 6
HALO = 128
SOFT_CAP = 10.0
F32 = jnp.float32
BF16 = jnp.bfloat16


def degree_of(comp):
    return math.isqrt(comp)


def nn(lhs, rhs):
    return lax.dot_general(lhs, rhs, (((1,), (0,)), ((), ())), preferred_element_type=F32)


def nt(lhs, rhs):
    return lax.dot_general(lhs, rhs, (((1,), (1,)), ((), ())), preferred_element_type=F32)


def tn(lhs, rhs):
    return lax.dot_general(lhs, rhs, (((0,), (0,)), ((), ())), preferred_element_type=F32)


def pick(table, index):
    return jnp.take_along_axis(table, index, axis=1, mode="promise_in_bounds")


def head_rows_of(ref, first_row, rows):
    block = ref[:, first_row : first_row + rows, :]
    return block.reshape(block.shape[0] * rows, block.shape[2])


def slot_tile(window_index, tile):
    atoms, slots = window_index.shape
    lane = lax.broadcasted_iota(jnp.int32, (atoms, HALO), 1) + tile * HALO
    found = jnp.full((atoms, HALO), -1, jnp.int32)
    for slot in range(slots):
        found = jnp.where(window_index[:, slot : slot + 1] == lane, slot, found)
    return found


def spread(slot, coef, quantity, slots):
    values = pick(coef, jnp.maximum(slot, 0) + quantity * slots)
    return jnp.where(slot >= 0, values, 0.0).astype(BF16)


def wide_transpose(rows):
    return jnp.concatenate([rows] * (HALO // rows.shape[0]), axis=0).T


def own_kernel(heads, total_atoms, place, fm, fo, cot, weights, neighbours,
               qkv, scores, slot_own, index_rows, index_wide, wp, wc):
    comps, chan_local = fm.shape[0], fm.shape[1]
    channels = weights.shape[3]
    rows = chan_local // heads
    slots = neighbours.shape[0]
    core, first_atom = place[0], place[1]
    for degree in range(LMAX + 1):
        mix = jnp.concatenate([weights[g, degree] for g in range(3)], axis=0).astype(F32)
        mix = jnp.where(core == 0, mix, pltpu.roll(mix, chan_local, 1))
        wp[degree] = mix.astype(BF16)
        padded = jnp.concatenate([mix, jnp.zeros((chan_local, channels), F32)], axis=0)
        wc[degree] = padded.T[:, : 3 * chan_local].astype(BF16)
    for comp in range(comps):
        feats = jnp.concatenate([fm[comp], fo[comp]], axis=0)
        qkv[comp] = nn(wp[degree_of(comp)], feats).astype(BF16)
    for head in range(heads):
        query = head_rows_of(qkv, head * rows, rows)
        key = head_rows_of(qkv, chan_local + head * rows, rows)
        value = head_rows_of(qkv, 2 * chan_local + head * rows, rows)
        scores[head] = tn(query, key)
        scores[heads + head] = tn(head_rows_of(cot, head * rows, rows), value)
    for half in range(2):
        span = slice(half * HALO, (half + 1) * HALO)
        index = neighbours[:, span] - (first_atom + (half - 1) * HALO)
        index = jnp.where(index < 0, index + total_atoms, index)
        index = jnp.where(index >= total_atoms, index - total_atoms, index)
        index_rows[:, span] = index
        wide = wide_transpose(index)
        index_wide[span, :] = wide
        for tile in range(3):
            slot_own[half, tile] = slot_tile(wide[:, :slots], tile)


def edge_kernel(heads, score_scale, flm, flo, frm, fro, wp, qkv, cot, scores, bias, valid,
                index_rows, index_wide, halo_qkv, grad_bias, message_a, message_b):
    comps, chan_local = flm.shape[0], flm.shape[1]
    rows = chan_local // heads
    slots = valid.shape[0]
    for comp in range(comps):
        feats = jnp.concatenate(
            [
                jnp.concatenate([flm[comp], frm[comp]], axis=1),
                jnp.concatenate([flo[comp], fro[comp]], axis=1),
            ],
            axis=0,
        )
        halo_qkv[comp] = nn(wp[degree_of(comp)], feats).astype(BF16)
    lane = lax.broadcasted_iota(jnp.int32, (HALO, 2 * heads * slots), 1)
    gathered = [jnp.zeros((HALO, 2 * heads * slots), F32) for _ in range(2)]
    for quantity in range(2 * heads):
        head = quantity % heads
        if quantity < heads:
            mine = head_rows_of(qkv, head * rows, rows)
            theirs = head_rows_of(halo_qkv, chan_local + head * rows, rows)
        else:
            mine = head_rows_of(cot, head * rows, rows)
            theirs = head_rows_of(halo_qkv, 2 * chan_local + head * rows, rows)
        left = tn(mine[:, :HALO], theirs[:, :HALO])
        right = tn(mine[:, HALO:], theirs[:, HALO:])
        for half in range(2):
            own = scores[quantity, half * HALO : (half + 1) * HALO, :]
            own = [own[:, :HALO], own[:, HALO:]]
            tiles = [left] + own if half == 0 else own + [right]
            index = index_wide[half * HALO : (half + 1) * HALO, :]
            inner, tile_of = index & (HALO - 1), index >> 7
            values = jnp.where(
                tile_of == 0,
                pick(tiles[0], inner),
                jnp.where(tile_of == 1, pick(tiles[1], inner), pick(tiles[2], inner)),
            )
            gathered[half] = jnp.where(lane // slots == quantity, values, gathered[half])
    for half, message in enumerate((message_a, message_b)):
        span = slice(half * HALO, (half + 1) * HALO)
        edges = gathered[half].T.reshape(2, heads, slots, HALO)
        squashed = jnp.tanh(edges[0] * (score_scale / SOFT_CAP))
        logits = SOFT_CAP * squashed + bias[:, :, span]
        live = valid[:, span][None] > 0
        weight = jnp.where(live, jnp.exp(logits), 0.0)
        attention = weight / jnp.sum(weight, axis=1, keepdims=True)
        grad_attn = edges[1]
        grad_logit = attention * (
            grad_attn - jnp.sum(attention * grad_attn, axis=1, keepdims=True)
        )
        grad_bias[:, :, span] = grad_logit
        grad_raw = score_scale * grad_logit * (1.0 - squashed * squashed)
        index = index_rows[:, span]
        both = jnp.stack([grad_raw, attention]).reshape(2 * heads, slots, HALO)
        merged = jnp.zeros_like(both)
        for slot in range(slots):
            same = (index == index[slot : slot + 1, :])[None]
            merged = merged + jnp.where(same, both[:, slot : slot + 1, :], 0.0)
        atom = lax.broadcasted_iota(jnp.int32, (slots, HALO), 1)
        message[: 2 * heads * slots, :] = merged.reshape(2 * heads * slots, HALO).astype(BF16)
        message[2 * heads * slots :, :] = (index - HALO - atom).astype(F32).astype(BF16)


def grads_kernel(heads, slots, place, fm, fo, flm, flo, frm, fro, qkv, halo_qkv, cot, slot_own,
                 message_a, message_b, grad_query, own_key, own_value, weight_terms, ext):
    comps, chan_local = fm.shape[0], fm.shape[1]
    rows = chan_local // heads
    atoms = 2 * HALO
    core = place[0]
    empty = jnp.zeros((HALO, HALO), BF16)
    coefs = [message[: 2 * heads * slots, :].astype(F32).T for message in (message_a, message_b)]
    for head in range(heads):
        tables = []
        for quantity in (head, heads + head):
            halves = []
            for half in range(2):
                tiles = [spread(slot_own[half, t], coefs[half], quantity, slots) for t in range(3)]
                tiles = tiles + [empty] if half == 0 else [empty] + tiles
                halves.append(jnp.concatenate(tiles, axis=1))
            tables.append(jnp.concatenate(halves, axis=0))
        raw_table, attn_table = tables
        query = head_rows_of(qkv, head * rows, rows)
        key = head_rows_of(qkv, chan_local + head * rows, rows)
        halo_key = head_rows_of(halo_qkv, chan_local + head * rows, rows)
        key_ext = jnp.concatenate([halo_key[:, :HALO], key, halo_key[:, HALO:]], axis=1)
        span = slice(head * rows, (head + 1) * rows)
        value_span = slice(chan_local + head * rows, chan_local + (head + 1) * rows)
        grad_query[:, span, :] = nt(key_ext, raw_table).astype(BF16).reshape(comps, rows, atoms)
        key_sums = nn(query, raw_table)
        own_key[:, span, :] = key_sums[:, HALO : HALO + atoms].reshape(comps, rows, atoms)
        ext[:, span, :] = key_sums.astype(BF16).reshape(comps, rows, atoms + 2 * HALO)
        value_sums = nn(head_rows_of(cot, head * rows, rows), attn_table)
        own_value[:, span, :] = value_sums[:, HALO : HALO + atoms].reshape(comps, rows, atoms)
        ext[:, value_span, :] = value_sums.astype(BF16).reshape(comps, rows, atoms + 2 * HALO)
    for degree in range(LMAX + 1):
        query_total = jnp.zeros((chan_local, 2 * chan_local), F32)
        keyval_total = jnp.zeros((2 * chan_local, 2 * chan_local), F32)
        for comp in range(degree * degree, (degree + 1) * (degree + 1)):
            own = jnp.concatenate([fm[comp], fo[comp]], axis=0)
            wide = jnp.concatenate(
                [
                    jnp.concatenate([flm[comp], fm[comp], frm[comp]], axis=1),
                    jnp.concatenate([flo[comp], fo[comp], fro[comp]], axis=1),
                ],
                axis=0,
            )
            query_total = query_total + nt(grad_query[comp], own)
            keyval_total = keyval_total + nt(ext[comp], wide)
        total = jnp.concatenate([query_total, keyval_total], axis=0)
        total = jnp.where(core == 0, total, pltpu.roll(total, chan_local, 1))
        for g in range(3):
            weight_terms[g, degree] = total[g * chan_local : (g + 1) * chan_local]


def halo_slots(message_left, message_right, quantities, slots):
    coefs, tables = [], []
    for message, tile in ((message_left, 2), (message_right, 0)):
        coefs.append(message[: quantities * slots, :].astype(F32).T)
        offset = message[quantities * slots :, :].astype(F32).astype(jnp.int32)
        atom = lax.broadcasted_iota(jnp.int32, offset.shape, 1)
        tables.append(slot_tile(wide_transpose(offset + HALO + atom)[:, :slots], tile))
    return coefs, tables


def key_kernel(heads, slots, grad_query, own_key, halo_qkv, message_left, message_right, wc,
               terms, grad):
    comps, chan_local = grad_query.shape[0], grad_query.shape[1]
    rows = chan_local // heads
    grad[:, :chan_local, :] = grad_query[...]
    coefs, tables = halo_slots(message_left, message_right, 2 * heads, slots)
    for head in range(heads):
        query = head_rows_of(halo_qkv, head * rows, rows)
        rim = jnp.concatenate(
            [
                nn(query[:, :HALO], spread(tables[0], coefs[0], head, slots)),
                nn(query[:, HALO:], spread(tables[1], coefs[1], head, slots)),
            ],
            axis=1,
        )
        total = head_rows_of(own_key, head * rows, rows) + rim
        span = slice(chan_local + head * rows, chan_local + (head + 1) * rows)
        grad[:, span, :] = total.astype(BF16).reshape(comps, rows, 2 * HALO)
    for comp in range(comps):
        terms[comp] = nn(wc[degree_of(comp)][:, : 2 * chan_local], grad[comp])


def value_kernel(heads, slots, start, own_value, cl, cr, message_left, message_right, wc, terms,
                 mine, theirs, grad):
    comps, chan_local = cl.shape[0], cl.shape[1]
    rows = chan_local // heads
    coefs, tables = halo_slots(message_left, message_right, 2 * heads, slots)
    for head in range(heads):
        span = slice(head * rows, (head + 1) * rows)
        rim = jnp.concatenate(
            [
                nn(head_rows_of(cl, head * rows, rows),
                   spread(tables[0], coefs[0], heads + head, slots)),
                nn(head_rows_of(cr, head * rows, rows),
                   spread(tables[1], coefs[1], heads + head, slots)),
            ],
            axis=1,
        )
        own = own_value[start : start + comps, span, :].reshape(comps * rows, 2 * HALO)
        grad[:, span, :] = (own + rim).astype(BF16).reshape(comps, rows, 2 * HALO)
    for comp in range(comps):
        mix = wc[degree_of(start + comp)][:, 2 * chan_local :]
        total = terms[start + comp] + nn(mix, grad[comp])
        mine[comp] = total[:chan_local]
        theirs[comp] = total[chan_local:].astype(BF16)


def finish_kernel(mine_a, theirs_a, mine_b, theirs_b, out):
    cut = mine_a.shape[0]
    out[:cut] = (mine_a[...] + theirs_a[...].astype(F32)).astype(BF16)
    out[cut:] = (mine_b[...] + theirs_b[...].astype(F32)).astype(BF16)


def call(kernel, args, outs, scratch=(), scalars=0, limit=24):
    whole = pl.BlockSpec(memory_space=pltpu.VMEM)
    small = pl.BlockSpec(memory_space=pltpu.SMEM)
    args = list(args)
    args[scalars:] = [pltpu.with_memory_space_constraint(a, pltpu.VMEM) for a in args[scalars:]]
    return pl.pallas_call(
        kernel,
        out_shape=tuple(outs),
        in_specs=[small] * scalars + [whole] * (len(args) - scalars),
        out_specs=tuple([whole] * len(outs)),
        scratch_shapes=list(scratch),
        compiler_params=pltpu.CompilerParams(vmem_limit_bytes=limit * 1024 * 1024),
        cost_estimate=pl.CostEstimate(flops=0, bytes_accessed=1024, transcendentals=0),
    )(*args)


def after(values, tokens):
    anywhere = pl.BlockSpec(memory_space=pl.ANY)
    count = len(values)

    def kernel(*refs):
        pass

    return pl.pallas_call(
        kernel,
        out_shape=tuple(jax.ShapeDtypeStruct(v.shape, v.dtype) for v in values),
        in_specs=[anywhere] * (count + len(tokens)),
        out_specs=tuple([anywhere] * count),
        input_output_aliases={i: i for i in range(count)},
        cost_estimate=pl.CostEstimate(flops=0, bytes_accessed=1024, transcendentals=0),
    )(*values, *tokens)


def shifted(value, axis, steps):
    count = lax.axis_size(axis)
    pairs = [(source, (source + steps) % count) for source in range(count)]
    return lax.ppermute(value, axis, pairs)


def summed_over(value, axis):
    count = lax.axis_size(axis)
    columns = value.shape[-1]
    flat = value.reshape(-1, columns)
    rows = -(-flat.shape[0] // count)
    padded = jnp.pad(flat, ((0, rows * count - flat.shape[0]), (0, 0)))
    pieces = padded.reshape(count, rows, columns).astype(BF16)
    pieces = lax.all_to_all(pieces, axis, 0, 0, tiled=True)
    piece = jnp.sum(pieces.astype(F32), axis=0).astype(BF16)
    every = lax.all_to_all(jnp.broadcast_to(piece[None], pieces.shape), axis, 0, 0, tiled=True)
    return every.astype(F32).reshape(rows * count, columns)[: flat.shape[0]].reshape(value.shape)


def on_device(features, weights, cotangent, edge_bias, neighbours, valid_mask):
    chan_local, comps, atoms_dev = features.shape
    heads, slots = edge_bias.shape[0], edge_bias.shape[1]
    channels = weights.shape[2]
    assert atoms_dev == 2 * HALO and channels == 2 * chan_local
    score_scale = 1.0 / math.sqrt(chan_local // heads * comps)
    total_atoms = atoms_dev * lax.axis_size("atom")
    place = jnp.stack([lax.axis_index("chan"), lax.axis_index("atom") * atoms_dev])
    place = place.astype(jnp.int32)
    cut = comps // 2

    def held(*dims, dtype=F32):
        return pltpu.VMEM(dims, dtype)

    def plain(*dims, dtype=F32):
        return jax.ShapeDtypeStruct(dims, dtype)

    fm = jnp.transpose(features, (1, 0, 2))
    cot = jnp.transpose(cotangent, (1, 0, 2))
    mix = jnp.transpose(weights, (0, 1, 3, 2))
    flm = shifted(fm[:, :, HALO:], "atom", 1)
    frm = shifted(fm[:, :, :HALO], "atom", -1)
    fo = shifted(fm, "chan", 1)
    rims = [cot[:cut, :, HALO:], cot[:cut, :, :HALO], cot[cut:, :, HALO:], cot[cut:, :, :HALO]]

    qkv, scores, slot_own, index_rows, index_wide, wp, wc = call(
        functools.partial(own_kernel, heads, total_atoms),
        (place, fm, fo, cot, mix, neighbours),
        (
            held(comps, 3 * chan_local, atoms_dev, dtype=BF16),
            held(2 * heads, atoms_dev, atoms_dev),
            held(2, 3, HALO, HALO, dtype=jnp.int32),
            held(slots, atoms_dev, dtype=jnp.int32),
            held(atoms_dev, HALO, dtype=jnp.int32),
            held(LMAX + 1, 3 * chan_local, channels, dtype=BF16),
            held(LMAX + 1, channels, 3 * chan_local, dtype=BF16),
        ),
        scalars=1,
    )
    flm, frm = after((flm, frm), (index_rows,))
    flo = shifted(flm, "chan", 1)
    fro = shifted(frm, "chan", 1)
    rims[:2] = after(rims[:2], (flm, frm))
    first = (shifted(rims[0], "atom", 1), shifted(rims[1], "atom", -1))
    halo_qkv, grad_bias, message_a, message_b = call(
        functools.partial(edge_kernel, heads, score_scale),
        (flm, flo, frm, fro, wp, qkv, cot, scores, edge_bias, valid_mask, index_rows, index_wide),
        (
            held(comps, 3 * chan_local, atoms_dev, dtype=BF16),
            plain(heads, slots, atoms_dev),
            held((2 * heads + 1) * slots, HALO, dtype=BF16),
            held((2 * heads + 1) * slots, HALO, dtype=BF16),
        ),
    )
    message_left = shifted(message_b, "atom", 1)
    message_right = shifted(message_a, "atom", -1)
    rims[2:] = after(rims[2:], (message_left, message_right))
    second = (shifted(rims[2], "atom", 1), shifted(rims[3], "atom", -1))
    grad_query, own_key, own_value, weight_terms = call(
        functools.partial(grads_kernel, heads, slots),
        (place, fm, fo, flm, flo, frm, fro, qkv, halo_qkv, cot, slot_own, message_a, message_b),
        (
            held(comps, chan_local, atoms_dev, dtype=BF16),
            held(comps, chan_local, atoms_dev),
            held(comps, chan_local, atoms_dev),
            held(3, LMAX + 1, chan_local, channels),
        ),
        scratch=[pltpu.VMEM((comps, 2 * chan_local, 2 * atoms_dev), BF16)],
        scalars=1,
    )
    grad_weights = summed_over(weight_terms, "atom")
    (terms,) = call(
        functools.partial(key_kernel, heads, slots),
        (grad_query, own_key, halo_qkv, message_left, message_right, wc),
        (held(comps, channels, atoms_dev),),
        scratch=[pltpu.VMEM((comps, 2 * chan_local, atoms_dev), BF16)],
    )
    parts = []
    for start, (cl, cr) in ((0, first), (cut, second)):
        count = cl.shape[0]
        mine, theirs = call(
            functools.partial(value_kernel, heads, slots, start),
            (own_value, cl, cr, message_left, message_right, wc, terms),
            (
                held(count, chan_local, atoms_dev),
                held(count, chan_local, atoms_dev, dtype=BF16),
            ),
            scratch=[pltpu.VMEM((count, chan_local, atoms_dev), BF16)],
        )
        parts += [mine, shifted(theirs, "chan", 1)]
    (out,) = call(finish_kernel, parts, (plain(comps, chan_local, atoms_dev, dtype=BF16),))
    grad_features = jnp.transpose(out, (1, 0, 2))
    grad_weights = jnp.transpose(grad_weights, (0, 1, 3, 2))
    return grad_features, grad_weights, grad_bias


def solution(mesh):
    in_specs = (
        P("chan", None, "atom"),
        P(None, None, None, "chan"),
        P("chan", None, "atom"),
        P("chan", None, "atom"),
        P(None, "atom"),
        P(None, "atom"),
    )
    out_specs = (P("chan", None, "atom"), P(None, None, None, "chan"), P("chan", None, "atom"))
    return jax.shard_map(
        on_device, mesh=mesh, in_specs=in_specs, out_specs=out_specs, check_vma=False
    )
```

```python
import functools
import math

import jax
import jax.numpy as jnp
from jax import lax
from jax.experimental import pallas as pl
from jax.experimental.pallas import tpu as pltpu
from jax.sharding import PartitionSpec as P

LMAX = 6
HALO = 128
SOFT_CAP = 10.0
F32 = jnp.float32
BF16 = jnp.bfloat16


def degree_of(comp):
    return math.isqrt(comp)


def nn(lhs, rhs):
    return lax.dot_general(lhs, rhs, (((1,), (0,)), ((), ())), preferred_element_type=F32)


def nt(lhs, rhs):
    return lax.dot_general(lhs, rhs, (((1,), (1,)), ((), ())), preferred_element_type=F32)


def tn(lhs, rhs):
    return lax.dot_general(lhs, rhs, (((0,), (0,)), ((), ())), preferred_element_type=F32)


def pick(table, index):
    return jnp.take_along_axis(table, index, axis=1, mode="promise_in_bounds")


def head_rows_of(ref, first_row, rows):
    block = ref[:, first_row : first_row + rows, :]
    return block.reshape(block.shape[0] * rows, block.shape[2])


def slot_tile(window_index, tile):
    atoms, slots = window_index.shape
    lane = lax.broadcasted_iota(jnp.int32, (atoms, HALO), 1) + tile * HALO
    found = jnp.full((atoms, HALO), -1, jnp.int32)
    for slot in range(slots):
        found = jnp.where(window_index[:, slot : slot + 1] == lane, slot, found)
    return found


def spread(slot, coef, quantity, slots):
    values = pick(coef, jnp.maximum(slot, 0) + quantity * slots)
    return jnp.where(slot >= 0, values, 0.0).astype(BF16)


def wide_transpose(rows):
    return jnp.concatenate([rows] * (HALO // rows.shape[0]), axis=0).T


def split_kernel(fm, low, high, sems):
    copies = [
        pltpu.make_async_copy(fm.at[:, :, pl.ds(at * HALO, HALO)], part, sems.at[at])
        for at, part in enumerate((low, high))
    ]
    for copy in copies:
        copy.start()
    for copy in copies:
        copy.wait()


def own_kernel(heads, total_atoms, cut, place, fm, fo, cot, weights, neighbours,
               qkv, scores, slot_own, index_rows, index_wide, wp, wc, rims_a, rims_b,
               rims_c, rims_d, token):
    token[...] = jnp.zeros_like(token)
    rims_a[...] = cot[:cut, :, HALO:]
    rims_b[...] = cot[:cut, :, :HALO]
    rims_c[...] = cot[cut:, :, HALO:]
    rims_d[...] = cot[cut:, :, :HALO]
    comps, chan_local = fm.shape[0], fm.shape[1]
    channels = weights.shape[3]
    rows = chan_local // heads
    slots = neighbours.shape[0]
    core, first_atom = place[0], place[1]
    for degree in range(LMAX + 1):
        mix = jnp.concatenate([weights[g, degree] for g in range(3)], axis=0).astype(F32)
        mix = jnp.where(core == 0, mix, pltpu.roll(mix, chan_local, 1))
        wp[degree] = mix.astype(BF16)
        padded = jnp.concatenate([mix, jnp.zeros((chan_local, channels), F32)], axis=0)
        wc[degree] = padded.T[:, : 3 * chan_local].astype(BF16)
    for comp in range(comps):
        feats = jnp.concatenate([fm[comp], fo[comp]], axis=0)
        qkv[comp] = nn(wp[degree_of(comp)], feats).astype(BF16)
    for head in range(heads):
        query = head_rows_of(qkv, head * rows, rows)
        key = head_rows_of(qkv, chan_local + head * rows, rows)
        value = head_rows_of(qkv, 2 * chan_local + head * rows, rows)
        scores[head] = tn(query, key)
        scores[heads + head] = tn(head_rows_of(cot, head * rows, rows), value)
    for half in range(2):
        span = slice(half * HALO, (half + 1) * HALO)
        index = neighbours[:, span] - (first_atom + (half - 1) * HALO)
        index = jnp.where(index < 0, index + total_atoms, index)
        index = jnp.where(index >= total_atoms, index - total_atoms, index)
        index_rows[:, span] = index
        wide = wide_transpose(index)
        index_wide[span, :] = wide
        for tile in range(3):
            slot_own[half, tile] = slot_tile(wide[:, :slots], tile)


def edge_kernel(heads, score_scale, flm, flo, frm, fro, wp, qkv, cot, scores, bias, valid,
                index_rows, index_wide, halo_qkv, grad_bias, message_a, message_b):
    comps, chan_local = flm.shape[0], flm.shape[1]
    rows = chan_local // heads
    slots = valid.shape[0]
    for comp in range(comps):
        feats = jnp.concatenate(
            [
                jnp.concatenate([flm[comp], frm[comp]], axis=1),
                jnp.concatenate([flo[comp], fro[comp]], axis=1),
            ],
            axis=0,
        )
        halo_qkv[comp] = nn(wp[degree_of(comp)], feats).astype(BF16)
    lane = lax.broadcasted_iota(jnp.int32, (HALO, 2 * heads * slots), 1)
    gathered = [jnp.zeros((HALO, 2 * heads * slots), F32) for _ in range(2)]
    for quantity in range(2 * heads):
        head = quantity % heads
        if quantity < heads:
            mine = head_rows_of(qkv, head * rows, rows)
            theirs = head_rows_of(halo_qkv, chan_local + head * rows, rows)
        else:
            mine = head_rows_of(cot, head * rows, rows)
            theirs = head_rows_of(halo_qkv, 2 * chan_local + head * rows, rows)
        left = tn(mine[:, :HALO], theirs[:, :HALO])
        right = tn(mine[:, HALO:], theirs[:, HALO:])
        for half in range(2):
            own = scores[quantity, half * HALO : (half + 1) * HALO, :]
            own = [own[:, :HALO], own[:, HALO:]]
            tiles = [left] + own if half == 0 else own + [right]
            index = index_wide[half * HALO : (half + 1) * HALO, :]
            inner, tile_of = index & (HALO - 1), index >> 7
            values = jnp.where(
                tile_of == 0,
                pick(tiles[0], inner),
                jnp.where(tile_of == 1, pick(tiles[1], inner), pick(tiles[2], inner)),
            )
            gathered[half] = jnp.where(lane // slots == quantity, values, gathered[half])
    for half, message in enumerate((message_a, message_b)):
        span = slice(half * HALO, (half + 1) * HALO)
        edges = gathered[half].T.reshape(2, heads, slots, HALO)
        squashed = jnp.tanh(edges[0] * (score_scale / SOFT_CAP))
        logits = SOFT_CAP * squashed + bias[:, :, span]
        live = valid[:, span][None] > 0
        weight = jnp.where(live, jnp.exp(logits), 0.0)
        attention = weight / jnp.sum(weight, axis=1, keepdims=True)
        grad_attn = edges[1]
        grad_logit = attention * (
            grad_attn - jnp.sum(attention * grad_attn, axis=1, keepdims=True)
        )
        grad_bias[:, :, span] = grad_logit
        grad_raw = score_scale * grad_logit * (1.0 - squashed * squashed)
        index = index_rows[:, span]
        both = jnp.stack([grad_raw, attention]).reshape(2 * heads, slots, HALO)
        merged = jnp.zeros_like(both)
        for slot in range(slots):
            same = (index == index[slot : slot + 1, :])[None]
            merged = merged + jnp.where(same, both[:, slot : slot + 1, :], 0.0)
        atom = lax.broadcasted_iota(jnp.int32, (slots, HALO), 1)
        message[: 2 * heads * slots, :] = merged.reshape(2 * heads * slots, HALO).astype(BF16)
        message[2 * heads * slots :, :] = (index - HALO - atom).astype(F32).astype(BF16)


def grads_kernel(heads, slots, place, fm, fo, flm, flo, frm, fro, qkv, halo_qkv, cot, slot_own,
                 message_a, message_b, grad_query, own_key, own_value, kept, sent_1, sent_2,
                 sent_3, ext, weight_terms):
    comps, chan_local = fm.shape[0], fm.shape[1]
    rows = chan_local // heads
    atoms = 2 * HALO
    core = place[0]
    empty = jnp.zeros((HALO, HALO), BF16)
    coefs = [message[: 2 * heads * slots, :].astype(F32).T for message in (message_a, message_b)]
    for head in range(heads):
        tables = []
        for quantity in (head, heads + head):
            halves = []
            for half in range(2):
                tiles = [spread(slot_own[half, t], coefs[half], quantity, slots) for t in range(3)]
                tiles = tiles + [empty] if half == 0 else [empty] + tiles
                halves.append(jnp.concatenate(tiles, axis=1))
            tables.append(jnp.concatenate(halves, axis=0))
        raw_table, attn_table = tables
        query = head_rows_of(qkv, head * rows, rows)
        key = head_rows_of(qkv, chan_local + head * rows, rows)
        halo_key = head_rows_of(halo_qkv, chan_local + head * rows, rows)
        key_ext = jnp.concatenate([halo_key[:, :HALO], key, halo_key[:, HALO:]], axis=1)
        span = slice(head * rows, (head + 1) * rows)
        value_span = slice(chan_local + head * rows, chan_local + (head + 1) * rows)
        grad_query[:, span, :] = nt(key_ext, raw_table).astype(BF16).reshape(comps, rows, atoms)
        key_sums = nn(query, raw_table)
        own_key[:, span, :] = key_sums[:, HALO : HALO + atoms].reshape(comps, rows, atoms)
        ext[:, span, :] = key_sums.astype(BF16).reshape(comps, rows, atoms + 2 * HALO)
        value_sums = nn(head_rows_of(cot, head * rows, rows), attn_table)
        own_value[:, span, :] = value_sums[:, HALO : HALO + atoms].reshape(comps, rows, atoms)
        ext[:, value_span, :] = value_sums.astype(BF16).reshape(comps, rows, atoms + 2 * HALO)
    for degree in range(LMAX + 1):
        query_total = jnp.zeros((chan_local, 2 * chan_local), F32)
        keyval_total = jnp.zeros((2 * chan_local, 2 * chan_local), F32)
        for comp in range(degree * degree, (degree + 1) * (degree + 1)):
            own = jnp.concatenate([fm[comp], fo[comp]], axis=0)
            wide = jnp.concatenate(
                [
                    jnp.concatenate([flm[comp], fm[comp], frm[comp]], axis=1),
                    jnp.concatenate([flo[comp], fo[comp], fro[comp]], axis=1),
                ],
                axis=0,
            )
            query_total = query_total + nt(grad_query[comp], own)
            keyval_total = keyval_total + nt(ext[comp], wide)
        total = jnp.concatenate([query_total, keyval_total], axis=0)
        total = jnp.where(core == 0, total, pltpu.roll(total, chan_local, 1))
        for g in range(3):
            weight_terms[g * (LMAX + 1) + degree] = total[g * chan_local : (g + 1) * chan_local]
    piece = chan_local // 4
    spot = place[2]
    for delta, part in enumerate((kept, sent_1, sent_2, sent_3)):
        first = pl.multiple_of((spot ^ delta) * piece, piece)
        part[...] = weight_terms[:, pl.ds(first, piece), :].astype(part.dtype)


def halo_slots(message_left, message_right, quantities, slots):
    coefs, tables = [], []
    for message, tile in ((message_left, 2), (message_right, 0)):
        coefs.append(message[: quantities * slots, :].astype(F32).T)
        offset = message[quantities * slots :, :].astype(F32).astype(jnp.int32)
        atom = lax.broadcasted_iota(jnp.int32, offset.shape, 1)
        tables.append(slot_tile(wide_transpose(offset + HALO + atom)[:, :slots], tile))
    return coefs, tables


def key_kernel(heads, slots, grad_query, own_key, halo_qkv, message_left, message_right, wc,
               terms, grad):
    comps, chan_local = grad_query.shape[0], grad_query.shape[1]
    rows = chan_local // heads
    grad[:, :chan_local, :] = grad_query[...]
    coefs, tables = halo_slots(message_left, message_right, 2 * heads, slots)
    for head in range(heads):
        query = head_rows_of(halo_qkv, head * rows, rows)
        rim = jnp.concatenate(
            [
                nn(query[:, :HALO], spread(tables[0], coefs[0], head, slots)),
                nn(query[:, HALO:], spread(tables[1], coefs[1], head, slots)),
            ],
            axis=1,
        )
        total = head_rows_of(own_key, head * rows, rows) + rim
        span = slice(chan_local + head * rows, chan_local + (head + 1) * rows)
        grad[:, span, :] = total.astype(BF16).reshape(comps, rows, 2 * HALO)
    for comp in range(comps):
        terms[comp] = nn(wc[degree_of(comp)][:, : 2 * chan_local], grad[comp])


def value_kernel(heads, slots, start, own_value, cl, cr, message_left, message_right, wc, terms,
                 mine, theirs, token, grad):
    token[...] = jnp.zeros_like(token)
    comps, chan_local = cl.shape[0], cl.shape[1]
    rows = chan_local // heads
    coefs, tables = halo_slots(message_left, message_right, 2 * heads, slots)
    for head in range(heads):
        span = slice(head * rows, (head + 1) * rows)
        rim = jnp.concatenate(
            [
                nn(head_rows_of(cl, head * rows, rows),
                   spread(tables[0], coefs[0], heads + head, slots)),
                nn(head_rows_of(cr, head * rows, rows),
                   spread(tables[1], coefs[1], heads + head, slots)),
            ],
            axis=1,
        )
        own = own_value[start : start + comps, span, :].reshape(comps * rows, 2 * HALO)
        grad[:, span, :] = (own + rim).astype(BF16).reshape(comps, rows, 2 * HALO)
    for comp in range(comps):
        mix = wc[degree_of(start + comp)][:, 2 * chan_local :]
        total = terms[start + comp] + nn(mix, grad[comp])
        mine[comp] = total[:chan_local]
        theirs[comp] = total[chan_local:].astype(BF16)


def finish_kernel(mine_a, theirs_a, mine_b, theirs_b, out):
    cut = mine_a.shape[0]
    out[:cut] = (mine_a[...] + theirs_a[...].astype(F32)).astype(BF16)
    out[cut:] = (mine_b[...] + theirs_b[...].astype(F32)).astype(BF16)


def gather_kernel(place, part_0, part_1, part_2, part_3, out):
    piece = part_0.shape[1]
    spot = place[2]
    for delta, part in enumerate((part_0, part_1, part_2, part_3)):
        first = pl.multiple_of((spot ^ delta) * piece, piece)
        out[:, pl.ds(first, piece), :] = part[...].astype(F32)


def call(kernel, args, outs, scratch=(), scalars=0, limit=24, stay=(), tokens=()):
    whole = pl.BlockSpec(memory_space=pltpu.VMEM)
    small = pl.BlockSpec(memory_space=pltpu.SMEM)
    args = [
        pltpu.with_memory_space_constraint(a, pltpu.VMEM) if at in stay else a
        for at, a in enumerate(args)
    ]
    count = len(args)

    def body(*refs):
        kernel(*refs[:count], *refs[count + len(tokens) :])

    return pl.pallas_call(
        body,
        out_shape=tuple(outs),
        in_specs=[small] * scalars
        + [whole] * (count - scalars)
        + [pl.BlockSpec(memory_space=pl.ANY)] * len(tokens),
        out_specs=tuple([whole] * len(outs)),
        scratch_shapes=list(scratch),
        compiler_params=pltpu.CompilerParams(vmem_limit_bytes=limit * 1024 * 1024),
        cost_estimate=pl.CostEstimate(flops=0, bytes_accessed=1024, transcendentals=0),
    )(*args, *tokens)


def after(values, tokens):
    anywhere = pl.BlockSpec(memory_space=pl.ANY)
    count = len(values)

    def kernel(*refs):
        pass

    return pl.pallas_call(
        kernel,
        out_shape=tuple(jax.ShapeDtypeStruct(v.shape, v.dtype) for v in values),
        in_specs=[anywhere] * (count + len(tokens)),
        out_specs=tuple([anywhere] * count),
        input_output_aliases={i: i for i in range(count)},
        compiler_params=pltpu.CompilerParams(vmem_limit_bytes=1024 * 1024),
        cost_estimate=pl.CostEstimate(flops=0, bytes_accessed=1024, transcendentals=0),
    )(*values, *tokens)


def shifted(value, axis, steps):
    count = lax.axis_size(axis)
    pairs = [(source, (source + steps) % count) for source in range(count)]
    return lax.ppermute(value, axis, pairs)


def exchanged(value, axis, offset):
    count = lax.axis_size(axis)
    return lax.ppermute(value, axis, [(source, source ^ offset) for source in range(count)])


def on_device(features, weights, cotangent, edge_bias, neighbours, valid_mask):
    chan_local, comps, atoms_dev = features.shape
    heads, slots = edge_bias.shape[0], edge_bias.shape[1]
    channels = weights.shape[2]
    assert atoms_dev == 2 * HALO and channels == 2 * chan_local
    score_scale = 1.0 / math.sqrt(chan_local // heads * comps)
    total_atoms = atoms_dev * lax.axis_size("atom")
    count = lax.axis_size("atom")
    assert count >= 4 and count & (count - 1) == 0
    atom_place = lax.axis_index("atom")
    cut_bits = (1, 2) if count >= 8 else (0, 1)
    spot = (atom_place >> cut_bits[0]) & 3
    place = jnp.stack([lax.axis_index("chan"), atom_place * atoms_dev, spot])
    place = place.astype(jnp.int32)
    cut = comps // 2

    def held(*dims, dtype=F32):
        return pltpu.VMEM(dims, dtype)

    def plain(*dims, dtype=F32):
        return jax.ShapeDtypeStruct(dims, dtype)

    fm = jnp.transpose(features, (1, 0, 2))
    cot = jnp.transpose(cotangent, (1, 0, 2))
    mix = jnp.transpose(weights, (0, 1, 3, 2))
    anywhere = pl.BlockSpec(memory_space=pl.ANY)
    low, high = pl.pallas_call(
        split_kernel,
        out_shape=(plain(comps, chan_local, HALO, dtype=BF16),) * 2,
        in_specs=[anywhere],
        out_specs=(anywhere, anywhere),
        scratch_shapes=[pltpu.SemaphoreType.DMA((2,))],
        compiler_params=pltpu.CompilerParams(vmem_limit_bytes=1024 * 1024),
    )(fm)
    flm = shifted(high, "atom", 1)
    frm = shifted(low, "atom", -1)
    fo = shifted(fm, "chan", 1)

    qkv, scores, slot_own, index_rows, index_wide, wp, wc, *rims, token = call(
        functools.partial(own_kernel, heads, total_atoms, cut),
        (place, fm, fo, cot, mix, neighbours),
        (
            held(comps, 3 * chan_local, atoms_dev, dtype=BF16),
            held(2 * heads, atoms_dev, atoms_dev),
            held(2, 3, HALO, HALO, dtype=jnp.int32),
            held(slots, atoms_dev, dtype=jnp.int32),
            held(atoms_dev, HALO, dtype=jnp.int32),
            held(LMAX + 1, 3 * chan_local, channels, dtype=BF16),
            held(LMAX + 1, channels, 3 * chan_local, dtype=BF16),
            plain(cut, chan_local, HALO, dtype=BF16),
            plain(cut, chan_local, HALO, dtype=BF16),
            plain(comps - cut, chan_local, HALO, dtype=BF16),
            plain(comps - cut, chan_local, HALO, dtype=BF16),
            plain(8, HALO),
        ),
        scalars=1,
        stay=(1, 2, 3),
    )
    flm, frm = after((flm, frm), (token,))
    flo = shifted(flm, "chan", 1)
    fro = shifted(frm, "chan", 1)
    rims[:2] = after(rims[:2], (flm, frm))
    first = (shifted(rims[0], "atom", 1), shifted(rims[1], "atom", -1))
    halo_qkv, grad_bias, message_a, message_b = call(
        functools.partial(edge_kernel, heads, score_scale),
        (flm, flo, frm, fro, wp, qkv, cot, scores, edge_bias, valid_mask, index_rows, index_wide),
        (
            held(comps, 3 * chan_local, atoms_dev, dtype=BF16),
            plain(heads, slots, atoms_dev),
            held((2 * heads + 1) * slots, HALO, dtype=BF16),
            held((2 * heads + 1) * slots, HALO, dtype=BF16),
        ),
        stay=(0, 1, 2, 3, 4, 5, 6, 7, 10, 11),
    )
    message_left = shifted(message_b, "atom", 1)
    message_right = shifted(message_a, "atom", -1)
    piece = (3 * (LMAX + 1), chan_local // 4, channels)
    grad_query, own_key, own_value, kept, *sent = call(
        functools.partial(grads_kernel, heads, slots),
        (place, fm, fo, flm, flo, frm, fro, qkv, halo_qkv, cot, slot_own, message_a, message_b),
        (
            held(comps, chan_local, atoms_dev, dtype=BF16),
            held(comps, chan_local, atoms_dev),
            held(comps, chan_local, atoms_dev),
            held(*piece),
            held(*piece, dtype=BF16),
            held(*piece, dtype=BF16),
            held(*piece, dtype=BF16),
        ),
        scratch=[
            pltpu.VMEM((comps, 2 * chan_local, 2 * atoms_dev), BF16),
            pltpu.VMEM((3 * (LMAX + 1), chan_local, channels), F32),
        ],
        scalars=1,
        stay=tuple(range(1, 13)),
    )
    arrived = [exchanged(sent[d - 1], "atom", d << cut_bits[0]) for d in range(1, 4)]
    rims[2:] = after(rims[2:], (message_left, message_right, arrived[0], *first))
    second = (shifted(rims[2], "atom", 1), shifted(rims[3], "atom", -1))
    kept = kept + arrived[0].astype(F32) + arrived[1].astype(F32) + arrived[2].astype(F32)
    rest = [bit for bit in range(count.bit_length() - 1) if bit not in cut_bits]
    while rest:
        group, rest = rest[:2], rest[2:]
        rounded = kept.astype(BF16)
        offsets = [1 << bit for bit in group]
        for offset in offsets + [sum(offsets)] * (len(group) - 1):
            kept = kept + exchanged(rounded, "atom", offset).astype(F32)
    rounded = kept.astype(BF16)
    pieces = [rounded] + [exchanged(rounded, "atom", d << cut_bits[0]) for d in range(1, 4)]
    (grad_weights,) = call(
        gather_kernel,
        (place, *pieces),
        (plain(3 * (LMAX + 1), chan_local, channels),),
        scalars=1,
        limit=8,
    )
    (terms,) = call(
        functools.partial(key_kernel, heads, slots),
        (grad_query, own_key, halo_qkv, message_left, message_right, wc),
        (held(comps, channels, atoms_dev),),
        scratch=[pltpu.VMEM((comps, 2 * chan_local, atoms_dev), BF16)],
        limit=16,
        stay=(0, 1, 2, 5),
    )
    parts = []
    tokens = ()
    for start, (cl, cr) in ((0, first), (cut, second)):
        size = cl.shape[0]
        mine, theirs, token = call(
            functools.partial(value_kernel, heads, slots, start),
            (own_value, cl, cr, message_left, message_right, wc, terms),
            (
                held(size, chan_local, atoms_dev),
                held(size, chan_local, atoms_dev, dtype=BF16),
                plain(8, HALO),
            ),
            scratch=[pltpu.VMEM((size, chan_local, atoms_dev), BF16)],
            limit=16,
            stay=(0, 5, 6),
            tokens=tokens,
        )
        tokens = (token, rounded)
        parts += [mine, shifted(theirs, "chan", 1)]
    (out,) = call(
        finish_kernel,
        parts,
        (plain(comps, chan_local, atoms_dev, dtype=BF16),),
        limit=8,
        stay=(0, 1, 2, 3),
    )
    grad_features = jnp.transpose(out, (1, 0, 2))
    grad_weights = grad_weights.reshape(3, LMAX + 1, chan_local, channels)
    grad_weights = jnp.transpose(grad_weights, (0, 1, 3, 2))
    return grad_features, grad_weights, grad_bias


def solution(mesh):
    in_specs = (
        P("chan", None, "atom"),
        P(None, None, None, "chan"),
        P("chan", None, "atom"),
        P("chan", None, "atom"),
        P(None, "atom"),
        P(None, "atom"),
    )
    out_specs = (P("chan", None, "atom"), P(None, None, None, "chan"), P("chan", None, "atom"))
    return jax.shard_map(
        on_device, mesh=mesh, in_specs=in_specs, out_specs=out_specs, check_vma=False
    )
```

```python
import functools
import math

import jax
import jax.numpy as jnp
from jax import lax
from jax.experimental import pallas as pl
from jax.experimental.pallas import tpu as pltpu
from jax.sharding import PartitionSpec as P

LMAX = 6
HALO = 128
SOFT_CAP = 10.0
F32 = jnp.float32
BF16 = jnp.bfloat16


def degree_of(comp):
    return math.isqrt(comp)


def nn(lhs, rhs):
    return lax.dot_general(lhs, rhs, (((1,), (0,)), ((), ())), preferred_element_type=F32)


def nt(lhs, rhs):
    return lax.dot_general(lhs, rhs, (((1,), (1,)), ((), ())), preferred_element_type=F32)


def tn(lhs, rhs):
    return lax.dot_general(lhs, rhs, (((0,), (0,)), ((), ())), preferred_element_type=F32)


def pick(table, index):
    return jnp.take_along_axis(table, index, axis=1, mode="promise_in_bounds")


def head_rows_of(ref, first_row, rows):
    block = ref[:, first_row : first_row + rows, :]
    return block.reshape(block.shape[0] * rows, block.shape[2])


def slot_tile(window_index, tile):
    atoms, slots = window_index.shape
    lane = lax.broadcasted_iota(jnp.int32, (atoms, HALO), 1) + tile * HALO
    found = jnp.full((atoms, HALO), -1, jnp.int32)
    for slot in range(slots):
        found = jnp.where(window_index[:, slot : slot + 1] == lane, slot, found)
    return found


def spread(slot, coef, quantity, slots):
    values = pick(coef, jnp.maximum(slot, 0) + quantity * slots)
    return jnp.where(slot >= 0, values, 0.0).astype(BF16)


def wide_transpose(rows):
    return jnp.concatenate([rows] * (HALO // rows.shape[0]), axis=0).T


def split_kernel(cut, fm, high_a, low_a, high_b, low_b, sems):
    ranges = (
        (high_a, 0, cut, HALO),
        (low_a, 0, cut, 0),
        (high_b, cut, fm.shape[0] - cut, HALO),
        (low_b, cut, fm.shape[0] - cut, 0),
    )
    copies = [
        pltpu.make_async_copy(
            fm.at[pl.ds(start, size), :, pl.ds(atom, HALO)], part, sems.at[at]
        )
        for at, (part, start, size, atom) in enumerate(ranges)
    ]
    for copy in copies:
        copy.start()
    for copy in copies:
        copy.wait()


def own_kernel(heads, total_atoms, cuts, place, fm, fo, cot, weights, neighbours,
               qkv, scores, slot_own, index_rows, index_wide, wp, wc, token, *rims):
    token[...] = jnp.zeros_like(token)
    for at, (start, stop) in enumerate(cuts):
        rims[2 * at][...] = cot[start:stop, :, HALO:]
        rims[2 * at + 1][...] = cot[start:stop, :, :HALO]
    comps, chan_local = fm.shape[0], fm.shape[1]
    channels = weights.shape[3]
    rows = chan_local // heads
    slots = neighbours.shape[0]
    core, first_atom = place[0], place[1]
    for degree in range(LMAX + 1):
        mix = jnp.concatenate([weights[g, degree] for g in range(3)], axis=0).astype(F32)
        mix = jnp.where(core == 0, mix, pltpu.roll(mix, chan_local, 1))
        wp[degree] = mix.astype(BF16)
        padded = jnp.concatenate([mix, jnp.zeros((chan_local, channels), F32)], axis=0)
        wc[degree] = padded.T[:, : 3 * chan_local].astype(BF16)
    for comp in range(comps):
        feats = jnp.concatenate([fm[comp], fo[comp]], axis=0)
        qkv[comp] = nn(wp[degree_of(comp)], feats).astype(BF16)
    for head in range(heads):
        query = head_rows_of(qkv, head * rows, rows)
        key = head_rows_of(qkv, chan_local + head * rows, rows)
        value = head_rows_of(qkv, 2 * chan_local + head * rows, rows)
        scores[head] = tn(query, key)
        scores[heads + head] = tn(head_rows_of(cot, head * rows, rows), value)
    for half in range(2):
        span = slice(half * HALO, (half + 1) * HALO)
        index = neighbours[:, span] - (first_atom + (half - 1) * HALO)
        index = jnp.where(index < 0, index + total_atoms, index)
        index = jnp.where(index >= total_atoms, index - total_atoms, index)
        index_rows[:, span] = index
        wide = wide_transpose(index)
        index_wide[span, :] = wide
        for tile in range(3):
            slot_own[half, tile] = slot_tile(wide[:, :slots], tile)


def project_halo(start, flm, flo, frm, fro, wp, halo_qkv):
    for comp in range(flm.shape[0]):
        feats = jnp.concatenate(
            [
                jnp.concatenate([flm[comp], frm[comp]], axis=1),
                jnp.concatenate([flo[comp], fro[comp]], axis=1),
            ],
            axis=0,
        )
        halo_qkv[comp] = nn(wp[degree_of(start + comp)], feats).astype(BF16)


def halo_scores(heads, quantity, start, qkv, cot, halo_qkv):
    size, chan_local = halo_qkv.shape[0], cot.shape[1]
    rows = chan_local // heads
    head = quantity % heads
    first = (1 if quantity < heads else 2) * chan_local + head * rows
    source = qkv if quantity < heads else cot
    mine = source[start : start + size, head * rows : (head + 1) * rows, :]
    mine = mine.reshape(size * rows, mine.shape[2])
    theirs = head_rows_of(halo_qkv, first, rows)
    return tn(mine[:, :HALO], theirs[:, :HALO]), tn(mine[:, HALO:], theirs[:, HALO:])


def early_kernel(heads, flm, flo, frm, fro, wp, qkv, cot, halo_qkv, partial, token):
    token[...] = jnp.zeros_like(token)
    project_halo(0, flm, flo, frm, fro, wp, halo_qkv)
    for quantity in range(2 * heads):
        left, right = halo_scores(heads, quantity, 0, qkv, cot, halo_qkv)
        partial[quantity, 0] = left
        partial[quantity, 1] = right


def edge_kernel(heads, score_scale, start, flm, flo, frm, fro, wp, qkv, cot, scores, partial, bias,
                valid, index_rows, index_wide, halo_qkv, grad_bias, message_a, message_b):
    slots = valid.shape[0]
    project_halo(start, flm, flo, frm, fro, wp, halo_qkv)
    lane = lax.broadcasted_iota(jnp.int32, (HALO, 2 * heads * slots), 1)
    gathered = [jnp.zeros((HALO, 2 * heads * slots), F32) for _ in range(2)]
    for quantity in range(2 * heads):
        left, right = halo_scores(heads, quantity, start, qkv, cot, halo_qkv)
        left, right = left + partial[quantity, 0], right + partial[quantity, 1]
        for half in range(2):
            own = scores[quantity, half * HALO : (half + 1) * HALO, :]
            own = [own[:, :HALO], own[:, HALO:]]
            tiles = [left] + own if half == 0 else own + [right]
            index = index_wide[half * HALO : (half + 1) * HALO, :]
            inner, tile_of = index & (HALO - 1), index >> 7
            values = jnp.where(
                tile_of == 0,
                pick(tiles[0], inner),
                jnp.where(tile_of == 1, pick(tiles[1], inner), pick(tiles[2], inner)),
            )
            gathered[half] = jnp.where(lane // slots == quantity, values, gathered[half])
    for half, message in enumerate((message_a, message_b)):
        span = slice(half * HALO, (half + 1) * HALO)
        edges = gathered[half].T.reshape(2, heads, slots, HALO)
        squashed = jnp.tanh(edges[0] * (score_scale / SOFT_CAP))
        logits = SOFT_CAP * squashed + bias[:, :, span]
        live = valid[:, span][None] > 0
        weight = jnp.where(live, jnp.exp(logits), 0.0)
        attention = weight / jnp.sum(weight, axis=1, keepdims=True)
        grad_attn = edges[1]
        grad_logit = attention * (
            grad_attn - jnp.sum(attention * grad_attn, axis=1, keepdims=True)
        )
        grad_bias[:, :, span] = grad_logit
        grad_raw = score_scale * grad_logit * (1.0 - squashed * squashed)
        index = index_rows[:, span]
        both = jnp.stack([grad_raw, attention]).reshape(2 * heads, slots, HALO)
        merged = jnp.zeros_like(both)
        for slot in range(slots):
            same = (index == index[slot : slot + 1, :])[None]
            merged = merged + jnp.where(same, both[:, slot : slot + 1, :], 0.0)
        atom = lax.broadcasted_iota(jnp.int32, (slots, HALO), 1)
        message[: 2 * heads * slots, :] = merged.reshape(2 * heads * slots, HALO).astype(BF16)
        message[2 * heads * slots :, :] = (index - HALO - atom).astype(F32).astype(BF16)


def joined_rows(early, late, first_row, rows):
    return jnp.concatenate(
        [head_rows_of(early, first_row, rows), head_rows_of(late, first_row, rows)], axis=0
    )


def grads_kernel(heads, slots, place, fm, fo, flm_a, flo_a, frm_a, fro_a, flm_b, flo_b, frm_b,
                 fro_b, qkv, halo_a, halo_b, cot, slot_own, message_a, message_b, grad_query, own_key, own_value, kept, sent_1, sent_2,
                 sent_3, ext, weight_terms):
    comps, chan_local = fm.shape[0], fm.shape[1]
    rows = chan_local // heads
    atoms = 2 * HALO
    core = place[0]
    cut = flm_a.shape[0]
    early, late = (flm_a, flo_a, frm_a, fro_a), (flm_b, flo_b, frm_b, fro_b)
    empty = jnp.zeros((HALO, HALO), BF16)
    coefs = [message[: 2 * heads * slots, :].astype(F32).T for message in (message_a, message_b)]
    for head in range(heads):
        tables = []
        for quantity in (head, heads + head):
            halves = []
            for half in range(2):
                tiles = [spread(slot_own[half, t], coefs[half], quantity, slots) for t in range(3)]
                tiles = tiles + [empty] if half == 0 else [empty] + tiles
                halves.append(jnp.concatenate(tiles, axis=1))
            tables.append(jnp.concatenate(halves, axis=0))
        raw_table, attn_table = tables
        query = head_rows_of(qkv, head * rows, rows)
        key = head_rows_of(qkv, chan_local + head * rows, rows)
        halo_key = joined_rows(halo_a, halo_b, chan_local + head * rows, rows)
        key_ext = jnp.concatenate([halo_key[:, :HALO], key, halo_key[:, HALO:]], axis=1)
        span = slice(head * rows, (head + 1) * rows)
        value_span = slice(chan_local + head * rows, chan_local + (head + 1) * rows)
        grad_query[:, span, :] = nt(key_ext, raw_table).astype(BF16).reshape(comps, rows, atoms)
        key_sums = nn(query, raw_table)
        own_key[:, span, :] = key_sums[:, HALO : HALO + atoms].reshape(comps, rows, atoms)
        ext[:, span, :] = key_sums.astype(BF16).reshape(comps, rows, atoms + 2 * HALO)
        value_sums = nn(head_rows_of(cot, head * rows, rows), attn_table)
        own_value[:, span, :] = value_sums[:, HALO : HALO + atoms].reshape(comps, rows, atoms)
        ext[:, value_span, :] = value_sums.astype(BF16).reshape(comps, rows, atoms + 2 * HALO)
    for degree in range(LMAX + 1):
        query_total = jnp.zeros((chan_local, 2 * chan_local), F32)
        keyval_total = jnp.zeros((2 * chan_local, 2 * chan_local), F32)
        for comp in range(degree * degree, (degree + 1) * (degree + 1)):
            own = jnp.concatenate([fm[comp], fo[comp]], axis=0)
            at = comp if comp < cut else comp - cut
            flm, flo, frm, fro = early if comp < cut else late
            wide = jnp.concatenate(
                [
                    jnp.concatenate([flm[at], fm[comp], frm[at]], axis=1),
                    jnp.concatenate([flo[at], fo[comp], fro[at]], axis=1),
                ],
                axis=0,
            )
            query_total = query_total + nt(grad_query[comp], own)
            keyval_total = keyval_total + nt(ext[comp], wide)
        total = jnp.concatenate([query_total, keyval_total], axis=0)
        total = jnp.where(core == 0, total, pltpu.roll(total, chan_local, 1))
        for g in range(3):
            weight_terms[g * (LMAX + 1) + degree] = total[g * chan_local : (g + 1) * chan_local]
    piece = chan_local // 4
    spot = place[2]
    for delta, part in enumerate((kept, sent_1, sent_2, sent_3)):
        first = pl.multiple_of((spot ^ delta) * piece, piece)
        part[...] = weight_terms[:, pl.ds(first, piece), :].astype(part.dtype)


def halo_slots(message_left, message_right, quantities, slots):
    coefs, tables = [], []
    for message, tile in ((message_left, 2), (message_right, 0)):
        coefs.append(message[: quantities * slots, :].astype(F32).T)
        offset = message[quantities * slots :, :].astype(F32).astype(jnp.int32)
        atom = lax.broadcasted_iota(jnp.int32, offset.shape, 1)
        tables.append(slot_tile(wide_transpose(offset + HALO + atom)[:, :slots], tile))
    return coefs, tables


def key_kernel(heads, slots, grad_query, own_key, halo_a, halo_b, message_left, message_right, wc,
               terms, grad):
    comps, chan_local = grad_query.shape[0], grad_query.shape[1]
    rows = chan_local // heads
    grad[:, :chan_local, :] = grad_query[...]
    coefs, tables = halo_slots(message_left, message_right, 2 * heads, slots)
    for head in range(heads):
        query = joined_rows(halo_a, halo_b, head * rows, rows)
        rim = jnp.concatenate(
            [
                nn(query[:, :HALO], spread(tables[0], coefs[0], head, slots)),
                nn(query[:, HALO:], spread(tables[1], coefs[1], head, slots)),
            ],
            axis=1,
        )
        total = head_rows_of(own_key, head * rows, rows) + rim
        span = slice(chan_local + head * rows, chan_local + (head + 1) * rows)
        grad[:, span, :] = total.astype(BF16).reshape(comps, rows, 2 * HALO)
    for comp in range(comps):
        terms[comp] = nn(wc[degree_of(comp)][:, : 2 * chan_local], grad[comp])


def value_kernel(heads, slots, start, own_value, cl, cr, message_left, message_right, wc, terms,
                 mine, token, *theirs):
    *theirs, grad = theirs
    token[...] = jnp.zeros_like(token)
    comps, chan_local = cl.shape[0], cl.shape[1]
    rows = chan_local // heads
    coefs, tables = halo_slots(message_left, message_right, 2 * heads, slots)
    for head in range(heads):
        span = slice(head * rows, (head + 1) * rows)
        rim = jnp.concatenate(
            [
                nn(head_rows_of(cl, head * rows, rows),
                   spread(tables[0], coefs[0], heads + head, slots)),
                nn(head_rows_of(cr, head * rows, rows),
                   spread(tables[1], coefs[1], heads + head, slots)),
            ],
            axis=1,
        )
        own = own_value[start : start + comps, span, :].reshape(comps * rows, 2 * HALO)
        grad[:, span, :] = (own + rim).astype(BF16).reshape(comps, rows, 2 * HALO)
    for comp in range(comps):
        mix = wc[degree_of(start + comp)][:, 2 * chan_local :]
        total = terms[start + comp] + nn(mix, grad[comp])
        mine[comp] = total[:chan_local]
        part = theirs[0].shape[0]
        theirs[comp // part][comp % part] = total[chan_local:].astype(BF16)


def finish_kernel(parts, *refs):
    *refs, out = refs
    start = 0
    for count in parts:
        mine, theirs, refs = refs[0], refs[1 : count + 1], refs[count + 1 :]
        at = 0
        for part in theirs:
            size = part.shape[0]
            total = mine[at : at + size] + part[...].astype(F32)
            out[start + at : start + at + size] = total.astype(BF16)
            at += size
        start += at


def gather_kernel(place, part_0, part_1, part_2, part_3, out):
    piece = part_0.shape[1]
    spot = place[2]
    for delta, part in enumerate((part_0, part_1, part_2, part_3)):
        first = pl.multiple_of((spot ^ delta) * piece, piece)
        out[:, pl.ds(first, piece), :] = part[...].astype(F32)


def call(kernel, args, outs, scratch=(), scalars=0, limit=24, stay=(), tokens=(), flops=0):
    whole = pl.BlockSpec(memory_space=pltpu.VMEM)
    small = pl.BlockSpec(memory_space=pltpu.SMEM)
    args = [
        pltpu.with_memory_space_constraint(a, pltpu.VMEM) if at in stay else a
        for at, a in enumerate(args)
    ]
    count = len(args)

    def body(*refs):
        kernel(*refs[:count], *refs[count + len(tokens) :])

    return pl.pallas_call(
        body,
        out_shape=tuple(outs),
        in_specs=[small] * scalars
        + [whole] * (count - scalars)
        + [pl.BlockSpec(memory_space=pl.ANY)] * len(tokens),
        out_specs=tuple([whole] * len(outs)),
        scratch_shapes=list(scratch),
        compiler_params=pltpu.CompilerParams(vmem_limit_bytes=limit * 1024 * 1024),
        cost_estimate=pl.CostEstimate(flops=flops, bytes_accessed=1024, transcendentals=0),
    )(*args, *tokens)


def after(values, tokens):
    anywhere = pl.BlockSpec(memory_space=pl.ANY)
    count = len(values)

    def kernel(*refs):
        pass

    return pl.pallas_call(
        kernel,
        out_shape=tuple(jax.ShapeDtypeStruct(v.shape, v.dtype) for v in values),
        in_specs=[anywhere] * (count + len(tokens)),
        out_specs=tuple([anywhere] * count),
        input_output_aliases={i: i for i in range(count)},
        compiler_params=pltpu.CompilerParams(vmem_limit_bytes=1024 * 1024),
        cost_estimate=pl.CostEstimate(flops=0, bytes_accessed=1024, transcendentals=0),
    )(*values, *tokens)


def shifted(value, axis, steps):
    count = lax.axis_size(axis)
    pairs = [(source, (source + steps) % count) for source in range(count)]
    return lax.ppermute(value, axis, pairs)


def exchanged(value, axis, offset):
    count = lax.axis_size(axis)
    return lax.ppermute(value, axis, [(source, source ^ offset) for source in range(count)])


def on_device(features, weights, cotangent, edge_bias, neighbours, valid_mask):
    chan_local, comps, atoms_dev = features.shape
    heads, slots = edge_bias.shape[0], edge_bias.shape[1]
    channels = weights.shape[2]
    assert atoms_dev == 2 * HALO and channels == 2 * chan_local
    score_scale = 1.0 / math.sqrt(chan_local // heads * comps)
    total_atoms = atoms_dev * lax.axis_size("atom")
    count = lax.axis_size("atom")
    assert count >= 4 and count & (count - 1) == 0
    atom_place = lax.axis_index("atom")
    cut_bits = (1, 2) if count >= 8 else (0, 1)
    spot = (atom_place >> cut_bits[0]) & 3
    place = jnp.stack([lax.axis_index("chan"), atom_place * atoms_dev, spot])
    place = place.astype(jnp.int32)
    feature_cut = comps // 2
    cotangent_cut = 2 * comps // 3
    cuts = ((0, cotangent_cut), (cotangent_cut, comps))

    def held(*dims, dtype=F32):
        return pltpu.VMEM(dims, dtype)

    def plain(*dims, dtype=F32):
        return jax.ShapeDtypeStruct(dims, dtype)

    fm = jnp.transpose(features, (1, 0, 2))
    cot = jnp.transpose(cotangent, (1, 0, 2))
    mix = jnp.transpose(weights, (0, 1, 3, 2))
    anywhere = pl.BlockSpec(memory_space=pl.ANY)
    sizes = (feature_cut, feature_cut, comps - feature_cut, comps - feature_cut)
    high_a, low_a, high_b, low_b = pl.pallas_call(
        functools.partial(split_kernel, feature_cut),
        out_shape=tuple(held(size, chan_local, HALO, dtype=BF16) for size in sizes),
        in_specs=[anywhere],
        out_specs=(pl.BlockSpec(memory_space=pltpu.VMEM),) * 4,
        scratch_shapes=[pltpu.SemaphoreType.DMA((4,))],
        compiler_params=pltpu.CompilerParams(vmem_limit_bytes=4 * 1024 * 1024),
    )(pltpu.with_memory_space_constraint(fm, pltpu.HBM))
    flm_a = shifted(high_a, "atom", 1)
    frm_a = shifted(low_a, "atom", -1)
    flm_b = shifted(high_b, "atom", 1)
    frm_b = shifted(low_b, "atom", -1)
    fo = shifted(fm, "chan", 1)

    qkv, scores, slot_own, index_rows, index_wide, wp, wc, token, *rims = call(
        functools.partial(own_kernel, heads, total_atoms, cuts),
        (place, fm, fo, cot, mix, neighbours),
        (
            held(comps, 3 * chan_local, atoms_dev, dtype=BF16),
            held(2 * heads, atoms_dev, atoms_dev),
            held(2, 3, HALO, HALO, dtype=jnp.int32),
            held(slots, atoms_dev, dtype=jnp.int32),
            held(atoms_dev, HALO, dtype=jnp.int32),
            held(LMAX + 1, 3 * chan_local, channels, dtype=BF16),
            held(LMAX + 1, channels, 3 * chan_local, dtype=BF16),
            plain(8, HALO),
            *(
                plain(stop - start, chan_local, HALO, dtype=BF16)
                for start, stop in cuts
                for _ in range(2)
            ),
        ),
        scalars=1,
        stay=(1, 2, 3),
        flops=12 * 10**9,
    )
    flm_a, frm_a = after((flm_a, frm_a), (token,))
    flo_a = shifted(flm_a, "chan", 1)
    fro_a = shifted(frm_a, "chan", 1)
    halo_a, partial, token = call(
        functools.partial(early_kernel, heads),
        (flm_a, flo_a, frm_a, fro_a, wp, qkv, cot),
        (
            held(feature_cut, 3 * chan_local, atoms_dev, dtype=BF16),
            held(2 * heads, 2, HALO, HALO),
            plain(8, HALO),
        ),
        stay=tuple(range(7)),
    )
    rims[:2] = after(rims[:2], (token,))
    flm_b, frm_b = after((flm_b, frm_b), (token,))
    halos = [(shifted(rims[0], "atom", 1), shifted(rims[1], "atom", -1))]
    flo_b = shifted(flm_b, "chan", 1)
    fro_b = shifted(frm_b, "chan", 1)
    halo_b, grad_bias, message_a, message_b = call(
        functools.partial(edge_kernel, heads, score_scale, feature_cut),
        (flm_b, flo_b, frm_b, fro_b, wp, qkv, cot, scores, partial, edge_bias, valid_mask,
         index_rows, index_wide),
        (
            held(comps - feature_cut, 3 * chan_local, atoms_dev, dtype=BF16),
            plain(heads, slots, atoms_dev),
            held((2 * heads + 1) * slots, HALO, dtype=BF16),
            held((2 * heads + 1) * slots, HALO, dtype=BF16),
        ),
        stay=(0, 1, 2, 3, 4, 5, 6, 7, 8, 11, 12),
    )
    message_left = shifted(message_b, "atom", 1)
    message_right = shifted(message_a, "atom", -1)
    piece = (3 * (LMAX + 1), chan_local // 4, channels)
    grad_query, own_key, own_value, kept, *sent = call(
        functools.partial(grads_kernel, heads, slots),
        (place, fm, fo, flm_a, flo_a, frm_a, fro_a, flm_b, flo_b, frm_b, fro_b, qkv, halo_a, halo_b,
         cot, slot_own, message_a, message_b),
        (
            held(comps, chan_local, atoms_dev, dtype=BF16),
            held(comps, chan_local, atoms_dev),
            held(comps, chan_local, atoms_dev),
            held(*piece),
            plain(*piece, dtype=BF16),
            plain(*piece, dtype=BF16),
            plain(*piece, dtype=BF16),
        ),
        scratch=[
            pltpu.VMEM((comps, 2 * chan_local, 2 * atoms_dev), BF16),
            pltpu.VMEM((3 * (LMAX + 1), chan_local, channels), F32),
        ],
        scalars=1,
        stay=tuple(range(1, 18)),
    )
    for delta, part in enumerate(sent, 1):
        kept = kept + exchanged(part, "atom", delta << cut_bits[0]).astype(F32)
    rest = [bit for bit in range(count.bit_length() - 1) if bit not in cut_bits]
    while rest:
        offsets = [1 << bit for bit in rest[:2]]
        rest = rest[2:]
        rounded = kept.astype(BF16)
        offsets += [sum(offsets)] * (len(offsets) - 1)
        arrived = [exchanged(rounded, "atom", offset) for offset in offsets]
        kept = functools.reduce(lambda total, part: total + part.astype(F32), arrived, kept)
    rims[2:] = after(rims[2:], (*arrived, *halos[0]))
    halos.append((shifted(rims[2], "atom", 1), shifted(rims[3], "atom", -1)))
    rounded = kept.astype(BF16)
    pieces = [rounded] + [exchanged(rounded, "atom", d << cut_bits[0]) for d in range(1, 4)]
    (grad_weights,) = call(
        gather_kernel,
        (place, *pieces),
        (plain(3 * (LMAX + 1), chan_local, channels),),
        scalars=1,
        limit=8,
    )
    (terms,) = call(
        functools.partial(key_kernel, heads, slots),
        (grad_query, own_key, halo_a, halo_b, message_left, message_right, wc),
        (held(comps, channels, atoms_dev),),
        scratch=[pltpu.VMEM((comps, 2 * chan_local, atoms_dev), BF16)],
        limit=16,
        stay=(0, 1, 2, 3, 6),
        tokens=tuple(arrived),
    )
    parts, counts = [], []
    tokens = tuple(arrived)
    for (start, stop), (cl, cr) in zip(cuts, halos):
        size = stop - start
        part = -(-size // -(-size // (comps // 6)))
        sizes = [min(part, size - at) for at in range(0, size, part)]
        mine, token, *theirs = call(
            functools.partial(value_kernel, heads, slots, start),
            (own_value, cl, cr, message_left, message_right, wc, terms),
            (
                held(size, chan_local, atoms_dev),
                plain(8, HALO),
                *(held(some, chan_local, atoms_dev, dtype=BF16) for some in sizes),
            ),
            scratch=[pltpu.VMEM((size, chan_local, atoms_dev), BF16)],
            limit=16,
            stay=(0, 5, 6),
            tokens=tokens,
        )
        tokens = (token, *pieces)
        counts.append(len(sizes))
        parts += [mine, *(shifted(some, "chan", 1) for some in theirs)]
    (out,) = call(
        functools.partial(finish_kernel, counts),
        parts,
        (plain(comps, chan_local, atoms_dev, dtype=BF16),),
        limit=8,
        stay=tuple(range(len(parts))),
    )
    grad_features = jnp.transpose(out, (1, 0, 2))
    grad_weights = grad_weights.reshape(3, LMAX + 1, chan_local, channels)
    grad_weights = jnp.transpose(grad_weights, (0, 1, 3, 2))
    return grad_features, grad_weights, grad_bias


def solution(mesh):
    in_specs = (
        P("chan", None, "atom"),
        P(None, None, None, "chan"),
        P("chan", None, "atom"),
        P("chan", None, "atom"),
        P(None, "atom"),
        P(None, "atom"),
    )
    out_specs = (P("chan", None, "atom"), P(None, None, None, "chan"), P("chan", None, "atom"))
    return jax.shard_map(
        on_device, mesh=mesh, in_specs=in_specs, out_specs=out_specs, check_vma=False
    )
```

```python
import functools
import math

import jax
import jax.numpy as jnp
from jax import lax
from jax.experimental import pallas as pl
from jax.experimental.pallas import tpu as pltpu
from jax.sharding import PartitionSpec as P

LMAX = 6
HALO = 128
SOFT_CAP = 10.0
F32 = jnp.float32
BF16 = jnp.bfloat16


def degree_of(comp):
    return math.isqrt(comp)


def nn(lhs, rhs):
    return lax.dot_general(lhs, rhs, (((1,), (0,)), ((), ())), preferred_element_type=F32)


def nt(lhs, rhs):
    return lax.dot_general(lhs, rhs, (((1,), (1,)), ((), ())), preferred_element_type=F32)


def tn(lhs, rhs):
    return lax.dot_general(lhs, rhs, (((0,), (0,)), ((), ())), preferred_element_type=F32)


def pick(table, index):
    return jnp.take_along_axis(table, index, axis=1, mode="promise_in_bounds")


def head_rows_of(ref, first_row, rows):
    block = ref[:, first_row : first_row + rows, :]
    return block.reshape(block.shape[0] * rows, block.shape[2])


def slot_tile(window_index, tile):
    atoms, slots = window_index.shape
    lane = lax.broadcasted_iota(jnp.int32, (atoms, HALO), 1) + tile * HALO
    found = jnp.full((atoms, HALO), -1, jnp.int32)
    for slot in range(slots):
        found = jnp.where(window_index[:, slot : slot + 1] == lane, slot, found)
    return found


def spread(slot, coef, quantity, slots):
    values = pick(coef, jnp.maximum(slot, 0) + quantity * slots)
    return jnp.where(slot >= 0, values, 0.0).astype(BF16)


def wide_transpose(rows):
    return jnp.concatenate([rows] * (HALO // rows.shape[0]), axis=0).T


def split_kernel(cut, fm, high_a, low_a, high_b, low_b, sems):
    ranges = (
        (high_a, 0, cut, HALO),
        (low_a, 0, cut, 0),
        (high_b, cut, fm.shape[0] - cut, HALO),
        (low_b, cut, fm.shape[0] - cut, 0),
    )
    copies = [
        pltpu.make_async_copy(
            fm.at[pl.ds(start, size), :, pl.ds(atom, HALO)], part, sems.at[at]
        )
        for at, (part, start, size, atom) in enumerate(ranges)
    ]
    for copy in copies:
        copy.start()
    for copy in copies:
        copy.wait()


def own_kernel(heads, total_atoms, cuts, place, fm, fo, cot, weights, neighbours,
               qkv, scores, slot_own, index_rows, index_wide, wp, wc, token, *rims):
    token[...] = jnp.zeros_like(token)
    for at, (start, stop) in enumerate(cuts):
        rims[2 * at][...] = cot[start:stop, :, HALO:]
        rims[2 * at + 1][...] = cot[start:stop, :, :HALO]
    comps, chan_local = fm.shape[0], fm.shape[1]
    channels = weights.shape[3]
    rows = chan_local // heads
    slots = neighbours.shape[0]
    core, first_atom = place[0], place[1]
    for degree in range(LMAX + 1):
        mix = jnp.concatenate([weights[g, degree] for g in range(3)], axis=0).astype(F32)
        mix = jnp.where(core == 0, mix, pltpu.roll(mix, chan_local, 1))
        wp[degree] = mix.astype(BF16)
        padded = jnp.concatenate([mix, jnp.zeros((chan_local, channels), F32)], axis=0)
        wc[degree] = padded.T[:, : 3 * chan_local].astype(BF16)
    for comp in range(comps):
        feats = jnp.concatenate([fm[comp], fo[comp]], axis=0)
        qkv[comp] = nn(wp[degree_of(comp)], feats).astype(BF16)
    for head in range(heads):
        query = head_rows_of(qkv, head * rows, rows)
        key = head_rows_of(qkv, chan_local + head * rows, rows)
        value = head_rows_of(qkv, 2 * chan_local + head * rows, rows)
        scores[head] = tn(query, key)
        scores[heads + head] = tn(head_rows_of(cot, head * rows, rows), value)
    for half in range(2):
        span = slice(half * HALO, (half + 1) * HALO)
        index = neighbours[:, span] - (first_atom + (half - 1) * HALO)
        index = jnp.where(index < 0, index + total_atoms, index)
        index = jnp.where(index >= total_atoms, index - total_atoms, index)
        index_rows[:, span] = index
        wide = wide_transpose(index)
        index_wide[span, :] = wide
        for tile in range(3):
            slot_own[half, tile] = slot_tile(wide[:, :slots], tile)


def project_halo(start, flm, flo, frm, fro, wp, halo_qkv):
    for comp in range(flm.shape[0]):
        feats = jnp.concatenate(
            [
                jnp.concatenate([flm[comp], frm[comp]], axis=1),
                jnp.concatenate([flo[comp], fro[comp]], axis=1),
            ],
            axis=0,
        )
        halo_qkv[comp] = nn(wp[degree_of(start + comp)], feats).astype(BF16)


def halo_scores(heads, quantity, start, qkv, cot, halo_qkv):
    size, chan_local = halo_qkv.shape[0], cot.shape[1]
    rows = chan_local // heads
    head = quantity % heads
    first = (1 if quantity < heads else 2) * chan_local + head * rows
    source = qkv if quantity < heads else cot
    mine = source[start : start + size, head * rows : (head + 1) * rows, :]
    mine = mine.reshape(size * rows, mine.shape[2])
    theirs = head_rows_of(halo_qkv, first, rows)
    return tn(mine[:, :HALO], theirs[:, :HALO]), tn(mine[:, HALO:], theirs[:, HALO:])


def early_kernel(heads, flm, flo, frm, fro, wp, qkv, cot, halo_qkv, partial, token):
    token[...] = jnp.zeros_like(token)
    project_halo(0, flm, flo, frm, fro, wp, halo_qkv)
    for quantity in range(2 * heads):
        left, right = halo_scores(heads, quantity, 0, qkv, cot, halo_qkv)
        partial[quantity, 0] = left
        partial[quantity, 1] = right


def edge_kernel(heads, score_scale, start, flm, flo, frm, fro, wp, qkv, cot, scores, partial, bias,
                valid, index_rows, index_wide, halo_qkv, grad_bias, message_a, message_b):
    slots = valid.shape[0]
    project_halo(start, flm, flo, frm, fro, wp, halo_qkv)
    lane = lax.broadcasted_iota(jnp.int32, (HALO, 2 * heads * slots), 1)
    gathered = [jnp.zeros((HALO, 2 * heads * slots), F32) for _ in range(2)]
    for quantity in range(2 * heads):
        left, right = halo_scores(heads, quantity, start, qkv, cot, halo_qkv)
        left, right = left + partial[quantity, 0], right + partial[quantity, 1]
        for half in range(2):
            own = scores[quantity, half * HALO : (half + 1) * HALO, :]
            own = [own[:, :HALO], own[:, HALO:]]
            tiles = [left] + own if half == 0 else own + [right]
            index = index_wide[half * HALO : (half + 1) * HALO, :]
            inner, tile_of = index & (HALO - 1), index >> 7
            values = jnp.where(
                tile_of == 0,
                pick(tiles[0], inner),
                jnp.where(tile_of == 1, pick(tiles[1], inner), pick(tiles[2], inner)),
            )
            gathered[half] = jnp.where(lane // slots == quantity, values, gathered[half])
    for half, message in enumerate((message_a, message_b)):
        span = slice(half * HALO, (half + 1) * HALO)
        edges = gathered[half].T.reshape(2, heads, slots, HALO)
        squashed = jnp.tanh(edges[0] * (score_scale / SOFT_CAP))
        logits = SOFT_CAP * squashed + bias[:, :, span]
        live = valid[:, span][None] > 0
        weight = jnp.where(live, jnp.exp(logits), 0.0)
        attention = weight / jnp.sum(weight, axis=1, keepdims=True)
        grad_attn = edges[1]
        grad_logit = attention * (
            grad_attn - jnp.sum(attention * grad_attn, axis=1, keepdims=True)
        )
        grad_bias[:, :, span] = grad_logit
        grad_raw = score_scale * grad_logit * (1.0 - squashed * squashed)
        index = index_rows[:, span]
        both = jnp.stack([grad_raw, attention]).reshape(2 * heads, slots, HALO)
        merged = jnp.zeros_like(both)
        for slot in range(slots):
            same = (index == index[slot : slot + 1, :])[None]
            merged = merged + jnp.where(same, both[:, slot : slot + 1, :], 0.0)
        atom = lax.broadcasted_iota(jnp.int32, (slots, HALO), 1)
        message[: 2 * heads * slots, :] = merged.reshape(2 * heads * slots, HALO).astype(BF16)
        message[2 * heads * slots :, :] = (index - HALO - atom).astype(F32).astype(BF16)


def joined_rows(early, late, first_row, rows):
    return jnp.concatenate(
        [head_rows_of(early, first_row, rows), head_rows_of(late, first_row, rows)], axis=0
    )


def grads_kernel(heads, slots, place, fm, fo, flm_a, flo_a, frm_a, fro_a, flm_b, flo_b, frm_b,
                 fro_b, qkv, halo_a, halo_b, cot, slot_own, message_a, message_b, grad_query, own_key, own_value, kept, sent_1, sent_2,
                 sent_3, ext, weight_terms):
    comps, chan_local = fm.shape[0], fm.shape[1]
    rows = chan_local // heads
    atoms = 2 * HALO
    core = place[0]
    cut = flm_a.shape[0]
    early, late = (flm_a, flo_a, frm_a, fro_a), (flm_b, flo_b, frm_b, fro_b)
    empty = jnp.zeros((HALO, HALO), BF16)
    coefs = [message[: 2 * heads * slots, :].astype(F32).T for message in (message_a, message_b)]
    for head in range(heads):
        tables = []
        for quantity in (head, heads + head):
            halves = []
            for half in range(2):
                tiles = [spread(slot_own[half, t], coefs[half], quantity, slots) for t in range(3)]
                tiles = tiles + [empty] if half == 0 else [empty] + tiles
                halves.append(jnp.concatenate(tiles, axis=1))
            tables.append(jnp.concatenate(halves, axis=0))
        raw_table, attn_table = tables
        query = head_rows_of(qkv, head * rows, rows)
        key = head_rows_of(qkv, chan_local + head * rows, rows)
        halo_key = joined_rows(halo_a, halo_b, chan_local + head * rows, rows)
        key_ext = jnp.concatenate([halo_key[:, :HALO], key, halo_key[:, HALO:]], axis=1)
        span = slice(head * rows, (head + 1) * rows)
        value_span = slice(chan_local + head * rows, chan_local + (head + 1) * rows)
        grad_query[:, span, :] = nt(key_ext, raw_table).astype(BF16).reshape(comps, rows, atoms)
        key_sums = nn(query, raw_table)
        own_key[:, span, :] = key_sums[:, HALO : HALO + atoms].reshape(comps, rows, atoms)
        ext[:, span, :] = key_sums.astype(BF16).reshape(comps, rows, atoms + 2 * HALO)
        value_sums = nn(head_rows_of(cot, head * rows, rows), attn_table)
        own_value[:, span, :] = value_sums[:, HALO : HALO + atoms].reshape(comps, rows, atoms)
        ext[:, value_span, :] = value_sums.astype(BF16).reshape(comps, rows, atoms + 2 * HALO)
    for degree in range(LMAX + 1):
        query_total = jnp.zeros((chan_local, 2 * chan_local), F32)
        keyval_total = jnp.zeros((2 * chan_local, 2 * chan_local), F32)
        for comp in range(degree * degree, (degree + 1) * (degree + 1)):
            own = jnp.concatenate([fm[comp], fo[comp]], axis=0)
            at = comp if comp < cut else comp - cut
            flm, flo, frm, fro = early if comp < cut else late
            wide = jnp.concatenate(
                [
                    jnp.concatenate([flm[at], fm[comp], frm[at]], axis=1),
                    jnp.concatenate([flo[at], fo[comp], fro[at]], axis=1),
                ],
                axis=0,
            )
            query_total = query_total + nt(grad_query[comp], own)
            keyval_total = keyval_total + nt(ext[comp], wide)
        total = jnp.concatenate([query_total, keyval_total], axis=0)
        total = jnp.where(core == 0, total, pltpu.roll(total, chan_local, 1))
        for g in range(3):
            weight_terms[g * (LMAX + 1) + degree] = total[g * chan_local : (g + 1) * chan_local]
    piece = chan_local // 4
    spot = place[2]
    for delta, part in enumerate((kept, sent_1, sent_2, sent_3)):
        first = pl.multiple_of((spot ^ delta) * piece, piece)
        part[...] = weight_terms[:, pl.ds(first, piece), :].astype(part.dtype)


def halo_slots(message_left, message_right, quantities, slots):
    coefs, tables = [], []
    for message, tile in ((message_left, 2), (message_right, 0)):
        coefs.append(message[: quantities * slots, :].astype(F32).T)
        offset = message[quantities * slots :, :].astype(F32).astype(jnp.int32)
        atom = lax.broadcasted_iota(jnp.int32, offset.shape, 1)
        tables.append(slot_tile(wide_transpose(offset + HALO + atom)[:, :slots], tile))
    return coefs, tables


def key_kernel(heads, slots, grad_query, own_key, halo_a, halo_b, message_left, message_right, wc,
               terms, grad):
    comps, chan_local = grad_query.shape[0], grad_query.shape[1]
    rows = chan_local // heads
    grad[:, :chan_local, :] = grad_query[...]
    coefs, tables = halo_slots(message_left, message_right, 2 * heads, slots)
    for head in range(heads):
        query = joined_rows(halo_a, halo_b, head * rows, rows)
        rim = jnp.concatenate(
            [
                nn(query[:, :HALO], spread(tables[0], coefs[0], head, slots)),
                nn(query[:, HALO:], spread(tables[1], coefs[1], head, slots)),
            ],
            axis=1,
        )
        total = head_rows_of(own_key, head * rows, rows) + rim
        span = slice(chan_local + head * rows, chan_local + (head + 1) * rows)
        grad[:, span, :] = total.astype(BF16).reshape(comps, rows, 2 * HALO)
    for comp in range(comps):
        terms[comp] = nn(wc[degree_of(comp)][:, : 2 * chan_local], grad[comp])


def value_kernel(heads, slots, start, own_value, cl, cr, message_left, message_right, wc, terms,
                 mine, token, *theirs):
    *theirs, grad = theirs
    token[...] = jnp.zeros_like(token)
    comps, chan_local = cl.shape[0], cl.shape[1]
    rows = chan_local // heads
    coefs, tables = halo_slots(message_left, message_right, 2 * heads, slots)
    for head in range(heads):
        span = slice(head * rows, (head + 1) * rows)
        rim = jnp.concatenate(
            [
                nn(head_rows_of(cl, head * rows, rows),
                   spread(tables[0], coefs[0], heads + head, slots)),
                nn(head_rows_of(cr, head * rows, rows),
                   spread(tables[1], coefs[1], heads + head, slots)),
            ],
            axis=1,
        )
        own = own_value[start : start + comps, span, :].reshape(comps * rows, 2 * HALO)
        grad[:, span, :] = (own + rim).astype(BF16).reshape(comps, rows, 2 * HALO)
    for comp in range(comps):
        mix = wc[degree_of(start + comp)][:, 2 * chan_local :]
        total = terms[start + comp] + nn(mix, grad[comp])
        mine[comp] = total[:chan_local]
        part = theirs[0].shape[0]
        theirs[comp // part][comp % part] = total[chan_local:].astype(BF16)


def finish_kernel(parts, *refs):
    *refs, out = refs
    start = 0
    for count in parts:
        mine, theirs, refs = refs[0], refs[1 : count + 1], refs[count + 1 :]
        at = 0
        for part in theirs:
            size = part.shape[0]
            total = mine[at : at + size] + part[...].astype(F32)
            out[start + at : start + at + size] = total.astype(BF16)
            at += size
        start += at


def gather_kernel(place, part_0, part_1, part_2, part_3, out, token):
    token[...] = jnp.zeros_like(token)
    piece = part_0.shape[1]
    spot = place[2]
    for delta, part in enumerate((part_0, part_1, part_2, part_3)):
        first = pl.multiple_of((spot ^ delta) * piece, piece)
        out[:, pl.ds(first, piece), :] = part[...].astype(F32)


def call(kernel, args, outs, scratch=(), scalars=0, limit=24, stay=(), tokens=(), flops=0):
    whole = pl.BlockSpec(memory_space=pltpu.VMEM)
    small = pl.BlockSpec(memory_space=pltpu.SMEM)
    args = [
        pltpu.with_memory_space_constraint(a, pltpu.VMEM) if at in stay else a
        for at, a in enumerate(args)
    ]
    count = len(args)

    def body(*refs):
        kernel(*refs[:count], *refs[count + len(tokens) :])

    return pl.pallas_call(
        body,
        out_shape=tuple(outs),
        in_specs=[small] * scalars
        + [whole] * (count - scalars)
        + [pl.BlockSpec(memory_space=pl.ANY)] * len(tokens),
        out_specs=tuple([whole] * len(outs)),
        scratch_shapes=list(scratch),
        compiler_params=pltpu.CompilerParams(vmem_limit_bytes=limit * 1024 * 1024),
        cost_estimate=pl.CostEstimate(flops=flops, bytes_accessed=1024, transcendentals=0),
    )(*args, *tokens)


def after(values, tokens):
    anywhere = pl.BlockSpec(memory_space=pl.ANY)
    count = len(values)

    def kernel(*refs):
        pass

    return pl.pallas_call(
        kernel,
        out_shape=tuple(jax.ShapeDtypeStruct(v.shape, v.dtype) for v in values),
        in_specs=[anywhere] * (count + len(tokens)),
        out_specs=tuple([anywhere] * count),
        input_output_aliases={i: i for i in range(count)},
        compiler_params=pltpu.CompilerParams(vmem_limit_bytes=1024 * 1024),
        cost_estimate=pl.CostEstimate(flops=0, bytes_accessed=1024, transcendentals=0),
    )(*values, *tokens)


def shifted(value, axis, steps):
    count = lax.axis_size(axis)
    pairs = [(source, (source + steps) % count) for source in range(count)]
    return lax.ppermute(value, axis, pairs)


def exchanged(value, axis, offset):
    count = lax.axis_size(axis)
    return lax.ppermute(value, axis, [(source, source ^ offset) for source in range(count)])


def on_device(features, weights, cotangent, edge_bias, neighbours, valid_mask):
    chan_local, comps, atoms_dev = features.shape
    heads, slots = edge_bias.shape[0], edge_bias.shape[1]
    channels = weights.shape[2]
    assert atoms_dev == 2 * HALO and channels == 2 * chan_local
    score_scale = 1.0 / math.sqrt(chan_local // heads * comps)
    total_atoms = atoms_dev * lax.axis_size("atom")
    count = lax.axis_size("atom")
    assert count >= 4 and count & (count - 1) == 0
    atom_place = lax.axis_index("atom")
    cut_bits = (1, 2) if count >= 8 else (0, 1)
    spot = (atom_place >> cut_bits[0]) & 3
    place = jnp.stack([lax.axis_index("chan"), atom_place * atoms_dev, spot])
    place = place.astype(jnp.int32)
    feature_cut = comps // 2
    cotangent_cut = comps - feature_cut + 2
    cuts = ((0, cotangent_cut), (cotangent_cut, comps))

    def held(*dims, dtype=F32):
        return pltpu.VMEM(dims, dtype)

    def plain(*dims, dtype=F32):
        return jax.ShapeDtypeStruct(dims, dtype)

    fm = jnp.transpose(features, (1, 0, 2))
    cot = jnp.transpose(cotangent, (1, 0, 2))
    mix = jnp.transpose(weights, (0, 1, 3, 2))
    anywhere = pl.BlockSpec(memory_space=pl.ANY)
    sizes = (feature_cut, feature_cut, comps - feature_cut, comps - feature_cut)
    high_a, low_a, high_b, low_b = pl.pallas_call(
        functools.partial(split_kernel, feature_cut),
        out_shape=tuple(held(size, chan_local, HALO, dtype=BF16) for size in sizes),
        in_specs=[anywhere],
        out_specs=(pl.BlockSpec(memory_space=pltpu.VMEM),) * 4,
        scratch_shapes=[pltpu.SemaphoreType.DMA((4,))],
        compiler_params=pltpu.CompilerParams(vmem_limit_bytes=4 * 1024 * 1024),
    )(pltpu.with_memory_space_constraint(fm, pltpu.HBM))
    flm_a = shifted(high_a, "atom", 1)
    frm_a = shifted(low_a, "atom", -1)
    flm_b = shifted(high_b, "atom", 1)
    frm_b = shifted(low_b, "atom", -1)
    fo = shifted(fm, "chan", 1)

    qkv, scores, slot_own, index_rows, index_wide, wp, wc, token, *rims = call(
        functools.partial(own_kernel, heads, total_atoms, cuts),
        (place, fm, fo, cot, mix, neighbours),
        (
            held(comps, 3 * chan_local, atoms_dev, dtype=BF16),
            held(2 * heads, atoms_dev, atoms_dev),
            held(2, 3, HALO, HALO, dtype=jnp.int32),
            held(slots, atoms_dev, dtype=jnp.int32),
            held(atoms_dev, HALO, dtype=jnp.int32),
            held(LMAX + 1, 3 * chan_local, channels, dtype=BF16),
            held(LMAX + 1, channels, 3 * chan_local, dtype=BF16),
            plain(8, HALO),
            *(
                plain(stop - start, chan_local, HALO, dtype=BF16)
                for start, stop in cuts
                for _ in range(2)
            ),
        ),
        scalars=1,
        stay=(1, 2, 3),
        flops=12 * 10**9,
    )
    flm_a, frm_a = after((flm_a, frm_a), (token,))
    flo_a = shifted(flm_a, "chan", 1)
    fro_a = shifted(frm_a, "chan", 1)
    halo_a, partial, token = call(
        functools.partial(early_kernel, heads),
        (flm_a, flo_a, frm_a, fro_a, wp, qkv, cot),
        (
            held(feature_cut, 3 * chan_local, atoms_dev, dtype=BF16),
            held(2 * heads, 2, HALO, HALO),
            plain(8, HALO),
        ),
        stay=tuple(range(7)),
    )
    rims[:2] = after(rims[:2], (token,))
    flm_b, frm_b = after((flm_b, frm_b), (token,))
    halos = [(shifted(rims[0], "atom", 1), shifted(rims[1], "atom", -1))]
    flo_b = shifted(flm_b, "chan", 1)
    fro_b = shifted(frm_b, "chan", 1)
    halo_b, grad_bias, message_a, message_b = call(
        functools.partial(edge_kernel, heads, score_scale, feature_cut),
        (flm_b, flo_b, frm_b, fro_b, wp, qkv, cot, scores, partial, edge_bias, valid_mask,
         index_rows, index_wide),
        (
            held(comps - feature_cut, 3 * chan_local, atoms_dev, dtype=BF16),
            plain(heads, slots, atoms_dev),
            held((2 * heads + 1) * slots, HALO, dtype=BF16),
            held((2 * heads + 1) * slots, HALO, dtype=BF16),
        ),
        stay=(0, 1, 2, 3, 4, 5, 6, 7, 8, 11, 12),
    )
    message_left = shifted(message_b, "atom", 1)
    message_right = shifted(message_a, "atom", -1)
    piece = (3 * (LMAX + 1), chan_local // 4, channels)
    grad_query, own_key, own_value, kept, *sent = call(
        functools.partial(grads_kernel, heads, slots),
        (place, fm, fo, flm_a, flo_a, frm_a, fro_a, flm_b, flo_b, frm_b, fro_b, qkv, halo_a, halo_b,
         cot, slot_own, message_a, message_b),
        (
            held(comps, chan_local, atoms_dev, dtype=BF16),
            held(comps, chan_local, atoms_dev),
            held(comps, chan_local, atoms_dev),
            held(*piece),
            plain(*piece, dtype=BF16),
            plain(*piece, dtype=BF16),
            plain(*piece, dtype=BF16),
        ),
        scratch=[
            pltpu.VMEM((comps, 2 * chan_local, 2 * atoms_dev), BF16),
            pltpu.VMEM((3 * (LMAX + 1), chan_local, channels), F32),
        ],
        scalars=1,
        stay=tuple(range(1, 18)),
    )
    (token,) = after((token,), halos[0])
    rims[2:] = after(rims[2:], (sent[0], shifted(token, "chan", 1)))
    halos.append((shifted(rims[2], "atom", 1), shifted(rims[3], "atom", -1)))
    for delta, part in enumerate(sent, 1):
        kept = kept + exchanged(part, "atom", delta << cut_bits[0]).astype(F32)
    rest = [bit for bit in range(count.bit_length() - 1) if bit not in cut_bits]
    while rest:
        offsets = [1 << bit for bit in rest[:2]]
        rest = rest[2:]
        rounded = kept.astype(BF16)
        offsets += [sum(offsets)] * (len(offsets) - 1)
        arrived = [exchanged(rounded, "atom", offset) for offset in offsets]
        kept = functools.reduce(lambda total, part: total + part.astype(F32), arrived, kept)
    rounded = kept.astype(BF16)
    pieces = [rounded] + [exchanged(rounded, "atom", d << cut_bits[0]) for d in range(1, 4)]
    grad_weights, gathered = call(
        gather_kernel,
        (place, *pieces),
        (plain(3 * (LMAX + 1), chan_local, channels), plain(8, HALO)),
        scalars=1,
        limit=8,
        flops=20 * 10**9,
    )
    (terms,) = call(
        functools.partial(key_kernel, heads, slots),
        (grad_query, own_key, halo_a, halo_b, message_left, message_right, wc),
        (held(comps, channels, atoms_dev),),
        scratch=[pltpu.VMEM((comps, 2 * chan_local, atoms_dev), BF16)],
        limit=16,
        stay=(0, 1, 2, 3, 6),
    )
    parts, counts = [], []
    tokens = ()
    for (start, stop), (cl, cr) in zip(cuts, halos):
        size = stop - start
        part = -(-size // -(-size // (comps // 6)))
        sizes = [min(part, size - at) for at in range(0, size, part)]
        mine, token, *theirs = call(
            functools.partial(value_kernel, heads, slots, start),
            (own_value, cl, cr, message_left, message_right, wc, terms),
            (
                held(size, chan_local, atoms_dev),
                plain(8, HALO),
                *(held(some, chan_local, atoms_dev, dtype=BF16) for some in sizes),
            ),
            scratch=[pltpu.VMEM((size, chan_local, atoms_dev), BF16)],
            limit=16,
            stay=(0, 5, 6),
            tokens=tokens,
        )
        tokens = (token, rounded)
        counts.append(len(sizes))
        parts += [mine, *(shifted(some, "chan", 1) for some in theirs)]
    (out,) = call(
        functools.partial(finish_kernel, counts),
        parts,
        (plain(comps, chan_local, atoms_dev, dtype=BF16),),
        limit=8,
        stay=tuple(range(len(parts))),
        tokens=(gathered,),
    )
    grad_features = jnp.transpose(out, (1, 0, 2))
    grad_weights = grad_weights.reshape(3, LMAX + 1, chan_local, channels)
    grad_weights = jnp.transpose(grad_weights, (0, 1, 3, 2))
    return grad_features, grad_weights, grad_bias


def solution(mesh):
    in_specs = (
        P("chan", None, "atom"),
        P(None, None, None, "chan"),
        P("chan", None, "atom"),
        P("chan", None, "atom"),
        P(None, "atom"),
        P(None, "atom"),
    )
    out_specs = (P("chan", None, "atom"), P(None, None, None, "chan"), P("chan", None, "atom"))
    return jax.shard_map(
        on_device, mesh=mesh, in_specs=in_specs, out_specs=out_specs, check_vma=False
    )
```

```python
import functools
import math
import operator

import jax
import jax.numpy as jnp
from jax import lax
from jax.experimental import pallas as pl
from jax.experimental.pallas import tpu as pltpu
from jax.sharding import PartitionSpec as P

LMAX = 6
HALO = 128
SOFT_CAP = 10.0
F32 = jnp.float32
BF16 = jnp.bfloat16


def degree_of(comp):
    return math.isqrt(comp)


def nn(lhs, rhs):
    return lax.dot_general(lhs, rhs, (((1,), (0,)), ((), ())), preferred_element_type=F32)


def nt(lhs, rhs):
    return lax.dot_general(lhs, rhs, (((1,), (1,)), ((), ())), preferred_element_type=F32)


def tn(lhs, rhs):
    return lax.dot_general(lhs, rhs, (((0,), (0,)), ((), ())), preferred_element_type=F32)


def pick(table, index):
    return jnp.take_along_axis(table, index, axis=1, mode="promise_in_bounds")


def head_rows_of(ref, first_row, rows):
    block = ref[:, first_row : first_row + rows, :]
    return block.reshape(block.shape[0] * rows, block.shape[2])


def slot_tile(window_index, tile):
    atoms, slots = window_index.shape
    lane = lax.broadcasted_iota(jnp.int32, (atoms, HALO), 1) + tile * HALO
    found = jnp.full((atoms, HALO), -1, jnp.int32)
    for slot in range(slots):
        found = jnp.where(window_index[:, slot : slot + 1] == lane, slot, found)
    return found


def spread(slot, coef, quantity, slots):
    values = pick(coef, jnp.maximum(slot, 0) + quantity * slots)
    return jnp.where(slot >= 0, values, 0.0).astype(BF16)


def wide_transpose(rows):
    return jnp.concatenate([rows] * (HALO // rows.shape[0]), axis=0).T


def split_kernel(cuts, fm, *refs):
    *parts, sems = refs
    copies = []
    for at, part in enumerate(parts):
        start, stop = cuts[at // 2]
        atom = HALO if at % 2 == 0 else 0
        copies.append(
            pltpu.make_async_copy(
                fm.at[pl.ds(start, stop - start), :, pl.ds(atom, HALO)], part, sems.at[at]
            )
        )
    for copy in copies:
        copy.start()
    for copy in copies:
        copy.wait()


def own_kernel(heads, total_atoms, place, fm, fo, cot, weights, neighbours,
               qkv, scores, slot_own, index_rows, index_wide, wp, wc, token, *rims):
    token[...] = jnp.zeros_like(token)
    rims[0][...] = cot[:, :, HALO:]
    rims[1][...] = cot[:, :, :HALO]
    comps, chan_local = fm.shape[0], fm.shape[1]
    channels = weights.shape[3]
    rows = chan_local // heads
    slots = neighbours.shape[0]
    core, first_atom = place[0], place[1]
    for degree in range(LMAX + 1):
        mix = jnp.concatenate([weights[g, degree] for g in range(3)], axis=0).astype(F32)
        mix = jnp.where(core == 0, mix, pltpu.roll(mix, chan_local, 1))
        wp[degree] = mix.astype(BF16)
        padded = jnp.concatenate([mix, jnp.zeros((chan_local, channels), F32)], axis=0)
        wc[degree] = padded.T[:, : 3 * chan_local].astype(BF16)
    for comp in range(comps):
        feats = jnp.concatenate([fm[comp], fo[comp]], axis=0)
        qkv[comp] = nn(wp[degree_of(comp)], feats).astype(BF16)
    for head in range(heads):
        query = head_rows_of(qkv, head * rows, rows)
        key = head_rows_of(qkv, chan_local + head * rows, rows)
        value = head_rows_of(qkv, 2 * chan_local + head * rows, rows)
        scores[head] = tn(query, key)
        scores[heads + head] = tn(head_rows_of(cot, head * rows, rows), value)
    for half in range(2):
        span = slice(half * HALO, (half + 1) * HALO)
        index = neighbours[:, span] - (first_atom + (half - 1) * HALO)
        index = jnp.where(index < 0, index + total_atoms, index)
        index = jnp.where(index >= total_atoms, index - total_atoms, index)
        index_rows[:, span] = index
        wide = wide_transpose(index)
        index_wide[span, :] = wide
        for tile in range(3):
            slot_own[half, tile] = slot_tile(wide[:, :slots], tile)


def project_halo(start, chunks, wp, halo_qkv):
    at = 0
    for flm, flo, frm, fro in chunks:
        for comp in range(flm.shape[0]):
            feats = jnp.concatenate(
                [
                    jnp.concatenate([flm[comp], frm[comp]], axis=1),
                    jnp.concatenate([flo[comp], fro[comp]], axis=1),
                ],
                axis=0,
            )
            halo_qkv[at] = nn(wp[degree_of(start + at)], feats).astype(BF16)
            at += 1


def halo_scores(heads, quantity, start, qkv, cot, halo_qkv):
    size, chan_local = halo_qkv.shape[0], cot.shape[1]
    rows = chan_local // heads
    head = quantity % heads
    first = (1 if quantity < heads else 2) * chan_local + head * rows
    source = qkv if quantity < heads else cot
    mine = source[start : start + size, head * rows : (head + 1) * rows, :]
    mine = mine.reshape(size * rows, mine.shape[2])
    theirs = head_rows_of(halo_qkv, first, rows)
    return tn(mine[:, :HALO], theirs[:, :HALO]), tn(mine[:, HALO:], theirs[:, HALO:])


def early_kernel(heads, flm, flo, frm, fro, wp, qkv, cot, halo_qkv, partial, token):
    token[...] = jnp.zeros_like(token)
    project_halo(0, [(flm, flo, frm, fro)], wp, halo_qkv)
    for quantity in range(2 * heads):
        left, right = halo_scores(heads, quantity, 0, qkv, cot, halo_qkv)
        partial[quantity, 0] = left
        partial[quantity, 1] = right


def edge_kernel(heads, score_scale, start, late, *refs):
    chunks = [refs[at : at + 4] for at in range(0, 4 * late, 4)]
    (wp, qkv, cot, scores, partial, bias, valid, index_rows, index_wide,
     halo_qkv, grad_bias, message_a, message_b) = refs[4 * late :]
    slots = valid.shape[0]
    project_halo(start, chunks, wp, halo_qkv)
    lane = lax.broadcasted_iota(jnp.int32, (HALO, 2 * heads * slots), 1)
    gathered = [jnp.zeros((HALO, 2 * heads * slots), F32) for _ in range(2)]
    for quantity in range(2 * heads):
        left, right = halo_scores(heads, quantity, start, qkv, cot, halo_qkv)
        left, right = left + partial[quantity, 0], right + partial[quantity, 1]
        for half in range(2):
            own = scores[quantity, half * HALO : (half + 1) * HALO, :]
            own = [own[:, :HALO], own[:, HALO:]]
            tiles = [left] + own if half == 0 else own + [right]
            index = index_wide[half * HALO : (half + 1) * HALO, :]
            inner, tile_of = index & (HALO - 1), index >> 7
            values = jnp.where(
                tile_of == 0,
                pick(tiles[0], inner),
                jnp.where(tile_of == 1, pick(tiles[1], inner), pick(tiles[2], inner)),
            )
            gathered[half] = jnp.where(lane // slots == quantity, values, gathered[half])
    for half, message in enumerate((message_a, message_b)):
        span = slice(half * HALO, (half + 1) * HALO)
        edges = gathered[half].T.reshape(2, heads, slots, HALO)
        squashed = jnp.tanh(edges[0] * (score_scale / SOFT_CAP))
        logits = SOFT_CAP * squashed + bias[:, :, span]
        live = valid[:, span][None] > 0
        weight = jnp.where(live, jnp.exp(logits), 0.0)
        attention = weight / jnp.sum(weight, axis=1, keepdims=True)
        grad_attn = edges[1]
        grad_logit = attention * (
            grad_attn - jnp.sum(attention * grad_attn, axis=1, keepdims=True)
        )
        grad_bias[:, :, span] = grad_logit
        grad_raw = score_scale * grad_logit * (1.0 - squashed * squashed)
        index = index_rows[:, span]
        both = jnp.stack([grad_raw, attention]).reshape(2 * heads, slots, HALO)
        merged = jnp.zeros_like(both)
        for slot in range(slots):
            same = (index == index[slot : slot + 1, :])[None]
            merged = merged + jnp.where(same, both[:, slot : slot + 1, :], 0.0)
        atom = lax.broadcasted_iota(jnp.int32, (slots, HALO), 1)
        message[: 2 * heads * slots, :] = merged.reshape(2 * heads * slots, HALO).astype(BF16)
        message[2 * heads * slots :, :] = (index - HALO - atom).astype(F32).astype(BF16)


def joined_rows(early, late, first_row, rows):
    return jnp.concatenate(
        [head_rows_of(early, first_row, rows), head_rows_of(late, first_row, rows)], axis=0
    )


def grads_kernel(heads, slots, pieces, place, fm, fo, *refs):
    chunks = [refs[at : at + 4] for at in range(0, 4 * pieces, 4)]
    (qkv, halo_a, halo_b, cot, slot_own, message_a, message_b, grad_query, own_key, own_value, kept,
     sent_1, sent_2, sent_3, ext, weight_terms) = refs[4 * pieces :]
    places = [(chunk, at) for chunk in chunks for at in range(chunk[0].shape[0])]
    comps, chan_local = fm.shape[0], fm.shape[1]
    rows = chan_local // heads
    atoms = 2 * HALO
    core = place[0]
    empty = jnp.zeros((HALO, HALO), BF16)
    coefs = [message[: 2 * heads * slots, :].astype(F32).T for message in (message_a, message_b)]
    for head in range(heads):
        tables = []
        for quantity in (head, heads + head):
            halves = []
            for half in range(2):
                tiles = [spread(slot_own[half, t], coefs[half], quantity, slots) for t in range(3)]
                tiles = tiles + [empty] if half == 0 else [empty] + tiles
                halves.append(jnp.concatenate(tiles, axis=1))
            tables.append(jnp.concatenate(halves, axis=0))
        raw_table, attn_table = tables
        query = head_rows_of(qkv, head * rows, rows)
        key = head_rows_of(qkv, chan_local + head * rows, rows)
        halo_key = joined_rows(halo_a, halo_b, chan_local + head * rows, rows)
        key_ext = jnp.concatenate([halo_key[:, :HALO], key, halo_key[:, HALO:]], axis=1)
        span = slice(head * rows, (head + 1) * rows)
        value_span = slice(chan_local + head * rows, chan_local + (head + 1) * rows)
        grad_query[:, span, :] = nt(key_ext, raw_table).astype(BF16).reshape(comps, rows, atoms)
        key_sums = nn(query, raw_table)
        own_key[:, span, :] = key_sums[:, HALO : HALO + atoms].reshape(comps, rows, atoms)
        ext[:, span, :] = key_sums.astype(BF16).reshape(comps, rows, atoms + 2 * HALO)
        value_sums = nn(head_rows_of(cot, head * rows, rows), attn_table)
        own_value[:, span, :] = value_sums[:, HALO : HALO + atoms].reshape(comps, rows, atoms)
        ext[:, value_span, :] = value_sums.astype(BF16).reshape(comps, rows, atoms + 2 * HALO)
    for degree in range(LMAX + 1):
        query_total = jnp.zeros((chan_local, 2 * chan_local), F32)
        keyval_total = jnp.zeros((2 * chan_local, 2 * chan_local), F32)
        for comp in range(degree * degree, (degree + 1) * (degree + 1)):
            own = jnp.concatenate([fm[comp], fo[comp]], axis=0)
            (flm, flo, frm, fro), at = places[comp]
            wide = jnp.concatenate(
                [
                    jnp.concatenate([flm[at], fm[comp], frm[at]], axis=1),
                    jnp.concatenate([flo[at], fo[comp], fro[at]], axis=1),
                ],
                axis=0,
            )
            query_total = query_total + nt(grad_query[comp], own)
            keyval_total = keyval_total + nt(ext[comp], wide)
        total = jnp.concatenate([query_total, keyval_total], axis=0)
        total = jnp.where(core == 0, total, pltpu.roll(total, chan_local, 1))
        for g in range(3):
            weight_terms[g * (LMAX + 1) + degree] = total[g * chan_local : (g + 1) * chan_local]
    piece = chan_local // 4
    spot = place[2]
    for delta, part in enumerate((kept, sent_1, sent_2, sent_3)):
        first = pl.multiple_of((spot ^ delta) * piece, piece)
        part[...] = weight_terms[:, pl.ds(first, piece), :].astype(part.dtype)


def halo_slots(message_left, message_right, quantities, slots):
    coefs, tables = [], []
    for message, tile in ((message_left, 2), (message_right, 0)):
        coefs.append(message[: quantities * slots, :].astype(F32).T)
        offset = message[quantities * slots :, :].astype(F32).astype(jnp.int32)
        atom = lax.broadcasted_iota(jnp.int32, offset.shape, 1)
        tables.append(slot_tile(wide_transpose(offset + HALO + atom)[:, :slots], tile))
    return coefs, tables


def key_kernel(heads, slots, grad_query, own_key, halo_a, halo_b, message_left, message_right, wc,
               terms, token, grad):
    token[...] = jnp.zeros_like(token)
    comps, chan_local = grad_query.shape[0], grad_query.shape[1]
    rows = chan_local // heads
    grad[:, :chan_local, :] = grad_query[...]
    coefs, tables = halo_slots(message_left, message_right, 2 * heads, slots)
    for head in range(heads):
        query = joined_rows(halo_a, halo_b, head * rows, rows)
        rim = jnp.concatenate(
            [
                nn(query[:, :HALO], spread(tables[0], coefs[0], head, slots)),
                nn(query[:, HALO:], spread(tables[1], coefs[1], head, slots)),
            ],
            axis=1,
        )
        total = head_rows_of(own_key, head * rows, rows) + rim
        span = slice(chan_local + head * rows, chan_local + (head + 1) * rows)
        grad[:, span, :] = total.astype(BF16).reshape(comps, rows, 2 * HALO)
    for comp in range(comps):
        terms[comp] = nn(wc[degree_of(comp)][:, : 2 * chan_local], grad[comp])


def value_kernel(heads, slots, start, stop, own_value, cl, cr, message_left, message_right, wc, terms,
                 mine, token, *theirs):
    *theirs, grad = theirs
    token[...] = jnp.zeros_like(token)
    comps, chan_local = stop - start, cl.shape[1]
    rows = chan_local // heads
    coefs, tables = halo_slots(message_left, message_right, 2 * heads, slots)
    for head in range(heads):
        span = slice(head * rows, (head + 1) * rows)
        rim = jnp.concatenate(
            [
                nn(cl[start:stop, span, :].reshape(comps * rows, HALO),
                   spread(tables[0], coefs[0], heads + head, slots)),
                nn(cr[start:stop, span, :].reshape(comps * rows, HALO),
                   spread(tables[1], coefs[1], heads + head, slots)),
            ],
            axis=1,
        )
        own = own_value[start:stop, span, :].reshape(comps * rows, 2 * HALO)
        grad[:, span, :] = (own + rim).astype(BF16).reshape(comps, rows, 2 * HALO)
    for comp in range(comps):
        mix = wc[degree_of(start + comp)][:, 2 * chan_local :]
        total = terms[start + comp] + nn(mix, grad[comp])
        mine[comp] = total[:chan_local]
        part = theirs[0].shape[0]
        theirs[comp // part][comp % part] = total[chan_local:].astype(BF16)


def finish_kernel(parts, *refs):
    *refs, out = refs
    start = 0
    for count in parts:
        mine, theirs, refs = refs[0], refs[1 : count + 1], refs[count + 1 :]
        at = 0
        for part in theirs:
            size = part.shape[0]
            total = mine[at : at + size] + part[...].astype(F32)
            out[start + at : start + at + size] = total.astype(BF16)
            at += size
        start += at


def gather_kernel(place, part_0, part_1, part_2, part_3, out, token):
    token[...] = jnp.zeros_like(token)
    piece = part_0.shape[1]
    spot = place[2]
    for delta, part in enumerate((part_0, part_1, part_2, part_3)):
        first = pl.multiple_of((spot ^ delta) * piece, piece)
        out[:, pl.ds(first, piece), :] = part[...].astype(F32)


def call(kernel, args, outs, scratch=(), scalars=0, limit=24, stay=(), tokens=(), flops=0):
    whole = pl.BlockSpec(memory_space=pltpu.VMEM)
    small = pl.BlockSpec(memory_space=pltpu.SMEM)
    args = [
        pltpu.with_memory_space_constraint(a, pltpu.VMEM) if at in stay else a
        for at, a in enumerate(args)
    ]
    count = len(args)

    def body(*refs):
        kernel(*refs[:count], *refs[count + len(tokens) :])

    return pl.pallas_call(
        body,
        out_shape=tuple(outs),
        in_specs=[small] * scalars
        + [whole] * (count - scalars)
        + [pl.BlockSpec(memory_space=pl.ANY)] * len(tokens),
        out_specs=tuple([whole] * len(outs)),
        scratch_shapes=list(scratch),
        compiler_params=pltpu.CompilerParams(vmem_limit_bytes=limit * 1024 * 1024),
        cost_estimate=pl.CostEstimate(flops=flops, bytes_accessed=1024, transcendentals=0),
    )(*args, *tokens)


def after(values, tokens):
    anywhere = pl.BlockSpec(memory_space=pl.ANY)
    count = len(values)

    def kernel(*refs):
        pass

    return pl.pallas_call(
        kernel,
        out_shape=tuple(jax.ShapeDtypeStruct(v.shape, v.dtype) for v in values),
        in_specs=[anywhere] * (count + len(tokens)),
        out_specs=tuple([anywhere] * count),
        input_output_aliases={i: i for i in range(count)},
        compiler_params=pltpu.CompilerParams(vmem_limit_bytes=1024 * 1024),
        cost_estimate=pl.CostEstimate(flops=0, bytes_accessed=1024, transcendentals=0),
    )(*values, *tokens)


def shifted(value, axis, steps):
    count = lax.axis_size(axis)
    pairs = [(source, (source + steps) % count) for source in range(count)]
    return lax.ppermute(value, axis, pairs)


def exchanged(value, axis, offset):
    count = lax.axis_size(axis)
    return lax.ppermute(value, axis, [(source, source ^ offset) for source in range(count)])


def crossed(value, target):
    count = lax.axis_size("atom")
    pairs = [(2 * at + core, 2 * target(at) + 1 - core) for at in range(count) for core in range(2)]
    return shifted(lax.ppermute(value, ("atom", "chan"), pairs), "chan", 1)


def on_device(features, weights, cotangent, edge_bias, neighbours, valid_mask):
    chan_local, comps, atoms_dev = features.shape
    heads, slots = edge_bias.shape[0], edge_bias.shape[1]
    channels = weights.shape[2]
    assert atoms_dev == 2 * HALO and channels == 2 * chan_local
    score_scale = 1.0 / math.sqrt(chan_local // heads * comps)
    total_atoms = atoms_dev * lax.axis_size("atom")
    count = lax.axis_size("atom")
    assert count >= 4 and count & (count - 1) == 0
    atom_place = lax.axis_index("atom")
    cut_bits = (1, 2) if count >= 8 else (0, 1)
    spot = (atom_place >> cut_bits[0]) & 3
    place = jnp.stack([lax.axis_index("chan"), atom_place * atoms_dev, spot])
    place = place.astype(jnp.int32)
    feature_cut = comps // 2
    value_cut = comps // 2
    feature_cuts = ((0, feature_cut), (feature_cut, comps))
    cuts = ((0, value_cut), (value_cut, comps))

    def held(*dims, dtype=F32):
        return pltpu.VMEM(dims, dtype)

    def plain(*dims, dtype=F32):
        return jax.ShapeDtypeStruct(dims, dtype)

    fm = jnp.transpose(features, (1, 0, 2))
    cot = jnp.transpose(cotangent, (1, 0, 2))
    mix = jnp.transpose(weights, (0, 1, 3, 2))
    anywhere = pl.BlockSpec(memory_space=pl.ANY)
    rim_count = 2 * len(feature_cuts)
    feature_rims = pl.pallas_call(
        functools.partial(split_kernel, feature_cuts),
        out_shape=tuple(
            held(stop - start, chan_local, HALO, dtype=BF16)
            for start, stop in feature_cuts
            for _ in range(2)
        ),
        in_specs=[anywhere],
        out_specs=(pl.BlockSpec(memory_space=pltpu.VMEM),) * rim_count,
        scratch_shapes=[pltpu.SemaphoreType.DMA((rim_count,))],
        compiler_params=pltpu.CompilerParams(vmem_limit_bytes=4 * 1024 * 1024),
    )(pltpu.with_memory_space_constraint(fm, pltpu.HBM))
    from_sides = [
        shifted(rim, "atom", 1 if at % 2 == 0 else -1) for at, rim in enumerate(feature_rims)
    ]
    fo = shifted(fm, "chan", 1)

    qkv, scores, slot_own, index_rows, index_wide, wp, wc, token, *rims = call(
        functools.partial(own_kernel, heads, total_atoms),
        (place, fm, fo, cot, mix, neighbours),
        (
            held(comps, 3 * chan_local, atoms_dev, dtype=BF16),
            held(2 * heads, atoms_dev, atoms_dev),
            held(2, 3, HALO, HALO, dtype=jnp.int32),
            held(slots, atoms_dev, dtype=jnp.int32),
            held(atoms_dev, HALO, dtype=jnp.int32),
            held(LMAX + 1, 3 * chan_local, channels, dtype=BF16),
            held(LMAX + 1, channels, 3 * chan_local, dtype=BF16),
            plain(8, HALO),
            *(
                plain(comps, chan_local, HALO, dtype=BF16) for _ in range(2)
            ),
        ),
        scalars=1,
        stay=(1, 2, 3),
        flops=12 * 10**9,
    )
    flm, frm = after(from_sides[:2], (token,))
    early_chunk = (flm, shifted(flm, "chan", 1), frm, shifted(frm, "chan", 1))
    halo_a, partial, token = call(
        functools.partial(early_kernel, heads),
        (*early_chunk, wp, qkv, cot),
        (
            held(feature_cut, 3 * chan_local, atoms_dev, dtype=BF16),
            held(2 * heads, 2, HALO, HALO),
            plain(8, HALO),
        ),
        stay=tuple(range(7)),
    )
    rims = after(rims, (token,))
    late_sides = after(from_sides[2:], (token,))
    late_chunks = []
    for flm, frm in zip(late_sides[::2], late_sides[1::2]):
        late_chunks += [flm, shifted(flm, "chan", 1), frm, shifted(frm, "chan", 1)]
    from_left, from_right = shifted(rims[0], "atom", 1), shifted(rims[1], "atom", -1)
    halo_b, grad_bias, message_a, message_b = call(
        functools.partial(edge_kernel, heads, score_scale, feature_cut, len(late_chunks) // 4),
        (*late_chunks, wp, qkv, cot, scores, partial, edge_bias, valid_mask, index_rows, index_wide),
        (
            held(comps - feature_cut, 3 * chan_local, atoms_dev, dtype=BF16),
            plain(heads, slots, atoms_dev),
            held((2 * heads + 1) * slots, HALO, dtype=BF16),
            held((2 * heads + 1) * slots, HALO, dtype=BF16),
        ),
        stay=(*range(len(late_chunks) + 5), len(late_chunks) + 7, len(late_chunks) + 8),
    )
    message_left = crossed(message_b, lambda at: (at + 1) % count)
    message_right = crossed(message_a, lambda at: (at - 1) % count)
    piece = (3 * (LMAX + 1), chan_local // 4, channels)
    grad_query, own_key, own_value, kept, *sent = call(
        functools.partial(grads_kernel, heads, slots, len(feature_cuts)),
        (place, fm, fo, *early_chunk, *late_chunks, qkv, halo_a, halo_b, cot, slot_own, message_a,
         message_b),
        (
            held(comps, chan_local, atoms_dev, dtype=BF16),
            held(comps, chan_local, atoms_dev),
            held(comps, chan_local, atoms_dev),
            held(*piece),
            plain(*piece, dtype=BF16),
            plain(*piece, dtype=BF16),
            plain(*piece, dtype=BF16),
        ),
        scratch=[
            pltpu.VMEM((comps, 2 * chan_local, 2 * atoms_dev), BF16),
            pltpu.VMEM((3 * (LMAX + 1), chan_local, channels), F32),
        ],
        scalars=1,
        stay=tuple(range(1, 10 + 4 * len(feature_cuts))),
    )
    for delta, part in enumerate(sent, 1):
        kept = kept + exchanged(part, "atom", delta << cut_bits[0]).astype(F32)
    rest = [bit for bit in range(count.bit_length() - 1) if bit not in cut_bits]
    while rest:
        offsets = [1 << bit for bit in rest[:2]]
        rest = rest[2:]
        rounded = kept.astype(BF16)
        offsets += [sum(offsets)] * (len(offsets) - 1)
        arrived = [
            crossed(rounded, functools.partial(operator.xor, offset))
            if offset == 1
            else exchanged(rounded, "atom", offset)
            for offset in offsets
        ]
        kept = functools.reduce(lambda total, part: total + part.astype(F32), arrived, kept)
    terms, token = call(
        functools.partial(key_kernel, heads, slots),
        (grad_query, own_key, halo_a, halo_b, message_left, message_right, wc),
        (held(comps, channels, atoms_dev), plain(8, HALO)),
        scratch=[pltpu.VMEM((comps, 2 * chan_local, atoms_dev), BF16)],
        limit=16,
        stay=(0, 1, 2, 3, 6),
    )
    from_left, from_right, rounded = after((from_left, from_right, kept.astype(BF16)), (token,))
    pieces = [rounded] + [exchanged(rounded, "atom", d << cut_bits[0]) for d in range(1, 4)]
    grad_weights, gathered = call(
        gather_kernel,
        (place, *pieces),
        (plain(3 * (LMAX + 1), chan_local, channels), plain(8, HALO)),
        scalars=1,
        limit=8,
        flops=20 * 10**9,
    )
    parts, counts = [], []
    tokens = ()
    for start, stop in cuts:
        size = stop - start
        sizes = [size]
        mine, token, *theirs = call(
            functools.partial(value_kernel, heads, slots, start, stop),
            (own_value, from_left, from_right, message_left, message_right, wc, terms),
            (
                held(size, chan_local, atoms_dev),
                plain(8, HALO),
                *(held(some, chan_local, atoms_dev, dtype=BF16) for some in sizes),
            ),
            scratch=[pltpu.VMEM((size, chan_local, atoms_dev), BF16)],
            limit=16,
            stay=(0, 1, 2, 5, 6),
            tokens=tokens,
        )
        tokens = (token, pieces[2])
        counts.append(len(sizes))
        parts += [mine, *(shifted(some, "chan", 1) for some in theirs)]
    (out,) = call(
        functools.partial(finish_kernel, counts),
        parts,
        (plain(comps, chan_local, atoms_dev, dtype=BF16),),
        limit=8,
        stay=tuple(range(len(parts))),
        tokens=(gathered,),
    )
    grad_features = jnp.transpose(out, (1, 0, 2))
    grad_weights = grad_weights.reshape(3, LMAX + 1, chan_local, channels)
    grad_weights = jnp.transpose(grad_weights, (0, 1, 3, 2))
    return grad_features, grad_weights, grad_bias


def solution(mesh):
    in_specs = (
        P("chan", None, "atom"),
        P(None, None, None, "chan"),
        P("chan", None, "atom"),
        P("chan", None, "atom"),
        P(None, "atom"),
        P(None, "atom"),
    )
    out_specs = (P("chan", None, "atom"), P(None, None, None, "chan"), P("chan", None, "atom"))
    return jax.shard_map(
        on_device, mesh=mesh, in_specs=in_specs, out_specs=out_specs, check_vma=False
    )
```

```python
import functools
import math

import jax
import jax.numpy as jnp
from jax import lax
from jax.experimental import pallas as pl
from jax.experimental.pallas import tpu as pltpu
from jax.sharding import PartitionSpec as P

LMAX = 6
HALO = 128
SOFT_CAP = 10.0
F32 = jnp.float32
BF16 = jnp.bfloat16


def degree_of(comp):
    return math.isqrt(comp)


def nn(lhs, rhs):
    return lax.dot_general(lhs, rhs, (((1,), (0,)), ((), ())), preferred_element_type=F32)


def nt(lhs, rhs):
    return lax.dot_general(lhs, rhs, (((1,), (1,)), ((), ())), preferred_element_type=F32)


def tn(lhs, rhs):
    return lax.dot_general(lhs, rhs, (((0,), (0,)), ((), ())), preferred_element_type=F32)


def pick(table, index):
    return jnp.take_along_axis(table, index, axis=1, mode="promise_in_bounds")


def head_rows_of(ref, first_row, rows):
    block = ref[:, first_row : first_row + rows, :]
    return block.reshape(block.shape[0] * rows, block.shape[2])


def slot_tile(window_index, tile):
    atoms, slots = window_index.shape
    lane = lax.broadcasted_iota(jnp.int32, (atoms, HALO), 1) + tile * HALO
    found = jnp.full((atoms, HALO), -1, jnp.int32)
    for slot in range(slots):
        found = jnp.where(window_index[:, slot : slot + 1] == lane, slot, found)
    return found


def spread(slot, coef, quantity, slots):
    values = pick(coef, jnp.maximum(slot, 0) + quantity * slots)
    return jnp.where(slot >= 0, values, 0.0).astype(BF16)


def wide_transpose(rows):
    return jnp.concatenate([rows] * (HALO // rows.shape[0]), axis=0).T


def split_kernel(cuts, fm, *refs):
    *parts, sems = refs
    copies = []
    for at, part in enumerate(parts):
        start, stop = cuts[at // 2]
        atom = HALO if at % 2 == 0 else 0
        copies.append(
            pltpu.make_async_copy(
                fm.at[pl.ds(start, stop - start), :, pl.ds(atom, HALO)], part, sems.at[at]
            )
        )
    for copy in copies:
        copy.start()
    for copy in copies:
        copy.wait()


def own_kernel(heads, total_atoms, place, fm, fo, cot, weights, neighbours,
               qkv, scores, slot_own, index_rows, index_wide, wp, wc, token, *rims):
    token[...] = jnp.zeros_like(token)
    rims[0][...] = cot[:, :, HALO:]
    rims[1][...] = cot[:, :, :HALO]
    comps, chan_local = fm.shape[0], fm.shape[1]
    channels = weights.shape[3]
    rows = chan_local // heads
    slots = neighbours.shape[0]
    core, first_atom = place[0], place[1]
    for degree in range(LMAX + 1):
        mix = jnp.concatenate([weights[g, degree] for g in range(3)], axis=0).astype(F32)
        mix = jnp.where(core == 0, mix, pltpu.roll(mix, chan_local, 1))
        wp[degree] = mix.astype(BF16)
        padded = jnp.concatenate([mix, jnp.zeros((chan_local, channels), F32)], axis=0)
        wc[degree] = padded.T[:, : 3 * chan_local].astype(BF16)
    for comp in range(comps):
        feats = jnp.concatenate([fm[comp], fo[comp]], axis=0)
        qkv[comp] = nn(wp[degree_of(comp)], feats).astype(BF16)
    for head in range(heads):
        query = head_rows_of(qkv, head * rows, rows)
        key = head_rows_of(qkv, chan_local + head * rows, rows)
        value = head_rows_of(qkv, 2 * chan_local + head * rows, rows)
        scores[head] = tn(query, key)
        scores[heads + head] = tn(head_rows_of(cot, head * rows, rows), value)
    for half in range(2):
        span = slice(half * HALO, (half + 1) * HALO)
        index = neighbours[:, span] - (first_atom + (half - 1) * HALO)
        index = jnp.where(index < 0, index + total_atoms, index)
        index = jnp.where(index >= total_atoms, index - total_atoms, index)
        index_rows[:, span] = index
        wide = wide_transpose(index)
        index_wide[span, :] = wide
        for tile in range(3):
            slot_own[half, tile] = slot_tile(wide[:, :slots], tile)


def project_halo(start, chunks, wp, halo_qkv):
    at = 0
    for flm, flo, frm, fro in chunks:
        for comp in range(flm.shape[0]):
            feats = jnp.concatenate(
                [
                    jnp.concatenate([flm[comp], frm[comp]], axis=1),
                    jnp.concatenate([flo[comp], fro[comp]], axis=1),
                ],
                axis=0,
            )
            halo_qkv[at] = nn(wp[degree_of(start + at)], feats).astype(BF16)
            at += 1


def halo_scores(heads, quantity, start, qkv, cot, halo_qkv):
    size, chan_local = halo_qkv.shape[0], cot.shape[1]
    rows = chan_local // heads
    head = quantity % heads
    first = (1 if quantity < heads else 2) * chan_local + head * rows
    source = qkv if quantity < heads else cot
    mine = source[start : start + size, head * rows : (head + 1) * rows, :]
    mine = mine.reshape(size * rows, mine.shape[2])
    theirs = head_rows_of(halo_qkv, first, rows)
    return tn(mine[:, :HALO], theirs[:, :HALO]), tn(mine[:, HALO:], theirs[:, HALO:])


def early_kernel(heads, flm, flo, frm, fro, wp, qkv, cot, halo_qkv, partial, token):
    token[...] = jnp.zeros_like(token)
    project_halo(0, [(flm, flo, frm, fro)], wp, halo_qkv)
    for quantity in range(2 * heads):
        left, right = halo_scores(heads, quantity, 0, qkv, cot, halo_qkv)
        partial[quantity, 0] = left
        partial[quantity, 1] = right


def edge_kernel(heads, score_scale, start, late, *refs):
    chunks = [refs[at : at + 4] for at in range(0, 4 * late, 4)]
    (wp, qkv, cot, scores, partial, bias, valid, index_rows, index_wide,
     halo_qkv, grad_bias, message_a, message_b) = refs[4 * late :]
    slots = valid.shape[0]
    project_halo(start, chunks, wp, halo_qkv)
    lane = lax.broadcasted_iota(jnp.int32, (HALO, 2 * heads * slots), 1)
    gathered = [jnp.zeros((HALO, 2 * heads * slots), F32) for _ in range(2)]
    for quantity in range(2 * heads):
        left, right = halo_scores(heads, quantity, start, qkv, cot, halo_qkv)
        left, right = left + partial[quantity, 0], right + partial[quantity, 1]
        for half in range(2):
            own = scores[quantity, half * HALO : (half + 1) * HALO, :]
            own = [own[:, :HALO], own[:, HALO:]]
            tiles = [left] + own if half == 0 else own + [right]
            index = index_wide[half * HALO : (half + 1) * HALO, :]
            inner, tile_of = index & (HALO - 1), index >> 7
            values = jnp.where(
                tile_of == 0,
                pick(tiles[0], inner),
                jnp.where(tile_of == 1, pick(tiles[1], inner), pick(tiles[2], inner)),
            )
            gathered[half] = jnp.where(lane // slots == quantity, values, gathered[half])
    for half, message in enumerate((message_a, message_b)):
        span = slice(half * HALO, (half + 1) * HALO)
        edges = gathered[half].T.reshape(2, heads, slots, HALO)
        squashed = jnp.tanh(edges[0] * (score_scale / SOFT_CAP))
        logits = SOFT_CAP * squashed + bias[:, :, span]
        live = valid[:, span][None] > 0
        weight = jnp.where(live, jnp.exp(logits), 0.0)
        attention = weight / jnp.sum(weight, axis=1, keepdims=True)
        grad_attn = edges[1]
        grad_logit = attention * (
            grad_attn - jnp.sum(attention * grad_attn, axis=1, keepdims=True)
        )
        grad_bias[:, :, span] = grad_logit
        grad_raw = score_scale * grad_logit * (1.0 - squashed * squashed)
        index = index_rows[:, span]
        both = jnp.stack([grad_raw, attention]).reshape(2 * heads, slots, HALO)
        merged = jnp.zeros_like(both)
        for slot in range(slots):
            same = (index == index[slot : slot + 1, :])[None]
            merged = merged + jnp.where(same, both[:, slot : slot + 1, :], 0.0)
        atom = lax.broadcasted_iota(jnp.int32, (slots, HALO), 1)
        edge_rows = 2 * heads * slots
        message[:edge_rows, :] = merged.reshape(edge_rows, HALO)
        message[edge_rows : edge_rows + slots, :] = (index - HALO - atom).astype(F32)
        message[edge_rows + slots :, :] = jnp.zeros_like(message[edge_rows + slots :, :])


def joined_rows(early, late, first_row, rows):
    return jnp.concatenate(
        [head_rows_of(early, first_row, rows), head_rows_of(late, first_row, rows)], axis=0
    )


def grads_kernel(heads, slots, pieces, place, fm, fo, *refs):
    chunks = [refs[at : at + 4] for at in range(0, 4 * pieces, 4)]
    (qkv, halo_a, halo_b, cot, slot_own, message_a, message_b, grad_query, own_key, own_value, kept,
     sent_1, sent_2, sent_3, ext, weight_terms) = refs[4 * pieces :]
    places = [(chunk, at) for chunk in chunks for at in range(chunk[0].shape[0])]
    comps, chan_local = fm.shape[0], fm.shape[1]
    rows = chan_local // heads
    atoms = 2 * HALO
    core = place[0]
    empty = jnp.zeros((HALO, HALO), BF16)
    coefs = [message[: 2 * heads * slots, :].T for message in (message_a, message_b)]
    for head in range(heads):
        tables = []
        for quantity in (head, heads + head):
            halves = []
            for half in range(2):
                tiles = [spread(slot_own[half, t], coefs[half], quantity, slots) for t in range(3)]
                tiles = tiles + [empty] if half == 0 else [empty] + tiles
                halves.append(jnp.concatenate(tiles, axis=1))
            tables.append(jnp.concatenate(halves, axis=0))
        raw_table, attn_table = tables
        query = head_rows_of(qkv, head * rows, rows)
        key = head_rows_of(qkv, chan_local + head * rows, rows)
        halo_key = joined_rows(halo_a, halo_b, chan_local + head * rows, rows)
        key_ext = jnp.concatenate([halo_key[:, :HALO], key, halo_key[:, HALO:]], axis=1)
        span = slice(head * rows, (head + 1) * rows)
        value_span = slice(chan_local + head * rows, chan_local + (head + 1) * rows)
        grad_query[:, span, :] = nt(key_ext, raw_table).astype(BF16).reshape(comps, rows, atoms)
        key_sums = nn(query, raw_table)
        own_key[:, span, :] = key_sums[:, HALO : HALO + atoms].reshape(comps, rows, atoms)
        ext[:, span, :] = key_sums.astype(BF16).reshape(comps, rows, atoms + 2 * HALO)
        value_sums = nn(head_rows_of(cot, head * rows, rows), attn_table)
        own_value[:, span, :] = value_sums[:, HALO : HALO + atoms].reshape(comps, rows, atoms)
        ext[:, value_span, :] = value_sums.astype(BF16).reshape(comps, rows, atoms + 2 * HALO)
    for degree in range(LMAX + 1):
        query_total = jnp.zeros((chan_local, 2 * chan_local), F32)
        keyval_total = jnp.zeros((2 * chan_local, 2 * chan_local), F32)
        for comp in range(degree * degree, (degree + 1) * (degree + 1)):
            own = jnp.concatenate([fm[comp], fo[comp]], axis=0)
            (flm, flo, frm, fro), at = places[comp]
            wide = jnp.concatenate(
                [
                    jnp.concatenate([flm[at], fm[comp], frm[at]], axis=1),
                    jnp.concatenate([flo[at], fo[comp], fro[at]], axis=1),
                ],
                axis=0,
            )
            query_total = query_total + nt(grad_query[comp], own)
            keyval_total = keyval_total + nt(ext[comp], wide)
        total = jnp.concatenate([query_total, keyval_total], axis=0)
        total = jnp.where(core == 0, total, pltpu.roll(total, chan_local, 1))
        for g in range(3):
            weight_terms[g * (LMAX + 1) + degree] = total[g * chan_local : (g + 1) * chan_local]
    piece = chan_local // 4
    spot = place[2]
    for delta, part in enumerate((kept, sent_1, sent_2, sent_3)):
        first = pl.multiple_of((spot ^ delta) * piece, piece)
        part[...] = weight_terms[:, pl.ds(first, piece), :].astype(part.dtype)


def halo_slots(message_left, message_right, quantities, slots):
    coefs, tables = [], []
    for message, tile in ((message_left, 2), (message_right, 0)):
        coefs.append(message[: quantities * slots, :].T)
        offset = message[quantities * slots : (quantities + 1) * slots, :].astype(jnp.int32)
        atom = lax.broadcasted_iota(jnp.int32, offset.shape, 1)
        tables.append(slot_tile(wide_transpose(offset + HALO + atom)[:, :slots], tile))
    return coefs, tables


def final_kernel(heads, slots, start, grad_query, own_key, own_value, halo_qkv, cl, cr,
                 message_left, message_right, wc, mine, theirs, token, grad):
    token[...] = jnp.zeros_like(token)
    comps, chan_local = halo_qkv.shape[0], cl.shape[1]
    rows = chan_local // heads
    stop = start + comps
    grad[:, :chan_local, :] = grad_query[start:stop]
    coefs, tables = halo_slots(message_left, message_right, 2 * heads, slots)
    for head in range(heads):
        span = slice(head * rows, (head + 1) * rows)
        query = head_rows_of(halo_qkv, head * rows, rows)
        sides = (
            (own_key, chan_local, head, (query[:, :HALO], query[:, HALO:])),
            (
                own_value,
                2 * chan_local,
                heads + head,
                tuple(side[start:stop, span, :].reshape(comps * rows, HALO) for side in (cl, cr)),
            ),
        )
        for own, first, quantity, outer in sides:
            rim = [
                nn(outer[at], spread(tables[at], coefs[at], quantity, slots)) for at in range(2)
            ]
            total = own[start:stop, span, :].reshape(comps * rows, 2 * HALO)
            total = total + jnp.concatenate(rim, axis=1)
            grad[:, first + head * rows : first + (head + 1) * rows, :] = (
                total.astype(BF16).reshape(comps, rows, 2 * HALO)
            )
    for comp in range(comps):
        total = nn(wc[degree_of(start + comp)], grad[comp])
        mine[comp] = total[:chan_local]
        theirs[comp] = total[chan_local:].astype(BF16)


def finish_kernel(*refs):
    out, start = refs[-1], 0
    for mine, theirs in zip(refs[:-1:2], refs[1:-1:2]):
        stop = start + mine.shape[0]
        out[start:stop] = (mine[...] + theirs[...].astype(F32)).astype(BF16)
        start = stop


def gather_kernel(place, part_0, part_1, part_2, part_3, out):
    piece = part_0.shape[1]
    spot = place[2]
    for delta, part in enumerate((part_0, part_1, part_2, part_3)):
        first = pl.multiple_of((spot ^ delta) * piece, piece)
        out[:, pl.ds(first, piece), :] = part[...].astype(F32)


def call(kernel, args, outs, scratch=(), scalars=0, limit=24, stay=(), tokens=(), flops=0):
    whole = pl.BlockSpec(memory_space=pltpu.VMEM)
    small = pl.BlockSpec(memory_space=pltpu.SMEM)
    args = [
        pltpu.with_memory_space_constraint(a, pltpu.VMEM) if at in stay else a
        for at, a in enumerate(args)
    ]
    count = len(args)

    def body(*refs):
        kernel(*refs[:count], *refs[count + len(tokens) :])

    return pl.pallas_call(
        body,
        out_shape=tuple(outs),
        in_specs=[small] * scalars
        + [whole] * (count - scalars)
        + [pl.BlockSpec(memory_space=pl.ANY)] * len(tokens),
        out_specs=tuple([whole] * len(outs)),
        scratch_shapes=list(scratch),
        compiler_params=pltpu.CompilerParams(vmem_limit_bytes=limit * 1024 * 1024),
        cost_estimate=pl.CostEstimate(flops=flops, bytes_accessed=1024, transcendentals=0),
    )(*args, *tokens)


def after(values, tokens):
    anywhere = pl.BlockSpec(memory_space=pl.ANY)
    count = len(values)

    def kernel(*refs):
        pass

    return pl.pallas_call(
        kernel,
        out_shape=tuple(jax.ShapeDtypeStruct(v.shape, v.dtype) for v in values),
        in_specs=[anywhere] * (count + len(tokens)),
        out_specs=tuple([anywhere] * count),
        input_output_aliases={i: i for i in range(count)},
        compiler_params=pltpu.CompilerParams(vmem_limit_bytes=1024 * 1024),
        cost_estimate=pl.CostEstimate(flops=0, bytes_accessed=1024, transcendentals=0),
    )(*values, *tokens)


def shifted(value, axis, steps):
    count = lax.axis_size(axis)
    pairs = [(source, (source + steps) % count) for source in range(count)]
    return lax.ppermute(value, axis, pairs)


def exchanged(value, axis, offset):
    count = lax.axis_size(axis)
    return lax.ppermute(value, axis, [(source, source ^ offset) for source in range(count)])


def on_device(features, weights, cotangent, edge_bias, neighbours, valid_mask):
    chan_local, comps, atoms_dev = features.shape
    heads, slots = edge_bias.shape[0], edge_bias.shape[1]
    channels = weights.shape[2]
    assert atoms_dev == 2 * HALO and channels == 2 * chan_local
    score_scale = 1.0 / math.sqrt(chan_local // heads * comps)
    total_atoms = atoms_dev * lax.axis_size("atom")
    count = lax.axis_size("atom")
    assert count >= 4 and count & (count - 1) == 0
    atom_place = lax.axis_index("atom")
    cut_bits = (1, 2) if count >= 8 else (0, 1)
    spot = (atom_place >> cut_bits[0]) & 3
    place = jnp.stack([lax.axis_index("chan"), atom_place * atoms_dev, spot])
    place = place.astype(jnp.int32)
    feature_cut = comps // 2
    feature_cuts = ((0, feature_cut), (feature_cut, comps))

    def held(*dims, dtype=F32):
        return pltpu.VMEM(dims, dtype)

    def plain(*dims, dtype=F32):
        return jax.ShapeDtypeStruct(dims, dtype)

    fm = jnp.transpose(features, (1, 0, 2))
    cot = jnp.transpose(cotangent, (1, 0, 2))
    mix = jnp.transpose(weights, (0, 1, 3, 2))
    anywhere = pl.BlockSpec(memory_space=pl.ANY)
    rim_count = 2 * len(feature_cuts)
    feature_rims = pl.pallas_call(
        functools.partial(split_kernel, feature_cuts),
        out_shape=tuple(
            held(stop - start, chan_local, HALO, dtype=BF16)
            for start, stop in feature_cuts
            for _ in range(2)
        ),
        in_specs=[anywhere],
        out_specs=(pl.BlockSpec(memory_space=pltpu.VMEM),) * rim_count,
        scratch_shapes=[pltpu.SemaphoreType.DMA((rim_count,))],
        compiler_params=pltpu.CompilerParams(vmem_limit_bytes=4 * 1024 * 1024),
    )(pltpu.with_memory_space_constraint(fm, pltpu.HBM))
    from_sides = [
        shifted(rim, "atom", 1 if at % 2 == 0 else -1) for at, rim in enumerate(feature_rims)
    ]
    fo = shifted(fm, "chan", 1)

    qkv, scores, slot_own, index_rows, index_wide, wp, wc, token, *rims = call(
        functools.partial(own_kernel, heads, total_atoms),
        (place, fm, fo, cot, mix, neighbours),
        (
            held(comps, 3 * chan_local, atoms_dev, dtype=BF16),
            held(2 * heads, atoms_dev, atoms_dev),
            held(2, 3, HALO, HALO, dtype=jnp.int32),
            held(slots, atoms_dev, dtype=jnp.int32),
            held(atoms_dev, HALO, dtype=jnp.int32),
            held(LMAX + 1, 3 * chan_local, channels, dtype=BF16),
            held(LMAX + 1, channels, 3 * chan_local, dtype=BF16),
            plain(8, HALO),
            *(
                plain(comps, chan_local, HALO, dtype=BF16) for _ in range(2)
            ),
        ),
        scalars=1,
        stay=(1, 2, 3),
        flops=12 * 10**9,
    )
    flm, frm = after(from_sides[:2], (token,))
    early_chunk = (flm, shifted(flm, "chan", 1), frm, shifted(frm, "chan", 1))
    halo_a, partial, token = call(
        functools.partial(early_kernel, heads),
        (*early_chunk, wp, qkv, cot),
        (
            held(feature_cut, 3 * chan_local, atoms_dev, dtype=BF16),
            held(2 * heads, 2, HALO, HALO),
            plain(8, HALO),
        ),
        stay=tuple(range(7)),
    )
    rims = after(rims, (token,))
    late_sides = after(from_sides[2:], (token,))
    late_chunks = []
    for flm, frm in zip(late_sides[::2], late_sides[1::2]):
        late_chunks += [flm, shifted(flm, "chan", 1), frm, shifted(frm, "chan", 1)]
    from_left, from_right = shifted(rims[0], "atom", 1), shifted(rims[1], "atom", -1)
    halo_b, grad_bias, message_a, message_b = call(
        functools.partial(edge_kernel, heads, score_scale, feature_cut, len(late_chunks) // 4),
        (*late_chunks, wp, qkv, cot, scores, partial, edge_bias, valid_mask, index_rows, index_wide),
        (
            held(comps - feature_cut, 3 * chan_local, atoms_dev, dtype=BF16),
            plain(heads, slots, atoms_dev),
            held((2 * heads + 3) * slots, HALO),
            held((2 * heads + 3) * slots, HALO),
        ),
        stay=(*range(len(late_chunks) + 5), len(late_chunks) + 7, len(late_chunks) + 8),
    )
    message_left = shifted(message_b, "atom", 1)
    message_right = shifted(message_a, "atom", -1)
    piece = (3 * (LMAX + 1), chan_local // 4, channels)
    grad_query, own_key, own_value, kept, *sent = call(
        functools.partial(grads_kernel, heads, slots, len(feature_cuts)),
        (place, fm, fo, *early_chunk, *late_chunks, qkv, halo_a, halo_b, cot, slot_own, message_a,
         message_b),
        (
            held(comps, chan_local, atoms_dev, dtype=BF16),
            held(comps, chan_local, atoms_dev),
            held(comps, chan_local, atoms_dev),
            held(*piece),
            plain(*piece, dtype=BF16),
            plain(*piece, dtype=BF16),
            plain(*piece, dtype=BF16),
        ),
        scratch=[
            pltpu.VMEM((comps, 2 * chan_local, 2 * atoms_dev), BF16),
            pltpu.VMEM((3 * (LMAX + 1), chan_local, channels), F32),
        ],
        scalars=1,
        stay=tuple(range(1, 10 + 4 * len(feature_cuts))),
    )
    for delta, part in enumerate(sent, 1):
        kept = kept + exchanged(part, "atom", delta << cut_bits[0]).astype(F32)
    rest = [bit for bit in reversed(range(count.bit_length() - 1)) if bit not in cut_bits]
    for bit in rest:
        arrived = exchanged(kept.astype(BF16), "atom", 1 << bit)
        if bit == rest[-1]:
            from_left, from_right, message_left, message_right, arrived = after(
                (from_left, from_right, message_left, message_right, arrived), ()
            )
        kept = kept + arrived.astype(F32)
    rounded = kept.astype(BF16)
    pieces = [rounded] + [exchanged(rounded, "atom", d << cut_bits[0]) for d in range(1, 4)]
    (grad_weights,) = call(
        gather_kernel,
        (place, *pieces),
        (plain(3 * (LMAX + 1), chan_local, channels),),
        scalars=1,
        limit=8,
        flops=20 * 10**9,
    )
    parts, tokens = [], ()
    for (start, stop), halo_qkv in zip(feature_cuts, (halo_a, halo_b)):
        size = stop - start
        mine, theirs, token = call(
            functools.partial(final_kernel, heads, slots, start),
            (grad_query, own_key, own_value, halo_qkv, from_left, from_right, message_left,
             message_right, wc),
            (
                held(size, chan_local, atoms_dev),
                held(size, chan_local, atoms_dev, dtype=BF16),
                plain(8, HALO),
            ),
            scratch=[pltpu.VMEM((size, 3 * chan_local, atoms_dev), BF16)],
            limit=16,
            stay=(0, 1, 2, 3, 4, 5, 8),
            tokens=tokens,
        )
        parts += [mine, shifted(theirs, "chan", 1)]
        tokens = (token, pieces[2])
    (out,) = call(
        finish_kernel,
        parts,
        (plain(comps, chan_local, atoms_dev, dtype=BF16),),
        limit=8,
        stay=tuple(range(len(parts))),
    )
    grad_features = jnp.transpose(out, (1, 0, 2))
    grad_weights = grad_weights.reshape(3, LMAX + 1, chan_local, channels)
    grad_weights = jnp.transpose(grad_weights, (0, 1, 3, 2))
    return grad_features, grad_weights, grad_bias


def solution(mesh):
    in_specs = (
        P("chan", None, "atom"),
        P(None, None, None, "chan"),
        P("chan", None, "atom"),
        P("chan", None, "atom"),
        P(None, "atom"),
        P(None, "atom"),
    )
    out_specs = (P("chan", None, "atom"), P(None, None, None, "chan"), P("chan", None, "atom"))
    return jax.shard_map(
        on_device, mesh=mesh, in_specs=in_specs, out_specs=out_specs, check_vma=False
    )
```

```python
import functools
import math

import jax
import jax.numpy as jnp
from jax import lax
from jax.experimental import pallas as pl
from jax.experimental.pallas import tpu as pltpu
from jax.sharding import PartitionSpec as P

LMAX = 6
HALO = 128
SOFT_CAP = 10.0
F32 = jnp.float32
BF16 = jnp.bfloat16


def degree_of(comp):
    return math.isqrt(comp)


def nn(lhs, rhs):
    return lax.dot_general(lhs, rhs, (((1,), (0,)), ((), ())), preferred_element_type=F32)


def nt(lhs, rhs):
    return lax.dot_general(lhs, rhs, (((1,), (1,)), ((), ())), preferred_element_type=F32)


def tn(lhs, rhs):
    return lax.dot_general(lhs, rhs, (((0,), (0,)), ((), ())), preferred_element_type=F32)


def pick(table, index):
    return jnp.take_along_axis(table, index, axis=1, mode="promise_in_bounds")


def head_rows_of(ref, first_row, rows):
    block = ref[:, first_row : first_row + rows, :]
    return block.reshape(block.shape[0] * rows, block.shape[2])


def slot_tile(window_index, tile):
    atoms, slots = window_index.shape
    lane = lax.broadcasted_iota(jnp.int32, (atoms, HALO), 1) + tile * HALO
    found = jnp.full((atoms, HALO), -1, jnp.int32)
    for slot in range(slots):
        found = jnp.where(window_index[:, slot : slot + 1] == lane, slot, found)
    return found


def spread(slot, coef, quantity, slots):
    values = pick(coef, jnp.maximum(slot, 0) + quantity * slots)
    return jnp.where(slot >= 0, values, 0.0).astype(BF16)


def wide_transpose(rows):
    return jnp.concatenate([rows] * (HALO // rows.shape[0]), axis=0).T


def split_kernel(cuts, fm, *refs):
    *parts, sems = refs
    copies = []
    for at, part in enumerate(parts):
        start, stop = cuts[at // 2]
        atom = HALO if at % 2 == 0 else 0
        copies.append(
            pltpu.make_async_copy(
                fm.at[pl.ds(start, stop - start), :, pl.ds(atom, HALO)], part, sems.at[at]
            )
        )
    for copy in copies:
        copy.start()
    for copy in copies:
        copy.wait()


def own_kernel(heads, total_atoms, place, fm, fo, cot, weights, neighbours,
               qkv, scores, slot_own, index_rows, index_wide, wp, wc, token, *rims):
    token[...] = jnp.zeros_like(token)
    rims[0][...] = cot[:, :, HALO:]
    rims[1][...] = cot[:, :, :HALO]
    comps, chan_local = fm.shape[0], fm.shape[1]
    channels = weights.shape[3]
    rows = chan_local // heads
    slots = neighbours.shape[0]
    core, first_atom = place[0], place[1]
    for degree in range(LMAX + 1):
        mix = jnp.concatenate([weights[g, degree] for g in range(3)], axis=0).astype(F32)
        mix = jnp.where(core == 0, mix, pltpu.roll(mix, chan_local, 1))
        wp[degree] = mix.astype(BF16)
        padded = jnp.concatenate([mix, jnp.zeros((chan_local, channels), F32)], axis=0)
        wc[degree] = padded.T[:, : 3 * chan_local].astype(BF16)
    for comp in range(comps):
        feats = jnp.concatenate([fm[comp], fo[comp]], axis=0)
        qkv[comp] = nn(wp[degree_of(comp)], feats).astype(BF16)
    for head in range(heads):
        query = head_rows_of(qkv, head * rows, rows)
        key = head_rows_of(qkv, chan_local + head * rows, rows)
        value = head_rows_of(qkv, 2 * chan_local + head * rows, rows)
        scores[head] = tn(query, key)
        scores[heads + head] = tn(head_rows_of(cot, head * rows, rows), value)
    for half in range(2):
        span = slice(half * HALO, (half + 1) * HALO)
        index = neighbours[:, span] - (first_atom + (half - 1) * HALO)
        index = jnp.where(index < 0, index + total_atoms, index)
        index = jnp.where(index >= total_atoms, index - total_atoms, index)
        index_rows[:, span] = index
        wide = wide_transpose(index)
        index_wide[span, :] = wide
        for tile in range(3):
            slot_own[half, tile] = slot_tile(wide[:, :slots], tile)


def project_halo(start, chunks, wp, halo_qkv):
    at = 0
    for flm, flo, frm, fro in chunks:
        for comp in range(flm.shape[0]):
            feats = jnp.concatenate(
                [
                    jnp.concatenate([flm[comp], frm[comp]], axis=1),
                    jnp.concatenate([flo[comp], fro[comp]], axis=1),
                ],
                axis=0,
            )
            halo_qkv[at] = nn(wp[degree_of(start + at)], feats).astype(BF16)
            at += 1


def halo_scores(heads, quantity, start, qkv, cot, halo_qkv):
    size, chan_local = halo_qkv.shape[0], cot.shape[1]
    rows = chan_local // heads
    head = quantity % heads
    first = (1 if quantity < heads else 2) * chan_local + head * rows
    source = qkv if quantity < heads else cot
    mine = source[start : start + size, head * rows : (head + 1) * rows, :]
    mine = mine.reshape(size * rows, mine.shape[2])
    theirs = head_rows_of(halo_qkv, first, rows)
    return tn(mine[:, :HALO], theirs[:, :HALO]), tn(mine[:, HALO:], theirs[:, HALO:])


def early_kernel(heads, flm, flo, frm, fro, wp, qkv, cot, halo_qkv, partial, token):
    token[...] = jnp.zeros_like(token)
    project_halo(0, [(flm, flo, frm, fro)], wp, halo_qkv)
    for quantity in range(2 * heads):
        left, right = halo_scores(heads, quantity, 0, qkv, cot, halo_qkv)
        partial[quantity, 0] = left
        partial[quantity, 1] = right


def edge_kernel(heads, score_scale, start, late, *refs):
    chunks = [refs[at : at + 4] for at in range(0, 4 * late, 4)]
    (wp, qkv, cot, scores, partial, bias, valid, index_rows, index_wide,
     halo_qkv, grad_bias, message_a, message_b) = refs[4 * late :]
    slots = valid.shape[0]
    project_halo(start, chunks, wp, halo_qkv)
    lane = lax.broadcasted_iota(jnp.int32, (HALO, 2 * heads * slots), 1)
    gathered = [jnp.zeros((HALO, 2 * heads * slots), F32) for _ in range(2)]
    for quantity in range(2 * heads):
        left, right = halo_scores(heads, quantity, start, qkv, cot, halo_qkv)
        left, right = left + partial[quantity, 0], right + partial[quantity, 1]
        for half in range(2):
            own = scores[quantity, half * HALO : (half + 1) * HALO, :]
            own = [own[:, :HALO], own[:, HALO:]]
            tiles = [left] + own if half == 0 else own + [right]
            index = index_wide[half * HALO : (half + 1) * HALO, :]
            inner, tile_of = index & (HALO - 1), index >> 7
            values = jnp.where(
                tile_of == 0,
                pick(tiles[0], inner),
                jnp.where(tile_of == 1, pick(tiles[1], inner), pick(tiles[2], inner)),
            )
            gathered[half] = jnp.where(lane // slots == quantity, values, gathered[half])
    for half, message in enumerate((message_a, message_b)):
        span = slice(half * HALO, (half + 1) * HALO)
        edges = gathered[half].T.reshape(2, heads, slots, HALO)
        squashed = jnp.tanh(edges[0] * (score_scale / SOFT_CAP))
        logits = SOFT_CAP * squashed + bias[:, :, span]
        live = valid[:, span][None] > 0
        weight = jnp.where(live, jnp.exp(logits), 0.0)
        attention = weight / jnp.sum(weight, axis=1, keepdims=True)
        grad_attn = edges[1]
        grad_logit = attention * (
            grad_attn - jnp.sum(attention * grad_attn, axis=1, keepdims=True)
        )
        grad_bias[:, :, span] = grad_logit
        grad_raw = score_scale * grad_logit * (1.0 - squashed * squashed)
        index = index_rows[:, span]
        both = jnp.stack([grad_raw, attention]).reshape(2 * heads, slots, HALO)
        merged = jnp.zeros_like(both)
        for slot in range(slots):
            same = (index == index[slot : slot + 1, :])[None]
            merged = merged + jnp.where(same, both[:, slot : slot + 1, :], 0.0)
        atom = lax.broadcasted_iota(jnp.int32, (slots, HALO), 1)
        edge_rows = 2 * heads * slots
        message[:edge_rows, :] = merged.reshape(edge_rows, HALO)
        message[edge_rows : edge_rows + slots, :] = (index - HALO - atom).astype(F32)
        message[edge_rows + slots :, :] = jnp.zeros_like(message[edge_rows + slots :, :])


def joined_rows(early, late, first_row, rows):
    return jnp.concatenate(
        [head_rows_of(early, first_row, rows), head_rows_of(late, first_row, rows)], axis=0
    )


def grads_kernel(heads, slots, pieces, place, fm, fo, *refs):
    chunks = [refs[at : at + 4] for at in range(0, 4 * pieces, 4)]
    (qkv, halo_a, halo_b, cot, slot_own, message_a, message_b, grad_query, own_key, own_value, kept,
     sent_1, sent_2, sent_3, ext, weight_terms) = refs[4 * pieces :]
    places = [(chunk, at) for chunk in chunks for at in range(chunk[0].shape[0])]
    comps, chan_local = fm.shape[0], fm.shape[1]
    rows = chan_local // heads
    atoms = 2 * HALO
    core = place[0]
    empty = jnp.zeros((HALO, HALO), BF16)
    coefs = [message[: 2 * heads * slots, :].T for message in (message_a, message_b)]
    for head in range(heads):
        tables = []
        for quantity in (head, heads + head):
            halves = []
            for half in range(2):
                tiles = [spread(slot_own[half, t], coefs[half], quantity, slots) for t in range(3)]
                tiles = tiles + [empty] if half == 0 else [empty] + tiles
                halves.append(jnp.concatenate(tiles, axis=1))
            tables.append(jnp.concatenate(halves, axis=0))
        raw_table, attn_table = tables
        query = head_rows_of(qkv, head * rows, rows)
        key = head_rows_of(qkv, chan_local + head * rows, rows)
        halo_key = joined_rows(halo_a, halo_b, chan_local + head * rows, rows)
        key_ext = jnp.concatenate([halo_key[:, :HALO], key, halo_key[:, HALO:]], axis=1)
        span = slice(head * rows, (head + 1) * rows)
        value_span = slice(chan_local + head * rows, chan_local + (head + 1) * rows)
        grad_query[:, span, :] = nt(key_ext, raw_table).astype(BF16).reshape(comps, rows, atoms)
        key_sums = nn(query, raw_table)
        own_key[:, span, :] = key_sums[:, HALO : HALO + atoms].reshape(comps, rows, atoms)
        ext[:, span, :] = key_sums.astype(BF16).reshape(comps, rows, atoms + 2 * HALO)
        value_sums = nn(head_rows_of(cot, head * rows, rows), attn_table)
        own_value[:, span, :] = value_sums[:, HALO : HALO + atoms].reshape(comps, rows, atoms)
        ext[:, value_span, :] = value_sums.astype(BF16).reshape(comps, rows, atoms + 2 * HALO)
    for degree in range(LMAX + 1):
        query_total = jnp.zeros((chan_local, 2 * chan_local), F32)
        keyval_total = jnp.zeros((2 * chan_local, 2 * chan_local), F32)
        for comp in range(degree * degree, (degree + 1) * (degree + 1)):
            own = jnp.concatenate([fm[comp], fo[comp]], axis=0)
            (flm, flo, frm, fro), at = places[comp]
            wide = jnp.concatenate(
                [
                    jnp.concatenate([flm[at], fm[comp], frm[at]], axis=1),
                    jnp.concatenate([flo[at], fo[comp], fro[at]], axis=1),
                ],
                axis=0,
            )
            query_total = query_total + nt(grad_query[comp], own)
            keyval_total = keyval_total + nt(ext[comp], wide)
        total = jnp.concatenate([query_total, keyval_total], axis=0)
        total = jnp.where(core == 0, total, pltpu.roll(total, chan_local, 1))
        for g in range(3):
            weight_terms[g * (LMAX + 1) + degree] = total[g * chan_local : (g + 1) * chan_local]
    piece = chan_local // 4
    spot = place[2]
    for delta, part in enumerate((kept, sent_1, sent_2, sent_3)):
        first = pl.multiple_of((spot ^ delta) * piece, piece)
        part[...] = weight_terms[:, pl.ds(first, piece), :].astype(part.dtype)


def halo_slots(message_left, message_right, quantities, slots):
    coefs, tables = [], []
    for message, tile in ((message_left, 2), (message_right, 0)):
        coefs.append(message[: quantities * slots, :].T)
        offset = message[quantities * slots : (quantities + 1) * slots, :].astype(jnp.int32)
        atom = lax.broadcasted_iota(jnp.int32, offset.shape, 1)
        tables.append(slot_tile(wide_transpose(offset + HALO + atom)[:, :slots], tile))
    return coefs, tables


def final_kernel(heads, slots, start, grad_query, own_key, own_value, halo_qkv, cl, cr,
                 message_left, message_right, wc, mine, theirs, token, grad):
    token[...] = jnp.zeros_like(token)
    comps, chan_local = halo_qkv.shape[0], cl.shape[1]
    rows = chan_local // heads
    stop = start + comps
    grad[:, :chan_local, :] = grad_query[start:stop]
    coefs, tables = halo_slots(message_left, message_right, 2 * heads, slots)
    for head in range(heads):
        span = slice(head * rows, (head + 1) * rows)
        query = head_rows_of(halo_qkv, head * rows, rows)
        sides = (
            (own_key, chan_local, head, (query[:, :HALO], query[:, HALO:])),
            (
                own_value,
                2 * chan_local,
                heads + head,
                tuple(side[start:stop, span, :].reshape(comps * rows, HALO) for side in (cl, cr)),
            ),
        )
        for own, first, quantity, outer in sides:
            rim = [
                nn(outer[at], spread(tables[at], coefs[at], quantity, slots)) for at in range(2)
            ]
            total = own[start:stop, span, :].reshape(comps * rows, 2 * HALO)
            total = total + jnp.concatenate(rim, axis=1)
            grad[:, first + head * rows : first + (head + 1) * rows, :] = (
                total.astype(BF16).reshape(comps, rows, 2 * HALO)
            )
    for comp in range(comps):
        total = nn(wc[degree_of(start + comp)], grad[comp])
        mine[comp] = total[:chan_local]
        theirs[comp] = total[chan_local:].astype(BF16)


def finish_kernel(*refs):
    out, start = refs[-1], 0
    for mine, theirs in zip(refs[:-1:2], refs[1:-1:2]):
        stop = start + mine.shape[0]
        out[start:stop] = (mine[...] + theirs[...].astype(F32)).astype(BF16)
        start = stop


def gather_kernel(place, part_0, part_1, part_2, part_3, out):
    piece = part_0.shape[1]
    spot = place[2]
    for delta, part in enumerate((part_0, part_1, part_2, part_3)):
        first = pl.multiple_of((spot ^ delta) * piece, piece)
        out[:, pl.ds(first, piece), :] = part[...].astype(F32)


def add_kernel(*refs):
    *parts, total, rounded = refs
    value = parts[0][...]
    for part in parts[1:]:
        value = value + part[...].astype(F32)
    total[...] = value
    rounded[...] = value.astype(BF16)


def call(kernel, args, outs, scratch=(), scalars=0, limit=24, stay=(), tokens=(), flops=0):
    whole = pl.BlockSpec(memory_space=pltpu.VMEM)
    small = pl.BlockSpec(memory_space=pltpu.SMEM)
    args = [
        pltpu.with_memory_space_constraint(a, pltpu.VMEM) if at in stay else a
        for at, a in enumerate(args)
    ]
    count = len(args)

    def body(*refs):
        kernel(*refs[:count], *refs[count + len(tokens) :])

    return pl.pallas_call(
        body,
        out_shape=tuple(outs),
        in_specs=[small] * scalars
        + [whole] * (count - scalars)
        + [pl.BlockSpec(memory_space=pl.ANY)] * len(tokens),
        out_specs=tuple([whole] * len(outs)),
        scratch_shapes=list(scratch),
        compiler_params=pltpu.CompilerParams(vmem_limit_bytes=limit * 1024 * 1024),
        cost_estimate=pl.CostEstimate(flops=flops, bytes_accessed=1024, transcendentals=0),
    )(*args, *tokens)


def after(values, tokens):
    anywhere = pl.BlockSpec(memory_space=pl.ANY)
    count = len(values)

    def kernel(*refs):
        pass

    return pl.pallas_call(
        kernel,
        out_shape=tuple(jax.ShapeDtypeStruct(v.shape, v.dtype) for v in values),
        in_specs=[anywhere] * (count + len(tokens)),
        out_specs=tuple([anywhere] * count),
        input_output_aliases={i: i for i in range(count)},
        compiler_params=pltpu.CompilerParams(vmem_limit_bytes=1024 * 1024),
        cost_estimate=pl.CostEstimate(flops=0, bytes_accessed=1024, transcendentals=0),
    )(*values, *tokens)


def shifted(value, axis, steps):
    count = lax.axis_size(axis)
    pairs = [(source, (source + steps) % count) for source in range(count)]
    return lax.ppermute(value, axis, pairs)


def exchanged(value, axis, offset):
    count = lax.axis_size(axis)
    return lax.ppermute(value, axis, [(source, source ^ offset) for source in range(count)])


def on_device(features, weights, cotangent, edge_bias, neighbours, valid_mask):
    chan_local, comps, atoms_dev = features.shape
    heads, slots = edge_bias.shape[0], edge_bias.shape[1]
    channels = weights.shape[2]
    assert atoms_dev == 2 * HALO and channels == 2 * chan_local
    score_scale = 1.0 / math.sqrt(chan_local // heads * comps)
    total_atoms = atoms_dev * lax.axis_size("atom")
    count = lax.axis_size("atom")
    assert count >= 4 and count & (count - 1) == 0
    atom_place = lax.axis_index("atom")
    cut_bits = (1, 2) if count >= 8 else (0, 1)
    spot = (atom_place >> cut_bits[0]) & 3
    place = jnp.stack([lax.axis_index("chan"), atom_place * atoms_dev, spot])
    place = place.astype(jnp.int32)
    feature_cut = comps // 2 - 6
    feature_cuts = ((0, feature_cut), (feature_cut, comps))

    def held(*dims, dtype=F32):
        return pltpu.VMEM(dims, dtype)

    def plain(*dims, dtype=F32):
        return jax.ShapeDtypeStruct(dims, dtype)

    fm = jnp.transpose(features, (1, 0, 2))
    cot = jnp.transpose(cotangent, (1, 0, 2))
    mix = jnp.transpose(weights, (0, 1, 3, 2))
    anywhere = pl.BlockSpec(memory_space=pl.ANY)
    rim_count = 2 * len(feature_cuts)
    feature_rims = pl.pallas_call(
        functools.partial(split_kernel, feature_cuts),
        out_shape=tuple(
            held(stop - start, chan_local, HALO, dtype=BF16)
            for start, stop in feature_cuts
            for _ in range(2)
        ),
        in_specs=[anywhere],
        out_specs=(pl.BlockSpec(memory_space=pltpu.VMEM),) * rim_count,
        scratch_shapes=[pltpu.SemaphoreType.DMA((rim_count,))],
        compiler_params=pltpu.CompilerParams(vmem_limit_bytes=4 * 1024 * 1024),
    )(pltpu.with_memory_space_constraint(fm, pltpu.HBM))
    from_sides = [
        shifted(rim, "atom", 1 if at % 2 == 0 else -1) for at, rim in enumerate(feature_rims)
    ]
    fo = shifted(fm, "chan", 1)

    qkv, scores, slot_own, index_rows, index_wide, wp, wc, token, *rims = call(
        functools.partial(own_kernel, heads, total_atoms),
        (place, fm, fo, cot, mix, neighbours),
        (
            held(comps, 3 * chan_local, atoms_dev, dtype=BF16),
            held(2 * heads, atoms_dev, atoms_dev),
            held(2, 3, HALO, HALO, dtype=jnp.int32),
            held(slots, atoms_dev, dtype=jnp.int32),
            held(atoms_dev, HALO, dtype=jnp.int32),
            held(LMAX + 1, 3 * chan_local, channels, dtype=BF16),
            held(LMAX + 1, channels, 3 * chan_local, dtype=BF16),
            plain(8, HALO),
            *(
                plain(comps, chan_local, HALO, dtype=BF16) for _ in range(2)
            ),
        ),
        scalars=1,
        stay=(1, 2, 3),
        flops=12 * 10**9,
    )
    flm, frm = after(from_sides[:2], (token,))
    early_chunk = (flm, shifted(flm, "chan", 1), frm, shifted(frm, "chan", 1))
    halo_a, partial, token = call(
        functools.partial(early_kernel, heads),
        (*early_chunk, wp, qkv, cot),
        (
            held(feature_cut, 3 * chan_local, atoms_dev, dtype=BF16),
            held(2 * heads, 2, HALO, HALO),
            plain(8, HALO),
        ),
        stay=tuple(range(7)),
    )
    rims = after(rims, (token,))
    late_sides = after(from_sides[2:], (token,))
    late_chunks = []
    for flm, frm in zip(late_sides[::2], late_sides[1::2]):
        late_chunks += [flm, shifted(flm, "chan", 1), frm, shifted(frm, "chan", 1)]
    from_left, from_right = shifted(rims[0], "atom", 1), shifted(rims[1], "atom", -1)
    halo_b, grad_bias, message_a, message_b = call(
        functools.partial(edge_kernel, heads, score_scale, feature_cut, len(late_chunks) // 4),
        (*late_chunks, wp, qkv, cot, scores, partial, edge_bias, valid_mask, index_rows, index_wide),
        (
            held(comps - feature_cut, 3 * chan_local, atoms_dev, dtype=BF16),
            plain(heads, slots, atoms_dev),
            held((2 * heads + 3) * slots, HALO),
            held((2 * heads + 3) * slots, HALO),
        ),
        stay=(*range(len(late_chunks) + 5), len(late_chunks) + 7, len(late_chunks) + 8),
    )
    message_left = shifted(message_b, "atom", 1)
    message_right = shifted(message_a, "atom", -1)
    piece = (3 * (LMAX + 1), chan_local // 4, channels)
    grad_query, own_key, own_value, kept, *sent = call(
        functools.partial(grads_kernel, heads, slots, len(feature_cuts)),
        (place, fm, fo, *early_chunk, *late_chunks, qkv, halo_a, halo_b, cot, slot_own, message_a,
         message_b),
        (
            held(comps, chan_local, atoms_dev, dtype=BF16),
            held(comps, chan_local, atoms_dev),
            held(comps, chan_local, atoms_dev),
            held(*piece),
            plain(*piece, dtype=BF16),
            plain(*piece, dtype=BF16),
            plain(*piece, dtype=BF16),
        ),
        scratch=[
            pltpu.VMEM((comps, 2 * chan_local, 2 * atoms_dev), BF16),
            pltpu.VMEM((3 * (LMAX + 1), chan_local, channels), F32),
        ],
        scalars=1,
        stay=tuple(range(1, 10 + 4 * len(feature_cuts))),
    )
    def summed(kept, parts):
        return call(
            add_kernel, (kept, *parts), (held(*piece), plain(*piece, dtype=BF16)), limit=8, stay=(0,)
        )

    kept, rounded = summed(
        kept, [exchanged(part, "atom", delta << cut_bits[0]) for delta, part in enumerate(sent, 1)]
    )
    rest = [bit for bit in reversed(range(count.bit_length() - 1)) if bit not in cut_bits]
    for bit in rest[:-1]:
        kept, rounded = summed(kept, [exchanged(rounded, "atom", 1 << bit)])
    last = exchanged(rounded, "atom", 1 << rest[-1])
    parts, tokens = [], (rounded,)
    for (start, stop), halo_qkv in zip(feature_cuts, (halo_a, halo_b)):
        size = stop - start
        mine, theirs, token = call(
            functools.partial(final_kernel, heads, slots, start),
            (grad_query, own_key, own_value, halo_qkv, from_left, from_right, message_left,
             message_right, wc),
            (
                held(size, chan_local, atoms_dev),
                held(size, chan_local, atoms_dev, dtype=BF16),
                plain(8, HALO),
            ),
            scratch=[pltpu.VMEM((size, 3 * chan_local, atoms_dev), BF16)],
            limit=16,
            stay=(0, 1, 2, 3, 4, 5, 8),
            tokens=tokens,
        )
        parts += [mine, shifted(theirs, "chan", 1)]
        tokens = (token, last)
    kept, rounded = summed(kept, after((last,), (token,)))
    pieces = [rounded] + [exchanged(rounded, "atom", d << cut_bits[0]) for d in range(1, 4)]
    (grad_weights,) = call(
        gather_kernel,
        (place, *pieces),
        (plain(3 * (LMAX + 1), chan_local, channels),),
        scalars=1,
        limit=8,
    )
    (out,) = call(
        finish_kernel,
        parts,
        (plain(comps, chan_local, atoms_dev, dtype=BF16),),
        limit=8,
        stay=tuple(range(len(parts))),
    )
    grad_features = jnp.transpose(out, (1, 0, 2))
    grad_weights = grad_weights.reshape(3, LMAX + 1, chan_local, channels)
    grad_weights = jnp.transpose(grad_weights, (0, 1, 3, 2))
    return grad_features, grad_weights, grad_bias


def solution(mesh):
    in_specs = (
        P("chan", None, "atom"),
        P(None, None, None, "chan"),
        P("chan", None, "atom"),
        P("chan", None, "atom"),
        P(None, "atom"),
        P(None, "atom"),
    )
    out_specs = (P("chan", None, "atom"), P(None, None, None, "chan"), P("chan", None, "atom"))
    return jax.shard_map(
        on_device, mesh=mesh, in_specs=in_specs, out_specs=out_specs, check_vma=False
    )
```

```python
import functools
import math

import jax
import jax.numpy as jnp
from jax import lax
from jax.experimental import pallas as pl
from jax.experimental.pallas import tpu as pltpu
from jax.sharding import PartitionSpec as P

LMAX = 6
HALO = 128
SOFT_CAP = 10.0
F32 = jnp.float32
BF16 = jnp.bfloat16


def degree_of(comp):
    return math.isqrt(comp)


def nn(lhs, rhs):
    return lax.dot_general(lhs, rhs, (((1,), (0,)), ((), ())), preferred_element_type=F32)


def nt(lhs, rhs):
    return lax.dot_general(lhs, rhs, (((1,), (1,)), ((), ())), preferred_element_type=F32)


def tn(lhs, rhs):
    return lax.dot_general(lhs, rhs, (((0,), (0,)), ((), ())), preferred_element_type=F32)


def pick(table, index):
    return jnp.take_along_axis(table, index, axis=1, mode="promise_in_bounds")


def head_rows_of(ref, first_row, rows):
    block = ref[:, first_row : first_row + rows, :]
    return block.reshape(block.shape[0] * rows, block.shape[2])


def slot_tile(window_index, tile):
    atoms, slots = window_index.shape
    lane = lax.broadcasted_iota(jnp.int32, (atoms, HALO), 1) + tile * HALO
    found = jnp.full((atoms, HALO), -1, jnp.int32)
    for slot in range(slots):
        found = jnp.where(window_index[:, slot : slot + 1] == lane, slot, found)
    return found


def spread(slot, coef, quantity, slots):
    values = pick(coef, jnp.maximum(slot, 0) + quantity * slots)
    return jnp.where(slot >= 0, values, 0.0).astype(BF16)


def wide_transpose(rows):
    return jnp.concatenate([rows] * (HALO // rows.shape[0]), axis=0).T


def split_kernel(start, parts, fm, *refs):
    *rims, sems = refs
    size = rims[0].shape[0]
    cuts = [size * at // parts for at in range(parts + 1)]
    copies = []
    for side, rim in enumerate(rims):
        atoms = pl.ds(HALO if side == 0 else 0, HALO)
        for at, (low, high) in enumerate(zip(cuts, cuts[1:])):
            copies.append(
                pltpu.make_async_copy(
                    fm.at[pl.ds(start + low, high - low), :, atoms],
                    rim.at[pl.ds(low, high - low)],
                    sems.at[side, at],
                )
            )
    for copy in copies:
        copy.start()
    for copy in copies:
        copy.wait()


def own_kernel(heads, total_atoms, place, fm, fo, cot, weights, neighbours,
               qkv, scores, slot_own, index_rows, index_wide, wp, wc, token, *rims):
    token[...] = jnp.zeros_like(token)
    rims[0][...] = cot[:, :, HALO:]
    rims[1][...] = cot[:, :, :HALO]
    comps, chan_local = fm.shape[0], fm.shape[1]
    channels = weights.shape[3]
    rows = chan_local // heads
    slots = neighbours.shape[0]
    core, first_atom = place[0], place[1]
    for degree in range(LMAX + 1):
        mix = jnp.concatenate([weights[g, degree] for g in range(3)], axis=0).astype(F32)
        mix = jnp.where(core == 0, mix, pltpu.roll(mix, chan_local, 1))
        wp[degree] = mix.astype(BF16)
        padded = jnp.concatenate([mix, jnp.zeros((chan_local, channels), F32)], axis=0)
        wc[degree] = padded.T[:, : 3 * chan_local].astype(BF16)
    for comp in range(comps):
        feats = jnp.concatenate([fm[comp], fo[comp]], axis=0)
        qkv[comp] = nn(wp[degree_of(comp)], feats).astype(BF16)
    for head in range(heads):
        query = head_rows_of(qkv, head * rows, rows)
        key = head_rows_of(qkv, chan_local + head * rows, rows)
        value = head_rows_of(qkv, 2 * chan_local + head * rows, rows)
        scores[head] = tn(query, key)
        scores[heads + head] = tn(head_rows_of(cot, head * rows, rows), value)
    for half in range(2):
        span = slice(half * HALO, (half + 1) * HALO)
        index = neighbours[:, span] - (first_atom + (half - 1) * HALO)
        index = jnp.where(index < 0, index + total_atoms, index)
        index = jnp.where(index >= total_atoms, index - total_atoms, index)
        index_rows[:, span] = index
        wide = wide_transpose(index)
        index_wide[span, :] = wide
        for tile in range(3):
            slot_own[half, tile] = slot_tile(wide[:, :slots], tile)


def project_halo(start, chunks, wp, halo_qkv):
    at = 0
    for flm, flo, frm, fro in chunks:
        for comp in range(flm.shape[0]):
            feats = jnp.concatenate(
                [
                    jnp.concatenate([flm[comp], frm[comp]], axis=1),
                    jnp.concatenate([flo[comp], fro[comp]], axis=1),
                ],
                axis=0,
            )
            halo_qkv[at] = nn(wp[degree_of(start + at)], feats).astype(BF16)
            at += 1


def halo_scores(heads, quantity, start, qkv, cot, halo_qkv):
    size, chan_local = halo_qkv.shape[0], cot.shape[1]
    rows = chan_local // heads
    head = quantity % heads
    first = (1 if quantity < heads else 2) * chan_local + head * rows
    source = qkv if quantity < heads else cot
    mine = source[start : start + size, head * rows : (head + 1) * rows, :]
    mine = mine.reshape(size * rows, mine.shape[2])
    theirs = head_rows_of(halo_qkv, first, rows)
    return tn(mine[:, :HALO], theirs[:, :HALO]), tn(mine[:, HALO:], theirs[:, HALO:])


def early_kernel(heads, flm, flo, frm, fro, wp, qkv, cot, halo_qkv, partial, token):
    token[...] = jnp.zeros_like(token)
    project_halo(0, [(flm, flo, frm, fro)], wp, halo_qkv)
    for quantity in range(2 * heads):
        left, right = halo_scores(heads, quantity, 0, qkv, cot, halo_qkv)
        partial[quantity, 0] = left
        partial[quantity, 1] = right


def edge_kernel(heads, score_scale, start, late, *refs):
    chunks = [refs[at : at + 4] for at in range(0, 4 * late, 4)]
    (wp, qkv, cot, scores, partial, bias, valid, index_rows, index_wide,
     halo_qkv, grad_bias, message_a, message_b, token) = refs[4 * late :]
    token[...] = jnp.zeros_like(token)
    slots = valid.shape[0]
    project_halo(start, chunks, wp, halo_qkv)
    lane = lax.broadcasted_iota(jnp.int32, (HALO, 2 * heads * slots), 1)
    gathered = [jnp.zeros((HALO, 2 * heads * slots), F32) for _ in range(2)]
    for quantity in range(2 * heads):
        left, right = halo_scores(heads, quantity, start, qkv, cot, halo_qkv)
        left, right = left + partial[quantity, 0], right + partial[quantity, 1]
        for half in range(2):
            own = scores[quantity, half * HALO : (half + 1) * HALO, :]
            own = [own[:, :HALO], own[:, HALO:]]
            tiles = [left] + own if half == 0 else own + [right]
            index = index_wide[half * HALO : (half + 1) * HALO, :]
            inner, tile_of = index & (HALO - 1), index >> 7
            values = jnp.where(
                tile_of == 0,
                pick(tiles[0], inner),
                jnp.where(tile_of == 1, pick(tiles[1], inner), pick(tiles[2], inner)),
            )
            gathered[half] = jnp.where(lane // slots == quantity, values, gathered[half])
    for half, message in enumerate((message_a, message_b)):
        span = slice(half * HALO, (half + 1) * HALO)
        edges = gathered[half].T.reshape(2, heads, slots, HALO)
        squashed = jnp.tanh(edges[0] * (score_scale / SOFT_CAP))
        logits = SOFT_CAP * squashed + bias[:, :, span]
        live = valid[:, span][None] > 0
        weight = jnp.where(live, jnp.exp(logits), 0.0)
        attention = weight / jnp.sum(weight, axis=1, keepdims=True)
        grad_attn = edges[1]
        grad_logit = attention * (
            grad_attn - jnp.sum(attention * grad_attn, axis=1, keepdims=True)
        )
        grad_bias[:, :, span] = grad_logit
        grad_raw = score_scale * grad_logit * (1.0 - squashed * squashed)
        index = index_rows[:, span]
        both = jnp.stack([grad_raw, attention]).reshape(2 * heads, slots, HALO)
        merged = jnp.zeros_like(both)
        for slot in range(slots):
            same = (index == index[slot : slot + 1, :])[None]
            merged = merged + jnp.where(same, both[:, slot : slot + 1, :], 0.0)
        atom = lax.broadcasted_iota(jnp.int32, (slots, HALO), 1)
        edge_rows = 2 * heads * slots
        message[:edge_rows, :] = merged.reshape(edge_rows, HALO).astype(BF16)
        message[edge_rows:, :] = (index - HALO - atom).astype(F32).astype(BF16)


def joined_rows(early, late, first_row, rows):
    return jnp.concatenate(
        [head_rows_of(early, first_row, rows), head_rows_of(late, first_row, rows)], axis=0
    )


def grads_kernel(heads, slots, pieces, place, fm, fo, *refs):
    chunks = [refs[at : at + 4] for at in range(0, 4 * pieces, 4)]
    (qkv, halo_a, halo_b, cot, slot_own, message_a, message_b, grad_query, own_key, own_value, kept,
     sent_1, sent_2, sent_3, ext, weight_terms) = refs[4 * pieces :]
    places = [(chunk, at) for chunk in chunks for at in range(chunk[0].shape[0])]
    comps, chan_local = fm.shape[0], fm.shape[1]
    rows = chan_local // heads
    atoms = 2 * HALO
    core = place[0]
    empty = jnp.zeros((HALO, HALO), BF16)
    coefs = [message[: 2 * heads * slots, :].astype(F32).T for message in (message_a, message_b)]
    for head in range(heads):
        tables = []
        for quantity in (head, heads + head):
            halves = []
            for half in range(2):
                tiles = [spread(slot_own[half, t], coefs[half], quantity, slots) for t in range(3)]
                tiles = tiles + [empty] if half == 0 else [empty] + tiles
                halves.append(jnp.concatenate(tiles, axis=1))
            tables.append(jnp.concatenate(halves, axis=0))
        raw_table, attn_table = tables
        query = head_rows_of(qkv, head * rows, rows)
        key = head_rows_of(qkv, chan_local + head * rows, rows)
        halo_key = joined_rows(halo_a, halo_b, chan_local + head * rows, rows)
        key_ext = jnp.concatenate([halo_key[:, :HALO], key, halo_key[:, HALO:]], axis=1)
        span = slice(head * rows, (head + 1) * rows)
        value_span = slice(chan_local + head * rows, chan_local + (head + 1) * rows)
        grad_query[:, span, :] = nt(key_ext, raw_table).astype(BF16).reshape(comps, rows, atoms)
        key_sums = nn(query, raw_table)
        own_key[:, span, :] = key_sums[:, HALO : HALO + atoms].reshape(comps, rows, atoms)
        ext[:, span, :] = key_sums.astype(BF16).reshape(comps, rows, atoms + 2 * HALO)
        value_sums = nn(head_rows_of(cot, head * rows, rows), attn_table)
        own_value[:, span, :] = value_sums[:, HALO : HALO + atoms].reshape(comps, rows, atoms)
        ext[:, value_span, :] = value_sums.astype(BF16).reshape(comps, rows, atoms + 2 * HALO)
    for degree in range(LMAX + 1):
        query_total = jnp.zeros((chan_local, 2 * chan_local), F32)
        keyval_total = jnp.zeros((2 * chan_local, 2 * chan_local), F32)
        for comp in range(degree * degree, (degree + 1) * (degree + 1)):
            own = jnp.concatenate([fm[comp], fo[comp]], axis=0)
            (flm, flo, frm, fro), at = places[comp]
            wide = jnp.concatenate(
                [
                    jnp.concatenate([flm[at], fm[comp], frm[at]], axis=1),
                    jnp.concatenate([flo[at], fo[comp], fro[at]], axis=1),
                ],
                axis=0,
            )
            query_total = query_total + nt(grad_query[comp], own)
            keyval_total = keyval_total + nt(ext[comp], wide)
        total = jnp.concatenate([query_total, keyval_total], axis=0)
        total = jnp.where(core == 0, total, pltpu.roll(total, chan_local, 1))
        for g in range(3):
            weight_terms[g * (LMAX + 1) + degree] = total[g * chan_local : (g + 1) * chan_local]
    piece = chan_local // 4
    spot = place[2]
    for delta, part in enumerate((kept, sent_1, sent_2, sent_3)):
        first = pl.multiple_of((spot ^ delta) * piece, piece)
        part[...] = weight_terms[:, pl.ds(first, piece), :].astype(part.dtype)


def halo_slots(message_left, message_right, quantities, slots):
    coefs, tables = [], []
    for message, tile in ((message_left, 2), (message_right, 0)):
        coefs.append(message[: quantities * slots, :].astype(F32).T)
        offset = message[quantities * slots :, :].astype(F32).astype(jnp.int32)
        atom = lax.broadcasted_iota(jnp.int32, offset.shape, 1)
        tables.append(slot_tile(wide_transpose(offset + HALO + atom)[:, :slots], tile))
    return coefs, tables


def final_kernel(heads, slots, start, grad_query, own_key, own_value, halo_qkv, cl, cr,
                 message_left, message_right, wc, mine, theirs, token, grad):
    token[...] = jnp.zeros_like(token)
    comps, chan_local = halo_qkv.shape[0], cl.shape[1]
    rows = chan_local // heads
    stop = start + comps
    grad[:, :chan_local, :] = grad_query[start:stop]
    coefs, tables = halo_slots(message_left, message_right, 2 * heads, slots)
    for head in range(heads):
        span = slice(head * rows, (head + 1) * rows)
        query = head_rows_of(halo_qkv, head * rows, rows)
        sides = (
            (own_key, chan_local, head, (query[:, :HALO], query[:, HALO:])),
            (
                own_value,
                2 * chan_local,
                heads + head,
                tuple(side[start:stop, span, :].reshape(comps * rows, HALO) for side in (cl, cr)),
            ),
        )
        for own, first, quantity, outer in sides:
            rim = [
                nn(outer[at], spread(tables[at], coefs[at], quantity, slots)) for at in range(2)
            ]
            total = own[start:stop, span, :].reshape(comps * rows, 2 * HALO)
            total = total + jnp.concatenate(rim, axis=1)
            grad[:, first + head * rows : first + (head + 1) * rows, :] = (
                total.astype(BF16).reshape(comps, rows, 2 * HALO)
            )
    for comp in range(comps):
        total = nn(wc[degree_of(start + comp)], grad[comp])
        mine[comp] = total[:chan_local]
        theirs[comp] = total[chan_local:].astype(BF16)


def finish_kernel(*refs):
    out, start = refs[-1], 0
    for mine, theirs in zip(refs[:-1:2], refs[1:-1:2]):
        stop = start + mine.shape[0]
        out[start:stop] = (mine[...] + theirs[...].astype(F32)).astype(BF16)
        start = stop


def gather_kernel(place, part_0, part_1, part_2, part_3, out):
    piece = part_0.shape[1]
    spot = place[2]
    for delta, part in enumerate((part_0, part_1, part_2, part_3)):
        first = pl.multiple_of((spot ^ delta) * piece, piece)
        out[:, pl.ds(first, piece), :] = part[...].astype(F32)


def call(kernel, args, outs, scratch=(), scalars=0, limit=24, stay=(), tokens=(), flops=0):
    whole = pl.BlockSpec(memory_space=pltpu.VMEM)
    small = pl.BlockSpec(memory_space=pltpu.SMEM)
    args = [
        pltpu.with_memory_space_constraint(a, pltpu.VMEM) if at in stay else a
        for at, a in enumerate(args)
    ]
    count = len(args)

    def body(*refs):
        kernel(*refs[:count], *refs[count + len(tokens) :])

    return pl.pallas_call(
        body,
        out_shape=tuple(outs),
        in_specs=[small] * scalars
        + [whole] * (count - scalars)
        + [pl.BlockSpec(memory_space=pl.ANY)] * len(tokens),
        out_specs=tuple([whole] * len(outs)),
        scratch_shapes=list(scratch),
        compiler_params=pltpu.CompilerParams(vmem_limit_bytes=limit * 1024 * 1024),
        cost_estimate=pl.CostEstimate(flops=flops, bytes_accessed=1024, transcendentals=0),
    )(*args, *tokens)


def after(values, tokens):
    anywhere = pl.BlockSpec(memory_space=pl.ANY)
    count = len(values)

    def kernel(*refs):
        pass

    return pl.pallas_call(
        kernel,
        out_shape=tuple(jax.ShapeDtypeStruct(v.shape, v.dtype) for v in values),
        in_specs=[anywhere] * (count + len(tokens)),
        out_specs=tuple([anywhere] * count),
        input_output_aliases={i: i for i in range(count)},
        compiler_params=pltpu.CompilerParams(vmem_limit_bytes=1024 * 1024),
        cost_estimate=pl.CostEstimate(flops=0, bytes_accessed=1024, transcendentals=0),
    )(*values, *tokens)


def shifted(value, axis, steps):
    count = lax.axis_size(axis)
    pairs = [(source, (source + steps) % count) for source in range(count)]
    return lax.ppermute(value, axis, pairs)


def exchanged(value, axis, offset):
    count = lax.axis_size(axis)
    return lax.ppermute(value, axis, [(source, source ^ offset) for source in range(count)])


def on_device(features, weights, cotangent, edge_bias, neighbours, valid_mask):
    chan_local, comps, atoms_dev = features.shape
    heads, slots = edge_bias.shape[0], edge_bias.shape[1]
    channels = weights.shape[2]
    assert atoms_dev == 2 * HALO and channels == 2 * chan_local
    score_scale = 1.0 / math.sqrt(chan_local // heads * comps)
    total_atoms = atoms_dev * lax.axis_size("atom")
    count = lax.axis_size("atom")
    assert count >= 4 and count & (count - 1) == 0
    atom_place = lax.axis_index("atom")
    cut_bits = (1, 2) if count >= 8 else (0, 1)
    spot = (atom_place >> cut_bits[0]) & 3
    place = jnp.stack([lax.axis_index("chan"), atom_place * atoms_dev, spot])
    place = place.astype(jnp.int32)
    feature_cut = comps // 2
    feature_cuts = ((0, feature_cut), (feature_cut, comps))

    def held(*dims, dtype=F32):
        return pltpu.VMEM(dims, dtype)

    def plain(*dims, dtype=F32):
        return jax.ShapeDtypeStruct(dims, dtype)

    fm = jnp.transpose(features, (1, 0, 2))
    cot = jnp.transpose(cotangent, (1, 0, 2))
    mix = jnp.transpose(weights, (0, 1, 3, 2))
    anywhere = pl.BlockSpec(memory_space=pl.ANY)
    pieces = 6
    feature_rims = []
    for start, stop in feature_cuts:
        feature_rims += pl.pallas_call(
            functools.partial(split_kernel, start, pieces),
            out_shape=(held(stop - start, chan_local, HALO, dtype=BF16),) * 2,
            in_specs=[anywhere],
            out_specs=(pl.BlockSpec(memory_space=pltpu.VMEM),) * 2,
            scratch_shapes=[pltpu.SemaphoreType.DMA((2, pieces))],
            compiler_params=pltpu.CompilerParams(vmem_limit_bytes=4 * 1024 * 1024),
            cost_estimate=pl.CostEstimate(flops=0, bytes_accessed=1024, transcendentals=0),
        )(pltpu.with_memory_space_constraint(fm, pltpu.HBM))
    from_sides = [
        shifted(rim, "atom", 1 if at % 2 == 0 else -1) for at, rim in enumerate(feature_rims)
    ]
    fo = shifted(fm, "chan", 1)

    qkv, scores, slot_own, index_rows, index_wide, wp, wc, token, *rims = call(
        functools.partial(own_kernel, heads, total_atoms),
        (place, fm, fo, cot, mix, neighbours),
        (
            held(comps, 3 * chan_local, atoms_dev, dtype=BF16),
            held(2 * heads, atoms_dev, atoms_dev),
            held(2, 3, HALO, HALO, dtype=jnp.int32),
            held(slots, atoms_dev, dtype=jnp.int32),
            held(atoms_dev, HALO, dtype=jnp.int32),
            held(LMAX + 1, 3 * chan_local, channels, dtype=BF16),
            held(LMAX + 1, channels, 3 * chan_local, dtype=BF16),
            plain(8, HALO),
            *(
                plain(comps, chan_local, HALO, dtype=BF16) for _ in range(2)
            ),
        ),
        scalars=1,
        stay=(1, 2, 3),
        flops=12 * 10**9,
    )
    flm, frm = after(from_sides[:2], (token,))
    early_chunk = (flm, shifted(flm, "chan", 1), frm, shifted(frm, "chan", 1))
    halo_a, partial, token = call(
        functools.partial(early_kernel, heads),
        (*early_chunk, wp, qkv, cot),
        (
            held(feature_cut, 3 * chan_local, atoms_dev, dtype=BF16),
            held(2 * heads, 2, HALO, HALO),
            plain(8, HALO),
        ),
        stay=tuple(range(7)),
    )
    (rims[0],) = after(rims[:1], (token,))
    from_left = shifted(rims[0], "atom", 1)
    late_sides = after(from_sides[2:], (token,))
    late_chunks = []
    for flm, frm in zip(late_sides[::2], late_sides[1::2]):
        late_chunks += [flm, shifted(flm, "chan", 1), frm, shifted(frm, "chan", 1)]
    halo_b, grad_bias, message_a, message_b, token = call(
        functools.partial(edge_kernel, heads, score_scale, feature_cut, len(late_chunks) // 4),
        (*late_chunks, wp, qkv, cot, scores, partial, edge_bias, valid_mask, index_rows, index_wide),
        (
            held(comps - feature_cut, 3 * chan_local, atoms_dev, dtype=BF16),
            plain(heads, slots, atoms_dev),
            held((2 * heads + 1) * slots, HALO, dtype=BF16),
            held((2 * heads + 1) * slots, HALO, dtype=BF16),
            plain(8, HALO),
        ),
        stay=(*range(len(late_chunks) + 5), len(late_chunks) + 7, len(late_chunks) + 8),
    )
    (rims[1],) = after(rims[1:], (token,))
    from_right = shifted(rims[1], "atom", -1)
    message_left = shifted(message_b, "atom", 1)
    message_right = shifted(message_a, "atom", -1)
    piece = (3 * (LMAX + 1), chan_local // 4, channels)
    grad_query, own_key, own_value, kept, *sent = call(
        functools.partial(grads_kernel, heads, slots, len(feature_cuts)),
        (place, fm, fo, *early_chunk, *late_chunks, qkv, halo_a, halo_b, cot, slot_own, message_a,
         message_b),
        (
            held(comps, chan_local, atoms_dev, dtype=BF16),
            held(comps, chan_local, atoms_dev),
            held(comps, chan_local, atoms_dev),
            held(*piece),
            plain(*piece, dtype=BF16),
            plain(*piece, dtype=BF16),
            plain(*piece, dtype=BF16),
        ),
        scratch=[
            pltpu.VMEM((comps, 2 * chan_local, 2 * atoms_dev), BF16),
            pltpu.VMEM((3 * (LMAX + 1), chan_local, channels), F32),
        ],
        scalars=1,
        stay=tuple(range(1, 10 + 4 * len(feature_cuts))),
    )
    for delta, part in enumerate(sent, 1):
        kept = kept + exchanged(part, "atom", delta << cut_bits[0]).astype(F32)
    rest = [bit for bit in reversed(range(count.bit_length() - 1)) if bit not in cut_bits]
    for bit in rest[:-1]:
        kept = kept + exchanged(kept.astype(BF16), "atom", 1 << bit).astype(F32)
    rounded = kept.astype(BF16)
    last = exchanged(rounded, "atom", 1 << rest[-1])
    parts, tokens = [], (rounded,)
    for (start, stop), halo_qkv in zip(feature_cuts, (halo_a, halo_b)):
        size = stop - start
        mine, theirs, token = call(
            functools.partial(final_kernel, heads, slots, start),
            (grad_query, own_key, own_value, halo_qkv, from_left, from_right, message_left,
             message_right, wc),
            (
                held(size, chan_local, atoms_dev),
                held(size, chan_local, atoms_dev, dtype=BF16),
                plain(8, HALO),
            ),
            scratch=[pltpu.VMEM((size, 3 * chan_local, atoms_dev), BF16)],
            limit=16,
            stay=(0, 1, 2, 3, 4, 5, 8),
            tokens=tokens,
        )
        parts += [mine, shifted(theirs, "chan", 1)]
        tokens = (token, last)
    (last,) = after((last,), (token,))
    rounded = (kept + last.astype(F32)).astype(BF16)
    pieces = [rounded] + [exchanged(rounded, "atom", d << cut_bits[0]) for d in range(1, 4)]
    (grad_weights,) = call(
        gather_kernel,
        (place, *pieces),
        (plain(3 * (LMAX + 1), chan_local, channels),),
        scalars=1,
        limit=8,
    )
    (out,) = call(
        finish_kernel,
        parts,
        (plain(comps, chan_local, atoms_dev, dtype=BF16),),
        limit=8,
        stay=tuple(range(len(parts))),
    )
    grad_features = jnp.transpose(out, (1, 0, 2))
    grad_weights = grad_weights.reshape(3, LMAX + 1, chan_local, channels)
    grad_weights = jnp.transpose(grad_weights, (0, 1, 3, 2))
    return grad_features, grad_weights, grad_bias


def solution(mesh):
    in_specs = (
        P("chan", None, "atom"),
        P(None, None, None, "chan"),
        P("chan", None, "atom"),
        P("chan", None, "atom"),
        P(None, "atom"),
        P(None, "atom"),
    )
    out_specs = (P("chan", None, "atom"), P(None, None, None, "chan"), P("chan", None, "atom"))
    return jax.shard_map(
        on_device, mesh=mesh, in_specs=in_specs, out_specs=out_specs, check_vma=False
    )
```

```python
import functools
import math

import jax
import jax.numpy as jnp
from jax import lax
from jax.experimental import pallas as pl
from jax.experimental.pallas import tpu as pltpu
from jax.sharding import PartitionSpec as P

LMAX = 6
HALO = 128
SOFT_CAP = 10.0
F32 = jnp.float32
BF16 = jnp.bfloat16


def degree_of(comp):
    return math.isqrt(comp)


def nn(lhs, rhs):
    return lax.dot_general(lhs, rhs, (((1,), (0,)), ((), ())), preferred_element_type=F32)


def nt(lhs, rhs):
    return lax.dot_general(lhs, rhs, (((1,), (1,)), ((), ())), preferred_element_type=F32)


def tn(lhs, rhs):
    return lax.dot_general(lhs, rhs, (((0,), (0,)), ((), ())), preferred_element_type=F32)


def pick(table, index):
    return jnp.take_along_axis(table, index, axis=1, mode="promise_in_bounds")


def head_rows_of(ref, first_row, rows):
    block = ref[:, first_row : first_row + rows, :]
    return block.reshape(block.shape[0] * rows, block.shape[2])


def slot_tile(window_index, tile):
    atoms, slots = window_index.shape
    lane = lax.broadcasted_iota(jnp.int32, (atoms, HALO), 1) + tile * HALO
    found = jnp.full((atoms, HALO), -1, jnp.int32)
    for slot in range(slots):
        found = jnp.where(window_index[:, slot : slot + 1] == lane, slot, found)
    return found


def spread(slot, coef, quantity, slots):
    values = pick(coef, jnp.maximum(slot, 0) + quantity * slots)
    return jnp.where(slot >= 0, values, 0.0).astype(BF16)


def wide_transpose(rows):
    return jnp.concatenate([rows] * (HALO // rows.shape[0]), axis=0).T


def split_kernel(cuts, fm, *refs):
    *parts, sems = refs
    copies = []
    for at, part in enumerate(parts):
        start, stop = cuts[at // 2]
        atom = HALO if at % 2 == 0 else 0
        copies.append(
            pltpu.make_async_copy(
                fm.at[pl.ds(start, stop - start), :, pl.ds(atom, HALO)], part, sems.at[at]
            )
        )
    for copy in copies:
        copy.start()
    for copy in copies:
        copy.wait()


def own_kernel(heads, total_atoms, place, fm, fo, cot, weights, neighbours,
               qkv, scores, slot_own, index_rows, index_wide, wp, wc, token, *rims):
    token[...] = jnp.zeros_like(token)
    rims[0][...] = cot[:, :, HALO:]
    rims[1][...] = cot[:, :, :HALO]
    comps, chan_local = fm.shape[0], fm.shape[1]
    channels = weights.shape[3]
    rows = chan_local // heads
    slots = neighbours.shape[0]
    core, first_atom = place[0], place[1]
    for degree in range(LMAX + 1):
        mix = jnp.concatenate([weights[g, degree] for g in range(3)], axis=0).astype(F32)
        mix = jnp.where(core == 0, mix, pltpu.roll(mix, chan_local, 1))
        wp[degree] = mix.astype(BF16)
        padded = jnp.concatenate([mix, jnp.zeros((chan_local, channels), F32)], axis=0)
        wc[degree] = padded.T[:, : 3 * chan_local].astype(BF16)
    for comp in range(comps):
        feats = jnp.concatenate([fm[comp], fo[comp]], axis=0)
        qkv[comp] = nn(wp[degree_of(comp)], feats).astype(BF16)
    for head in range(heads):
        query = head_rows_of(qkv, head * rows, rows)
        key = head_rows_of(qkv, chan_local + head * rows, rows)
        value = head_rows_of(qkv, 2 * chan_local + head * rows, rows)
        scores[head] = tn(query, key)
        scores[heads + head] = tn(head_rows_of(cot, head * rows, rows), value)
    for half in range(2):
        span = slice(half * HALO, (half + 1) * HALO)
        index = neighbours[:, span] - (first_atom + (half - 1) * HALO)
        index = jnp.where(index < 0, index + total_atoms, index)
        index = jnp.where(index >= total_atoms, index - total_atoms, index)
        index_rows[:, span] = index
        wide = wide_transpose(index)
        index_wide[span, :] = wide
        for tile in range(3):
            slot_own[half, tile] = slot_tile(wide[:, :slots], tile)


def project_halo(start, chunks, wp, halo_qkv):
    at = 0
    for flm, flo, frm, fro in chunks:
        for comp in range(flm.shape[0]):
            feats = jnp.concatenate(
                [
                    jnp.concatenate([flm[comp], frm[comp]], axis=1),
                    jnp.concatenate([flo[comp], fro[comp]], axis=1),
                ],
                axis=0,
            )
            halo_qkv[at] = nn(wp[degree_of(start + at)], feats).astype(BF16)
            at += 1


def halo_scores(heads, quantity, start, qkv, cot, halo_qkv):
    size, chan_local = halo_qkv.shape[0], cot.shape[1]
    rows = chan_local // heads
    head = quantity % heads
    first = (1 if quantity < heads else 2) * chan_local + head * rows
    source = qkv if quantity < heads else cot
    mine = source[start : start + size, head * rows : (head + 1) * rows, :]
    mine = mine.reshape(size * rows, mine.shape[2])
    theirs = head_rows_of(halo_qkv, first, rows)
    return tn(mine[:, :HALO], theirs[:, :HALO]), tn(mine[:, HALO:], theirs[:, HALO:])


def early_kernel(heads, flm, flo, frm, fro, wp, qkv, cot, halo_qkv, partial, token):
    token[...] = jnp.zeros_like(token)
    project_halo(0, [(flm, flo, frm, fro)], wp, halo_qkv)
    for quantity in range(2 * heads):
        left, right = halo_scores(heads, quantity, 0, qkv, cot, halo_qkv)
        partial[quantity, 0] = left
        partial[quantity, 1] = right


def edge_kernel(heads, score_scale, start, late, *refs):
    chunks = [refs[at : at + 4] for at in range(0, 4 * late, 4)]
    (wp, qkv, cot, scores, partial, bias, valid, index_rows, index_wide,
     halo_qkv, grad_bias, message_a, message_b) = refs[4 * late :]
    slots = valid.shape[0]
    project_halo(start, chunks, wp, halo_qkv)
    lane = lax.broadcasted_iota(jnp.int32, (HALO, 2 * heads * slots), 1)
    gathered = [jnp.zeros((HALO, 2 * heads * slots), F32) for _ in range(2)]
    for quantity in range(2 * heads):
        left, right = halo_scores(heads, quantity, start, qkv, cot, halo_qkv)
        left, right = left + partial[quantity, 0], right + partial[quantity, 1]
        for half in range(2):
            own = scores[quantity, half * HALO : (half + 1) * HALO, :]
            own = [own[:, :HALO], own[:, HALO:]]
            tiles = [left] + own if half == 0 else own + [right]
            index = index_wide[half * HALO : (half + 1) * HALO, :]
            inner, tile_of = index & (HALO - 1), index >> 7
            values = jnp.where(
                tile_of == 0,
                pick(tiles[0], inner),
                jnp.where(tile_of == 1, pick(tiles[1], inner), pick(tiles[2], inner)),
            )
            gathered[half] = jnp.where(lane // slots == quantity, values, gathered[half])
    for half, message in enumerate((message_a, message_b)):
        span = slice(half * HALO, (half + 1) * HALO)
        edges = gathered[half].T.reshape(2, heads, slots, HALO)
        squashed = jnp.tanh(edges[0] * (score_scale / SOFT_CAP))
        logits = SOFT_CAP * squashed + bias[:, :, span]
        live = valid[:, span][None] > 0
        weight = jnp.where(live, jnp.exp(logits), 0.0)
        attention = weight / jnp.sum(weight, axis=1, keepdims=True)
        grad_attn = edges[1]
        grad_logit = attention * (
            grad_attn - jnp.sum(attention * grad_attn, axis=1, keepdims=True)
        )
        grad_bias[:, :, span] = grad_logit
        grad_raw = score_scale * grad_logit * (1.0 - squashed * squashed)
        index = index_rows[:, span]
        both = jnp.stack([grad_raw, attention]).reshape(2 * heads, slots, HALO)
        merged = jnp.zeros_like(both)
        for slot in range(slots):
            same = (index == index[slot : slot + 1, :])[None]
            merged = merged + jnp.where(same, both[:, slot : slot + 1, :], 0.0)
        atom = lax.broadcasted_iota(jnp.int32, (slots, HALO), 1)
        edge_rows = 2 * heads * slots
        message[:edge_rows, :] = merged.reshape(edge_rows, HALO).astype(BF16)
        message[edge_rows:, :] = (index - HALO - atom).astype(F32).astype(BF16)


def joined_rows(early, late, first_row, rows):
    return jnp.concatenate(
        [head_rows_of(early, first_row, rows), head_rows_of(late, first_row, rows)], axis=0
    )


def grads_kernel(heads, slots, pieces, place, fm, fo, *refs):
    chunks = [refs[at : at + 4] for at in range(0, 4 * pieces, 4)]
    (qkv, halo_a, halo_b, cot, slot_own, message_a, message_b, grad_query, own_key, own_value, kept,
     sent_1, sent_2, sent_3, ext, weight_terms) = refs[4 * pieces :]
    places = [(chunk, at) for chunk in chunks for at in range(chunk[0].shape[0])]
    comps, chan_local = fm.shape[0], fm.shape[1]
    rows = chan_local // heads
    atoms = 2 * HALO
    core = place[0]
    empty = jnp.zeros((HALO, HALO), BF16)
    coefs = [message[: 2 * heads * slots, :].astype(F32).T for message in (message_a, message_b)]
    for head in range(heads):
        tables = []
        for quantity in (head, heads + head):
            halves = []
            for half in range(2):
                tiles = [spread(slot_own[half, t], coefs[half], quantity, slots) for t in range(3)]
                tiles = tiles + [empty] if half == 0 else [empty] + tiles
                halves.append(jnp.concatenate(tiles, axis=1))
            tables.append(jnp.concatenate(halves, axis=0))
        raw_table, attn_table = tables
        query = head_rows_of(qkv, head * rows, rows)
        key = head_rows_of(qkv, chan_local + head * rows, rows)
        halo_key = joined_rows(halo_a, halo_b, chan_local + head * rows, rows)
        key_ext = jnp.concatenate([halo_key[:, :HALO], key, halo_key[:, HALO:]], axis=1)
        span = slice(head * rows, (head + 1) * rows)
        value_span = slice(chan_local + head * rows, chan_local + (head + 1) * rows)
        grad_query[:, span, :] = nt(key_ext, raw_table).astype(BF16).reshape(comps, rows, atoms)
        key_sums = nn(query, raw_table)
        own_key[:, span, :] = key_sums[:, HALO : HALO + atoms].reshape(comps, rows, atoms)
        ext[:, span, :] = key_sums.astype(BF16).reshape(comps, rows, atoms + 2 * HALO)
        value_sums = nn(head_rows_of(cot, head * rows, rows), attn_table)
        own_value[:, span, :] = value_sums[:, HALO : HALO + atoms].reshape(comps, rows, atoms)
        ext[:, value_span, :] = value_sums.astype(BF16).reshape(comps, rows, atoms + 2 * HALO)
    for degree in range(LMAX + 1):
        query_total = jnp.zeros((chan_local, 2 * chan_local), F32)
        keyval_total = jnp.zeros((2 * chan_local, 2 * chan_local), F32)
        for comp in range(degree * degree, (degree + 1) * (degree + 1)):
            own = jnp.concatenate([fm[comp], fo[comp]], axis=0)
            (flm, flo, frm, fro), at = places[comp]
            wide = jnp.concatenate(
                [
                    jnp.concatenate([flm[at], fm[comp], frm[at]], axis=1),
                    jnp.concatenate([flo[at], fo[comp], fro[at]], axis=1),
                ],
                axis=0,
            )
            query_total = query_total + nt(grad_query[comp], own)
            keyval_total = keyval_total + nt(ext[comp], wide)
        total = jnp.concatenate([query_total, keyval_total], axis=0)
        total = jnp.where(core == 0, total, pltpu.roll(total, chan_local, 1))
        for g in range(3):
            weight_terms[g * (LMAX + 1) + degree] = total[g * chan_local : (g + 1) * chan_local]
    piece = chan_local // 4
    spot = place[2]
    for delta, part in enumerate((kept, sent_1, sent_2, sent_3)):
        first = pl.multiple_of((spot ^ delta) * piece, piece)
        part[...] = weight_terms[:, pl.ds(first, piece), :].astype(part.dtype)


def halo_slots(message_left, message_right, quantities, slots):
    coefs, tables = [], []
    for message, tile in ((message_left, 2), (message_right, 0)):
        coefs.append(message[: quantities * slots, :].astype(F32).T)
        offset = message[quantities * slots :, :].astype(F32).astype(jnp.int32)
        atom = lax.broadcasted_iota(jnp.int32, offset.shape, 1)
        tables.append(slot_tile(wide_transpose(offset + HALO + atom)[:, :slots], tile))
    return coefs, tables


def key_kernel(heads, slots, grad_query, own_key, halo_a, halo_b, message_left, message_right, wc,
               terms, token, grad):
    token[...] = jnp.zeros_like(token)
    comps, chan_local = grad_query.shape[0], grad_query.shape[1]
    rows = chan_local // heads
    grad[:, :chan_local, :] = grad_query[...]
    coefs, tables = halo_slots(message_left, message_right, 2 * heads, slots)
    for head in range(heads):
        query = joined_rows(halo_a, halo_b, head * rows, rows)
        rim = jnp.concatenate(
            [
                nn(query[:, :HALO], spread(tables[0], coefs[0], head, slots)),
                nn(query[:, HALO:], spread(tables[1], coefs[1], head, slots)),
            ],
            axis=1,
        )
        total = head_rows_of(own_key, head * rows, rows) + rim
        span = slice(chan_local + head * rows, chan_local + (head + 1) * rows)
        grad[:, span, :] = total.astype(BF16).reshape(comps, rows, 2 * HALO)
    for comp in range(comps):
        terms[comp] = nn(wc[degree_of(comp)][:, : 2 * chan_local], grad[comp])


def value_kernel(heads, slots, start, stop, own_value, cl, cr, message_left, message_right, wc, terms,
                 mine, theirs, grad):
    comps, chan_local = stop - start, cl.shape[1]
    rows = chan_local // heads
    coefs, tables = halo_slots(message_left, message_right, 2 * heads, slots)
    for head in range(heads):
        span = slice(head * rows, (head + 1) * rows)
        rim = jnp.concatenate(
            [
                nn(cl[start:stop, span, :].reshape(comps * rows, HALO),
                   spread(tables[0], coefs[0], heads + head, slots)),
                nn(cr[start:stop, span, :].reshape(comps * rows, HALO),
                   spread(tables[1], coefs[1], heads + head, slots)),
            ],
            axis=1,
        )
        own = own_value[start:stop, span, :].reshape(comps * rows, 2 * HALO)
        grad[:, span, :] = (own + rim).astype(BF16).reshape(comps, rows, 2 * HALO)
    for comp in range(comps):
        mix = wc[degree_of(start + comp)][:, 2 * chan_local :]
        total = terms[start + comp] + nn(mix, grad[comp])
        mine[comp] = total[:chan_local]
        theirs[comp] = total[chan_local:].astype(BF16)


def finish_kernel(*refs):
    out, start = refs[-1], 0
    for mine, theirs in zip(refs[:-1:2], refs[1:-1:2]):
        stop = start + mine.shape[0]
        out[start:stop] = (mine[...] + theirs[...].astype(F32)).astype(BF16)
        start = stop


def gather_kernel(place, part_0, part_1, part_2, part_3, out):
    piece = part_0.shape[1]
    spot = place[2]
    for delta, part in enumerate((part_0, part_1, part_2, part_3)):
        first = pl.multiple_of((spot ^ delta) * piece, piece)
        out[:, pl.ds(first, piece), :] = part[...].astype(F32)


def call(kernel, args, outs, scratch=(), scalars=0, limit=24, stay=(), tokens=(), flops=0):
    whole = pl.BlockSpec(memory_space=pltpu.VMEM)
    small = pl.BlockSpec(memory_space=pltpu.SMEM)
    args = [
        pltpu.with_memory_space_constraint(a, pltpu.VMEM) if at in stay else a
        for at, a in enumerate(args)
    ]
    count = len(args)

    def body(*refs):
        kernel(*refs[:count], *refs[count + len(tokens) :])

    return pl.pallas_call(
        body,
        out_shape=tuple(outs),
        in_specs=[small] * scalars
        + [whole] * (count - scalars)
        + [pl.BlockSpec(memory_space=pl.ANY)] * len(tokens),
        out_specs=tuple([whole] * len(outs)),
        scratch_shapes=list(scratch),
        compiler_params=pltpu.CompilerParams(vmem_limit_bytes=limit * 1024 * 1024),
        cost_estimate=pl.CostEstimate(flops=flops, bytes_accessed=1024, transcendentals=0),
    )(*args, *tokens)


def after(values, tokens):
    anywhere = pl.BlockSpec(memory_space=pl.ANY)
    count = len(values)

    def kernel(*refs):
        pass

    return pl.pallas_call(
        kernel,
        out_shape=tuple(jax.ShapeDtypeStruct(v.shape, v.dtype) for v in values),
        in_specs=[anywhere] * (count + len(tokens)),
        out_specs=tuple([anywhere] * count),
        input_output_aliases={i: i for i in range(count)},
        compiler_params=pltpu.CompilerParams(vmem_limit_bytes=1024 * 1024),
        cost_estimate=pl.CostEstimate(flops=0, bytes_accessed=1024, transcendentals=0),
    )(*values, *tokens)


def shifted(value, axis, steps):
    count = lax.axis_size(axis)
    pairs = [(source, (source + steps) % count) for source in range(count)]
    return lax.ppermute(value, axis, pairs)


def exchanged(value, axis, offset):
    count = lax.axis_size(axis)
    return lax.ppermute(value, axis, [(source, source ^ offset) for source in range(count)])


def on_device(features, weights, cotangent, edge_bias, neighbours, valid_mask):
    chan_local, comps, atoms_dev = features.shape
    heads, slots = edge_bias.shape[0], edge_bias.shape[1]
    channels = weights.shape[2]
    assert atoms_dev == 2 * HALO and channels == 2 * chan_local
    score_scale = 1.0 / math.sqrt(chan_local // heads * comps)
    total_atoms = atoms_dev * lax.axis_size("atom")
    count = lax.axis_size("atom")
    assert count >= 4 and count & (count - 1) == 0
    atom_place = lax.axis_index("atom")
    cut_bits = (1, 2) if count >= 8 else (0, 1)
    spot = (atom_place >> cut_bits[0]) & 3
    place = jnp.stack([lax.axis_index("chan"), atom_place * atoms_dev, spot])
    place = place.astype(jnp.int32)
    feature_cut = comps // 2
    feature_cuts = ((0, feature_cut), (feature_cut, comps))

    def held(*dims, dtype=F32):
        return pltpu.VMEM(dims, dtype)

    def plain(*dims, dtype=F32):
        return jax.ShapeDtypeStruct(dims, dtype)

    fm = jnp.transpose(features, (1, 0, 2))
    cot = jnp.transpose(cotangent, (1, 0, 2))
    mix = jnp.transpose(weights, (0, 1, 3, 2))
    anywhere = pl.BlockSpec(memory_space=pl.ANY)
    rim_count = 2 * len(feature_cuts)
    feature_rims = pl.pallas_call(
        functools.partial(split_kernel, feature_cuts),
        out_shape=tuple(
            held(stop - start, chan_local, HALO, dtype=BF16)
            for start, stop in feature_cuts
            for _ in range(2)
        ),
        in_specs=[anywhere],
        out_specs=(pl.BlockSpec(memory_space=pltpu.VMEM),) * rim_count,
        scratch_shapes=[pltpu.SemaphoreType.DMA((rim_count,))],
        compiler_params=pltpu.CompilerParams(vmem_limit_bytes=4 * 1024 * 1024),
    )(pltpu.with_memory_space_constraint(fm, pltpu.HBM))
    from_sides = [
        shifted(rim, "atom", 1 if at % 2 == 0 else -1) for at, rim in enumerate(feature_rims)
    ]
    fo = shifted(fm, "chan", 1)

    qkv, scores, slot_own, index_rows, index_wide, wp, wc, token, *rims = call(
        functools.partial(own_kernel, heads, total_atoms),
        (place, fm, fo, cot, mix, neighbours),
        (
            held(comps, 3 * chan_local, atoms_dev, dtype=BF16),
            held(2 * heads, atoms_dev, atoms_dev),
            held(2, 3, HALO, HALO, dtype=jnp.int32),
            held(slots, atoms_dev, dtype=jnp.int32),
            held(atoms_dev, HALO, dtype=jnp.int32),
            held(LMAX + 1, 3 * chan_local, channels, dtype=BF16),
            held(LMAX + 1, channels, 3 * chan_local, dtype=BF16),
            plain(8, HALO),
            *(
                plain(comps, chan_local, HALO, dtype=BF16) for _ in range(2)
            ),
        ),
        scalars=1,
        stay=(1, 2, 3),
        flops=12 * 10**9,
    )
    flm, frm = after(from_sides[:2], (token,))
    early_chunk = (flm, shifted(flm, "chan", 1), frm, shifted(frm, "chan", 1))
    halo_a, partial, token = call(
        functools.partial(early_kernel, heads),
        (*early_chunk, wp, qkv, cot),
        (
            held(feature_cut, 3 * chan_local, atoms_dev, dtype=BF16),
            held(2 * heads, 2, HALO, HALO),
            plain(8, HALO),
        ),
        stay=tuple(range(7)),
    )
    rims = after(rims, (token,))
    late_sides = after(from_sides[2:], (token,))
    late_chunks = []
    for flm, frm in zip(late_sides[::2], late_sides[1::2]):
        late_chunks += [flm, shifted(flm, "chan", 1), frm, shifted(frm, "chan", 1)]
    from_left, from_right = shifted(rims[0], "atom", 1), shifted(rims[1], "atom", -1)
    halo_b, grad_bias, message_a, message_b = call(
        functools.partial(edge_kernel, heads, score_scale, feature_cut, len(late_chunks) // 4),
        (*late_chunks, wp, qkv, cot, scores, partial, edge_bias, valid_mask, index_rows, index_wide),
        (
            held(comps - feature_cut, 3 * chan_local, atoms_dev, dtype=BF16),
            plain(heads, slots, atoms_dev),
            held((2 * heads + 1) * slots, HALO, dtype=BF16),
            held((2 * heads + 1) * slots, HALO, dtype=BF16),
        ),
        stay=(*range(len(late_chunks) + 5), len(late_chunks) + 7, len(late_chunks) + 8),
    )
    message_left = shifted(message_b, "atom", 1)
    message_right = shifted(message_a, "atom", -1)
    piece = (3 * (LMAX + 1), chan_local // 4, channels)
    grad_query, own_key, own_value, kept, *sent = call(
        functools.partial(grads_kernel, heads, slots, len(feature_cuts)),
        (place, fm, fo, *early_chunk, *late_chunks, qkv, halo_a, halo_b, cot, slot_own, message_a,
         message_b),
        (
            held(comps, chan_local, atoms_dev, dtype=BF16),
            held(comps, chan_local, atoms_dev),
            held(comps, chan_local, atoms_dev),
            held(*piece),
            plain(*piece, dtype=BF16),
            plain(*piece, dtype=BF16),
            plain(*piece, dtype=BF16),
        ),
        scratch=[
            pltpu.VMEM((comps, 2 * chan_local, 2 * atoms_dev), BF16),
            pltpu.VMEM((3 * (LMAX + 1), chan_local, channels), F32),
        ],
        scalars=1,
        stay=tuple(range(1, 10 + 4 * len(feature_cuts))),
    )
    message_left, message_right, *sent = after((message_left, message_right, *sent), ())
    terms, token = call(
        functools.partial(key_kernel, heads, slots),
        (grad_query, own_key, halo_a, halo_b, message_left, message_right, wc),
        (held(comps, channels, atoms_dev), plain(8, HALO)),
        scratch=[pltpu.VMEM((comps, 2 * chan_local, atoms_dev), BF16)],
        limit=16,
        stay=(0, 1, 2, 3, 6),
    )
    for delta, part in enumerate(sent, 1):
        kept = kept + exchanged(part, "atom", delta << cut_bits[0]).astype(F32)
    rest = [bit for bit in reversed(range(count.bit_length() - 1)) if bit not in cut_bits]
    for bit in rest[:-1]:
        kept = kept + exchanged(kept.astype(BF16), "atom", 1 << bit).astype(F32)
    (rounded,) = after((kept.astype(BF16),), (token,))
    last = exchanged(rounded, "atom", 1 << rest[-1])
    parts = []
    for start, stop in feature_cuts:
        size = stop - start
        mine, theirs = call(
            functools.partial(value_kernel, heads, slots, start, stop),
            (own_value, from_left, from_right, message_left, message_right, wc, terms),
            (
                held(size, chan_local, atoms_dev),
                held(size, chan_local, atoms_dev, dtype=BF16),
            ),
            scratch=[pltpu.VMEM((size, chan_local, atoms_dev), BF16)],
            limit=16,
            stay=(0, 1, 2, 5, 6),
            tokens=(last,) if parts else (rounded,),
        )
        parts += [mine, shifted(theirs, "chan", 1)]
    rounded = (kept + last.astype(F32)).astype(BF16)
    pieces = [rounded] + [exchanged(rounded, "atom", d << cut_bits[0]) for d in range(1, 4)]
    (grad_weights,) = call(
        gather_kernel,
        (place, *pieces),
        (plain(3 * (LMAX + 1), chan_local, channels),),
        scalars=1,
        limit=8,
    )
    (out,) = call(
        finish_kernel,
        parts,
        (plain(comps, chan_local, atoms_dev, dtype=BF16),),
        limit=8,
        stay=tuple(range(len(parts))),
    )
    grad_features = jnp.transpose(out, (1, 0, 2))
    grad_weights = grad_weights.reshape(3, LMAX + 1, chan_local, channels)
    grad_weights = jnp.transpose(grad_weights, (0, 1, 3, 2))
    return grad_features, grad_weights, grad_bias


def solution(mesh):
    in_specs = (
        P("chan", None, "atom"),
        P(None, None, None, "chan"),
        P("chan", None, "atom"),
        P("chan", None, "atom"),
        P(None, "atom"),
        P(None, "atom"),
    )
    out_specs = (P("chan", None, "atom"), P(None, None, None, "chan"), P("chan", None, "atom"))
    return jax.shard_map(
        on_device, mesh=mesh, in_specs=in_specs, out_specs=out_specs, check_vma=False
    )
```

```python
import functools
import math

import jax
import jax.numpy as jnp
from jax import lax
from jax.experimental import pallas as pl
from jax.experimental.pallas import tpu as pltpu
from jax.sharding import PartitionSpec as P

LMAX = 6
HALO = 128
SOFT_CAP = 10.0
F32 = jnp.float32
BF16 = jnp.bfloat16


def degree_of(comp):
    return math.isqrt(comp)


def nn(lhs, rhs):
    return lax.dot_general(lhs, rhs, (((1,), (0,)), ((), ())), preferred_element_type=F32)


def nt(lhs, rhs):
    return lax.dot_general(lhs, rhs, (((1,), (1,)), ((), ())), preferred_element_type=F32)


def tn(lhs, rhs):
    return lax.dot_general(lhs, rhs, (((0,), (0,)), ((), ())), preferred_element_type=F32)


def pick(table, index):
    return jnp.take_along_axis(table, index, axis=1, mode="promise_in_bounds")


def head_rows_of(ref, first_row, rows):
    block = ref[:, first_row : first_row + rows, :]
    return block.reshape(block.shape[0] * rows, block.shape[2])


def slot_tile(window_index, tile):
    atoms, slots = window_index.shape
    lane = lax.broadcasted_iota(jnp.int32, (atoms, HALO), 1) + tile * HALO
    found = jnp.full((atoms, HALO), -1, jnp.int32)
    for slot in range(slots):
        found = jnp.where(window_index[:, slot : slot + 1] == lane, slot, found)
    return found


def spread(slot, coef, quantity, slots):
    values = pick(coef, jnp.maximum(slot, 0) + quantity * slots)
    return jnp.where(slot >= 0, values, 0.0).astype(BF16)


def wide_transpose(rows):
    return jnp.concatenate([rows] * (HALO // rows.shape[0]), axis=0).T


def split_kernel(cuts, fm, *refs):
    *parts, sems = refs
    copies = []
    for at, part in enumerate(parts):
        start, stop = cuts[at // 2]
        atom = HALO if at % 2 == 0 else 0
        copies.append(
            pltpu.make_async_copy(
                fm.at[pl.ds(start, stop - start), :, pl.ds(atom, HALO)], part, sems.at[at]
            )
        )
    for copy in copies:
        copy.start()
    for copy in copies:
        copy.wait()


def own_kernel(heads, total_atoms, place, fm, fo, cot, weights, neighbours,
               qkv, scores, slot_own, index_rows, index_wide, wp, wc, token, *rims):
    token[...] = jnp.zeros_like(token)
    rims[0][...] = cot[:, :, HALO:]
    rims[1][...] = cot[:, :, :HALO]
    comps, chan_local = fm.shape[0], fm.shape[1]
    channels = weights.shape[3]
    rows = chan_local // heads
    slots = neighbours.shape[0]
    core, first_atom = place[0], place[1]
    for degree in range(LMAX + 1):
        mix = jnp.concatenate([weights[g, degree] for g in range(3)], axis=0).astype(F32)
        mix = jnp.where(core == 0, mix, pltpu.roll(mix, chan_local, 1))
        wp[degree] = mix.astype(BF16)
        padded = jnp.concatenate([mix, jnp.zeros((chan_local, channels), F32)], axis=0)
        wc[degree] = padded.T[:, : 3 * chan_local].astype(BF16)
    for comp in range(comps):
        feats = jnp.concatenate([fm[comp], fo[comp]], axis=0)
        qkv[comp] = nn(wp[degree_of(comp)], feats).astype(BF16)
    for head in range(heads):
        query = head_rows_of(qkv, head * rows, rows)
        key = head_rows_of(qkv, chan_local + head * rows, rows)
        value = head_rows_of(qkv, 2 * chan_local + head * rows, rows)
        scores[head] = tn(query, key)
        scores[heads + head] = tn(head_rows_of(cot, head * rows, rows), value)
    for half in range(2):
        span = slice(half * HALO, (half + 1) * HALO)
        index = neighbours[:, span] - (first_atom + (half - 1) * HALO)
        index = jnp.where(index < 0, index + total_atoms, index)
        index = jnp.where(index >= total_atoms, index - total_atoms, index)
        index_rows[:, span] = index
        wide = wide_transpose(index)
        index_wide[span, :] = wide
        for tile in range(3):
            slot_own[half, tile] = slot_tile(wide[:, :slots], tile)


def project_halo(start, chunks, wp, halo_qkv):
    at = 0
    for flm, flo, frm, fro in chunks:
        for comp in range(flm.shape[0]):
            feats = jnp.concatenate(
                [
                    jnp.concatenate([flm[comp], frm[comp]], axis=1),
                    jnp.concatenate([flo[comp], fro[comp]], axis=1),
                ],
                axis=0,
            )
            halo_qkv[at] = nn(wp[degree_of(start + at)], feats).astype(BF16)
            at += 1


def halo_scores(heads, quantity, start, qkv, cot, halo_qkv):
    size, chan_local = halo_qkv.shape[0], cot.shape[1]
    rows = chan_local // heads
    head = quantity % heads
    first = (1 if quantity < heads else 2) * chan_local + head * rows
    source = qkv if quantity < heads else cot
    mine = source[start : start + size, head * rows : (head + 1) * rows, :]
    mine = mine.reshape(size * rows, mine.shape[2])
    theirs = head_rows_of(halo_qkv, first, rows)
    return tn(mine[:, :HALO], theirs[:, :HALO]), tn(mine[:, HALO:], theirs[:, HALO:])


def early_kernel(heads, flm, flo, frm, fro, wp, qkv, cot, halo_qkv, partial, token):
    token[...] = jnp.zeros_like(token)
    project_halo(0, [(flm, flo, frm, fro)], wp, halo_qkv)
    for quantity in range(2 * heads):
        left, right = halo_scores(heads, quantity, 0, qkv, cot, halo_qkv)
        partial[quantity, 0] = left
        partial[quantity, 1] = right


def edge_kernel(heads, score_scale, start, late, *refs):
    chunks = [refs[at : at + 4] for at in range(0, 4 * late, 4)]
    (wp, qkv, cot, scores, partial, bias, valid, index_rows, index_wide,
     halo_qkv, grad_bias, message_a, message_b) = refs[4 * late :]
    slots = valid.shape[0]
    project_halo(start, chunks, wp, halo_qkv)
    lane = lax.broadcasted_iota(jnp.int32, (HALO, 2 * heads * slots), 1)
    gathered = [jnp.zeros((HALO, 2 * heads * slots), F32) for _ in range(2)]
    for quantity in range(2 * heads):
        left, right = halo_scores(heads, quantity, start, qkv, cot, halo_qkv)
        left, right = left + partial[quantity, 0], right + partial[quantity, 1]
        for half in range(2):
            own = scores[quantity, half * HALO : (half + 1) * HALO, :]
            own = [own[:, :HALO], own[:, HALO:]]
            tiles = [left] + own if half == 0 else own + [right]
            index = index_wide[half * HALO : (half + 1) * HALO, :]
            inner, tile_of = index & (HALO - 1), index >> 7
            values = jnp.where(
                tile_of == 0,
                pick(tiles[0], inner),
                jnp.where(tile_of == 1, pick(tiles[1], inner), pick(tiles[2], inner)),
            )
            gathered[half] = jnp.where(lane // slots == quantity, values, gathered[half])
    for half, message in enumerate((message_a, message_b)):
        span = slice(half * HALO, (half + 1) * HALO)
        edges = gathered[half].T.reshape(2, heads, slots, HALO)
        squashed = jnp.tanh(edges[0] * (score_scale / SOFT_CAP))
        logits = SOFT_CAP * squashed + bias[:, :, span]
        live = valid[:, span][None] > 0
        weight = jnp.where(live, jnp.exp(logits), 0.0)
        attention = weight / jnp.sum(weight, axis=1, keepdims=True)
        grad_attn = edges[1]
        grad_logit = attention * (
            grad_attn - jnp.sum(attention * grad_attn, axis=1, keepdims=True)
        )
        grad_bias[:, :, span] = grad_logit
        grad_raw = score_scale * grad_logit * (1.0 - squashed * squashed)
        index = index_rows[:, span]
        both = jnp.stack([grad_raw, attention]).reshape(2 * heads, slots, HALO)
        merged = jnp.zeros_like(both)
        for slot in range(slots):
            same = (index == index[slot : slot + 1, :])[None]
            merged = merged + jnp.where(same, both[:, slot : slot + 1, :], 0.0)
        atom = lax.broadcasted_iota(jnp.int32, (slots, HALO), 1)
        edge_rows = 2 * heads * slots
        message[:edge_rows, :] = merged.reshape(edge_rows, HALO).astype(BF16)
        message[edge_rows:, :] = (index - HALO - atom).astype(F32).astype(BF16)


def joined_rows(early, late, first_row, rows):
    return jnp.concatenate(
        [head_rows_of(early, first_row, rows), head_rows_of(late, first_row, rows)], axis=0
    )


def grads_kernel(heads, slots, pieces, place, fm, fo, *refs):
    chunks = [refs[at : at + 4] for at in range(0, 4 * pieces, 4)]
    (qkv, halo_a, halo_b, cot, slot_own, message_a, message_b, grad_query, own_key, own_value, kept,
     sent_1, sent_2, sent_3, ext, weight_terms) = refs[4 * pieces :]
    places = [(chunk, at) for chunk in chunks for at in range(chunk[0].shape[0])]
    comps, chan_local = fm.shape[0], fm.shape[1]
    rows = chan_local // heads
    atoms = 2 * HALO
    core = place[0]
    empty = jnp.zeros((HALO, HALO), BF16)
    coefs = [message[: 2 * heads * slots, :].astype(F32).T for message in (message_a, message_b)]
    for head in range(heads):
        tables = []
        for quantity in (head, heads + head):
            halves = []
            for half in range(2):
                tiles = [spread(slot_own[half, t], coefs[half], quantity, slots) for t in range(3)]
                tiles = tiles + [empty] if half == 0 else [empty] + tiles
                halves.append(jnp.concatenate(tiles, axis=1))
            tables.append(jnp.concatenate(halves, axis=0))
        raw_table, attn_table = tables
        query = head_rows_of(qkv, head * rows, rows)
        key = head_rows_of(qkv, chan_local + head * rows, rows)
        halo_key = joined_rows(halo_a, halo_b, chan_local + head * rows, rows)
        key_ext = jnp.concatenate([halo_key[:, :HALO], key, halo_key[:, HALO:]], axis=1)
        span = slice(head * rows, (head + 1) * rows)
        value_span = slice(chan_local + head * rows, chan_local + (head + 1) * rows)
        grad_query[:, span, :] = nt(key_ext, raw_table).astype(BF16).reshape(comps, rows, atoms)
        key_sums = nn(query, raw_table)
        own_key[:, span, :] = key_sums[:, HALO : HALO + atoms].reshape(comps, rows, atoms)
        ext[:, span, :] = key_sums.astype(BF16).reshape(comps, rows, atoms + 2 * HALO)
        value_sums = nn(head_rows_of(cot, head * rows, rows), attn_table)
        own_value[:, span, :] = value_sums[:, HALO : HALO + atoms].reshape(comps, rows, atoms)
        ext[:, value_span, :] = value_sums.astype(BF16).reshape(comps, rows, atoms + 2 * HALO)
    for degree in range(LMAX + 1):
        query_total = jnp.zeros((chan_local, 2 * chan_local), F32)
        keyval_total = jnp.zeros((2 * chan_local, 2 * chan_local), F32)
        for comp in range(degree * degree, (degree + 1) * (degree + 1)):
            own = jnp.concatenate([fm[comp], fo[comp]], axis=0)
            (flm, flo, frm, fro), at = places[comp]
            wide = jnp.concatenate(
                [
                    jnp.concatenate([flm[at], fm[comp], frm[at]], axis=1),
                    jnp.concatenate([flo[at], fo[comp], fro[at]], axis=1),
                ],
                axis=0,
            )
            query_total = query_total + nt(grad_query[comp], own)
            keyval_total = keyval_total + nt(ext[comp], wide)
        total = jnp.concatenate([query_total, keyval_total], axis=0)
        total = jnp.where(core == 0, total, pltpu.roll(total, chan_local, 1))
        for g in range(3):
            weight_terms[g * (LMAX + 1) + degree] = total[g * chan_local : (g + 1) * chan_local]
    piece = chan_local // 4
    spot = place[2]
    for delta, part in enumerate((kept, sent_1, sent_2, sent_3)):
        first = pl.multiple_of((spot ^ delta) * piece, piece)
        part[...] = weight_terms[:, pl.ds(first, piece), :].astype(part.dtype)


def halo_slots(message_left, message_right, quantities, slots):
    coefs, tables = [], []
    for message, tile in ((message_left, 2), (message_right, 0)):
        coefs.append(message[: quantities * slots, :].astype(F32).T)
        offset = message[quantities * slots :, :].astype(F32).astype(jnp.int32)
        atom = lax.broadcasted_iota(jnp.int32, offset.shape, 1)
        tables.append(slot_tile(wide_transpose(offset + HALO + atom)[:, :slots], tile))
    return coefs, tables


def final_kernel(heads, slots, start, grad_query, own_key, own_value, halo_qkv, cl, cr,
                 message_left, message_right, wc, mine, theirs, token, grad):
    token[...] = jnp.zeros_like(token)
    comps, chan_local = halo_qkv.shape[0], cl.shape[1]
    rows = chan_local // heads
    stop = start + comps
    grad[:, :chan_local, :] = grad_query[start:stop]
    coefs, tables = halo_slots(message_left, message_right, 2 * heads, slots)
    for head in range(heads):
        span = slice(head * rows, (head + 1) * rows)
        query = head_rows_of(halo_qkv, head * rows, rows)
        sides = (
            (own_key, chan_local, head, (query[:, :HALO], query[:, HALO:])),
            (
                own_value,
                2 * chan_local,
                heads + head,
                tuple(side[start:stop, span, :].reshape(comps * rows, HALO) for side in (cl, cr)),
            ),
        )
        for own, first, quantity, outer in sides:
            rim = [
                nn(outer[at], spread(tables[at], coefs[at], quantity, slots)) for at in range(2)
            ]
            total = own[start:stop, span, :].reshape(comps * rows, 2 * HALO)
            total = total + jnp.concatenate(rim, axis=1)
            grad[:, first + head * rows : first + (head + 1) * rows, :] = (
                total.astype(BF16).reshape(comps, rows, 2 * HALO)
            )
    for comp in range(comps):
        total = nn(wc[degree_of(start + comp)], grad[comp])
        mine[comp] = total[:chan_local]
        theirs[comp] = total[chan_local:].astype(BF16)


def finish_kernel(*refs):
    out, start = refs[-1], 0
    for mine, theirs in zip(refs[:-1:2], refs[1:-1:2]):
        stop = start + mine.shape[0]
        out[start:stop] = (mine[...] + theirs[...].astype(F32)).astype(BF16)
        start = stop


def gather_kernel(place, part_0, part_1, part_2, part_3, out):
    piece = part_0.shape[1]
    spot = place[2]
    for delta, part in enumerate((part_0, part_1, part_2, part_3)):
        first = pl.multiple_of((spot ^ delta) * piece, piece)
        out[:, pl.ds(first, piece), :] = part[...].astype(F32)


def call(kernel, args, outs, scratch=(), scalars=0, limit=24, stay=(), tokens=(), flops=0):
    whole = pl.BlockSpec(memory_space=pltpu.VMEM)
    small = pl.BlockSpec(memory_space=pltpu.SMEM)
    args = [
        pltpu.with_memory_space_constraint(a, pltpu.VMEM) if at in stay else a
        for at, a in enumerate(args)
    ]
    count = len(args)

    def body(*refs):
        kernel(*refs[:count], *refs[count + len(tokens) :])

    return pl.pallas_call(
        body,
        out_shape=tuple(outs),
        in_specs=[small] * scalars
        + [whole] * (count - scalars)
        + [pl.BlockSpec(memory_space=pl.ANY)] * len(tokens),
        out_specs=tuple([whole] * len(outs)),
        scratch_shapes=list(scratch),
        compiler_params=pltpu.CompilerParams(vmem_limit_bytes=limit * 1024 * 1024),
        cost_estimate=pl.CostEstimate(flops=flops, bytes_accessed=1024, transcendentals=0),
    )(*args, *tokens)


def after(values, tokens):
    anywhere = pl.BlockSpec(memory_space=pl.ANY)
    count = len(values)

    def kernel(*refs):
        pass

    return pl.pallas_call(
        kernel,
        out_shape=tuple(jax.ShapeDtypeStruct(v.shape, v.dtype) for v in values),
        in_specs=[anywhere] * (count + len(tokens)),
        out_specs=tuple([anywhere] * count),
        input_output_aliases={i: i for i in range(count)},
        compiler_params=pltpu.CompilerParams(vmem_limit_bytes=1024 * 1024),
        cost_estimate=pl.CostEstimate(flops=0, bytes_accessed=1024, transcendentals=0),
    )(*values, *tokens)


def shifted(value, axis, steps):
    count = lax.axis_size(axis)
    pairs = [(source, (source + steps) % count) for source in range(count)]
    return lax.ppermute(value, axis, pairs)


def exchanged(value, axis, offset):
    count = lax.axis_size(axis)
    return lax.ppermute(value, axis, [(source, source ^ offset) for source in range(count)])


def on_device(features, weights, cotangent, edge_bias, neighbours, valid_mask):
    chan_local, comps, atoms_dev = features.shape
    heads, slots = edge_bias.shape[0], edge_bias.shape[1]
    channels = weights.shape[2]
    assert atoms_dev == 2 * HALO and channels == 2 * chan_local
    score_scale = 1.0 / math.sqrt(chan_local // heads * comps)
    total_atoms = atoms_dev * lax.axis_size("atom")
    count = lax.axis_size("atom")
    assert count >= 4 and count & (count - 1) == 0
    atom_place = lax.axis_index("atom")
    cut_bits = (1, 2) if count >= 8 else (0, 1)
    spot = (atom_place >> cut_bits[0]) & 3
    place = jnp.stack([lax.axis_index("chan"), atom_place * atoms_dev, spot])
    place = place.astype(jnp.int32)
    feature_cut = comps // 2
    feature_cuts = ((0, feature_cut), (feature_cut, comps))

    def held(*dims, dtype=F32):
        return pltpu.VMEM(dims, dtype)

    def plain(*dims, dtype=F32):
        return jax.ShapeDtypeStruct(dims, dtype)

    fm = jnp.transpose(features, (1, 0, 2))
    cot = jnp.transpose(cotangent, (1, 0, 2))
    mix = jnp.transpose(weights, (0, 1, 3, 2))
    anywhere = pl.BlockSpec(memory_space=pl.ANY)
    rim_count = 2 * len(feature_cuts)
    feature_rims = pl.pallas_call(
        functools.partial(split_kernel, feature_cuts),
        out_shape=tuple(
            held(stop - start, chan_local, HALO, dtype=BF16)
            for start, stop in feature_cuts
            for _ in range(2)
        ),
        in_specs=[anywhere],
        out_specs=(pl.BlockSpec(memory_space=pltpu.VMEM),) * rim_count,
        scratch_shapes=[pltpu.SemaphoreType.DMA((rim_count,))],
        compiler_params=pltpu.CompilerParams(vmem_limit_bytes=4 * 1024 * 1024),
    )(pltpu.with_memory_space_constraint(fm, pltpu.HBM))
    from_sides = [
        shifted(rim, "atom", 1 if at % 2 == 0 else -1) for at, rim in enumerate(feature_rims)
    ]
    fo = shifted(fm, "chan", 1)

    qkv, scores, slot_own, index_rows, index_wide, wp, wc, token, *rims = call(
        functools.partial(own_kernel, heads, total_atoms),
        (place, fm, fo, cot, mix, neighbours),
        (
            held(comps, 3 * chan_local, atoms_dev, dtype=BF16),
            held(2 * heads, atoms_dev, atoms_dev),
            held(2, 3, HALO, HALO, dtype=jnp.int32),
            held(slots, atoms_dev, dtype=jnp.int32),
            held(atoms_dev, HALO, dtype=jnp.int32),
            held(LMAX + 1, 3 * chan_local, channels, dtype=BF16),
            held(LMAX + 1, channels, 3 * chan_local, dtype=BF16),
            plain(8, HALO),
            *(
                plain(comps, chan_local, HALO, dtype=BF16) for _ in range(2)
            ),
        ),
        scalars=1,
        stay=(1, 2, 3),
        flops=12 * 10**9,
    )
    flm, frm = after(from_sides[:2], (token,))
    early_chunk = (flm, shifted(flm, "chan", 1), frm, shifted(frm, "chan", 1))
    halo_a, partial, token = call(
        functools.partial(early_kernel, heads),
        (*early_chunk, wp, qkv, cot),
        (
            held(feature_cut, 3 * chan_local, atoms_dev, dtype=BF16),
            held(2 * heads, 2, HALO, HALO),
            plain(8, HALO),
        ),
        stay=tuple(range(7)),
    )
    rims = after(rims, (token,))
    late_sides = after(from_sides[2:], (token,))
    late_chunks = []
    for flm, frm in zip(late_sides[::2], late_sides[1::2]):
        late_chunks += [flm, shifted(flm, "chan", 1), frm, shifted(frm, "chan", 1)]
    from_left, from_right = shifted(rims[0], "atom", 1), shifted(rims[1], "atom", -1)
    halo_b, grad_bias, message_a, message_b = call(
        functools.partial(edge_kernel, heads, score_scale, feature_cut, len(late_chunks) // 4),
        (*late_chunks, wp, qkv, cot, scores, partial, edge_bias, valid_mask, index_rows, index_wide),
        (
            held(comps - feature_cut, 3 * chan_local, atoms_dev, dtype=BF16),
            plain(heads, slots, atoms_dev),
            held((2 * heads + 1) * slots, HALO, dtype=BF16),
            held((2 * heads + 1) * slots, HALO, dtype=BF16),
        ),
        stay=(*range(len(late_chunks) + 5), len(late_chunks) + 7, len(late_chunks) + 8),
    )
    message_left = shifted(message_b, "atom", 1)
    message_right = shifted(message_a, "atom", -1)
    piece = (3 * (LMAX + 1), chan_local // 4, channels)
    grad_query, own_key, own_value, kept, *sent = call(
        functools.partial(grads_kernel, heads, slots, len(feature_cuts)),
        (place, fm, fo, *early_chunk, *late_chunks, qkv, halo_a, halo_b, cot, slot_own, message_a,
         message_b),
        (
            held(comps, chan_local, atoms_dev, dtype=BF16),
            held(comps, chan_local, atoms_dev),
            held(comps, chan_local, atoms_dev),
            held(*piece),
            plain(*piece, dtype=BF16),
            plain(*piece, dtype=BF16),
            plain(*piece, dtype=BF16),
        ),
        scratch=[
            pltpu.VMEM((comps, 2 * chan_local, 2 * atoms_dev), BF16),
            pltpu.VMEM((3 * (LMAX + 1), chan_local, channels), F32),
        ],
        scalars=1,
        stay=tuple(range(1, 10 + 4 * len(feature_cuts))),
    )
    for delta, part in enumerate(sent, 1):
        kept = kept + exchanged(part, "atom", delta << cut_bits[0]).astype(F32)
    rest = [bit for bit in reversed(range(count.bit_length() - 1)) if bit not in cut_bits]
    for at, bit in enumerate(rest):
        also = 1 << rest[at - 1] if 0 < at == len(rest) - 1 else 0
        arrived = exchanged(kept.astype(BF16), "atom", 1 << bit | also)
        if bit == rest[-1]:
            from_left, from_right, message_left, message_right, arrived = after(
                (from_left, from_right, message_left, message_right, arrived), ()
            )
        kept = kept + arrived.astype(F32)
    rounded = kept.astype(BF16)
    pieces = [rounded] + [exchanged(rounded, "atom", d << cut_bits[0]) for d in range(1, 4)]
    (grad_weights,) = call(
        gather_kernel,
        (place, *pieces),
        (plain(3 * (LMAX + 1), chan_local, channels),),
        scalars=1,
        limit=8,
        flops=20 * 10**9,
    )
    parts, tokens = [], ()
    for (start, stop), halo_qkv in zip(feature_cuts, (halo_a, halo_b)):
        size = stop - start
        mine, theirs, token = call(
            functools.partial(final_kernel, heads, slots, start),
            (grad_query, own_key, own_value, halo_qkv, from_left, from_right, message_left,
             message_right, wc),
            (
                held(size, chan_local, atoms_dev),
                held(size, chan_local, atoms_dev, dtype=BF16),
                plain(8, HALO),
            ),
            scratch=[pltpu.VMEM((size, 3 * chan_local, atoms_dev), BF16)],
            limit=16,
            stay=(0, 1, 2, 3, 4, 5, 8),
            tokens=tokens,
        )
        parts += [mine, shifted(theirs, "chan", 1)]
        tokens = (token, pieces[2])
    (out,) = call(
        finish_kernel,
        parts,
        (plain(comps, chan_local, atoms_dev, dtype=BF16),),
        limit=8,
        stay=tuple(range(len(parts))),
    )
    grad_features = jnp.transpose(out, (1, 0, 2))
    grad_weights = grad_weights.reshape(3, LMAX + 1, chan_local, channels)
    grad_weights = jnp.transpose(grad_weights, (0, 1, 3, 2))
    return grad_features, grad_weights, grad_bias


def solution(mesh):
    in_specs = (
        P("chan", None, "atom"),
        P(None, None, None, "chan"),
        P("chan", None, "atom"),
        P("chan", None, "atom"),
        P(None, "atom"),
        P(None, "atom"),
    )
    out_specs = (P("chan", None, "atom"), P(None, None, None, "chan"), P("chan", None, "atom"))
    return jax.shard_map(
        on_device, mesh=mesh, in_specs=in_specs, out_specs=out_specs, check_vma=False
    )
```

```python
import functools
import math

import jax
import jax.numpy as jnp
from jax import lax
from jax.experimental import pallas as pl
from jax.experimental.pallas import tpu as pltpu
from jax.sharding import PartitionSpec as P

LMAX = 6
HALO = 128
SOFT_CAP = 10.0
F32 = jnp.float32
BF16 = jnp.bfloat16


def degree_of(comp):
    return math.isqrt(comp)


def nn(lhs, rhs):
    return lax.dot_general(lhs, rhs, (((1,), (0,)), ((), ())), preferred_element_type=F32)


def nt(lhs, rhs):
    return lax.dot_general(lhs, rhs, (((1,), (1,)), ((), ())), preferred_element_type=F32)


def tn(lhs, rhs):
    return lax.dot_general(lhs, rhs, (((0,), (0,)), ((), ())), preferred_element_type=F32)


def pick(table, index):
    return jnp.take_along_axis(table, index, axis=1, mode="promise_in_bounds")


def head_rows_of(ref, first_row, rows):
    block = ref[:, first_row : first_row + rows, :]
    return block.reshape(block.shape[0] * rows, block.shape[2])


def slot_tile(window_index, tile):
    atoms, slots = window_index.shape
    lane = lax.broadcasted_iota(jnp.int32, (atoms, HALO), 1) + tile * HALO
    found = jnp.full((atoms, HALO), -1, jnp.int32)
    for slot in range(slots):
        found = jnp.where(window_index[:, slot : slot + 1] == lane, slot, found)
    return found


def spread(slot, coef, quantity, slots):
    values = pick(coef, jnp.maximum(slot, 0) + quantity * slots)
    return jnp.where(slot >= 0, values, 0.0).astype(BF16)


def wide_transpose(rows):
    return jnp.concatenate([rows] * (HALO // rows.shape[0]), axis=0).T


def split_kernel(cuts, fm, *refs):
    *parts, sems = refs
    copies = []
    for at, part in enumerate(parts):
        start, stop = cuts[at // 2]
        atom = HALO if at % 2 == 0 else 0
        copies.append(
            pltpu.make_async_copy(
                fm.at[pl.ds(start, stop - start), :, pl.ds(atom, HALO)], part, sems.at[at]
            )
        )
    for copy in copies:
        copy.start()
    for copy in copies:
        copy.wait()


def own_kernel(heads, total_atoms, place, fm, fo, cot, weights, neighbours,
               qkv, scores, slot_own, index_rows, index_wide, wp, wc, token, *rims):
    token[...] = jnp.zeros_like(token)
    rims[0][...] = cot[:, :, HALO:]
    rims[1][...] = cot[:, :, :HALO]
    comps, chan_local = fm.shape[0], fm.shape[1]
    channels = weights.shape[3]
    rows = chan_local // heads
    slots = neighbours.shape[0]
    core, first_atom = place[0], place[1]
    for degree in range(LMAX + 1):
        mix = jnp.concatenate([weights[g, degree] for g in range(3)], axis=0).astype(F32)
        mix = jnp.where(core == 0, mix, pltpu.roll(mix, chan_local, 1))
        wp[degree] = mix.astype(BF16)
        padded = jnp.concatenate([mix, jnp.zeros((chan_local, channels), F32)], axis=0)
        wc[degree] = padded.T[:, : 3 * chan_local].astype(BF16)
    for comp in range(comps):
        feats = jnp.concatenate([fm[comp], fo[comp]], axis=0)
        qkv[comp] = nn(wp[degree_of(comp)], feats).astype(BF16)
    for head in range(heads):
        query = head_rows_of(qkv, head * rows, rows)
        key = head_rows_of(qkv, chan_local + head * rows, rows)
        value = head_rows_of(qkv, 2 * chan_local + head * rows, rows)
        scores[head] = tn(query, key)
        scores[heads + head] = tn(head_rows_of(cot, head * rows, rows), value)
    for half in range(2):
        span = slice(half * HALO, (half + 1) * HALO)
        index = neighbours[:, span] - (first_atom + (half - 1) * HALO)
        index = jnp.where(index < 0, index + total_atoms, index)
        index = jnp.where(index >= total_atoms, index - total_atoms, index)
        index_rows[:, span] = index
        wide = wide_transpose(index)
        index_wide[span, :] = wide
        for tile in range(3):
            slot_own[half, tile] = slot_tile(wide[:, :slots], tile)


def project_halo(start, chunks, wp, halo_qkv):
    at = 0
    for flm, flo, frm, fro in chunks:
        for comp in range(flm.shape[0]):
            feats = jnp.concatenate(
                [
                    jnp.concatenate([flm[comp], frm[comp]], axis=1),
                    jnp.concatenate([flo[comp], fro[comp]], axis=1),
                ],
                axis=0,
            )
            halo_qkv[at] = nn(wp[degree_of(start + at)], feats).astype(BF16)
            at += 1


def halo_scores(heads, quantity, start, qkv, cot, halo_qkv):
    size, chan_local = halo_qkv.shape[0], cot.shape[1]
    rows = chan_local // heads
    head = quantity % heads
    first = (1 if quantity < heads else 2) * chan_local + head * rows
    source = qkv if quantity < heads else cot
    mine = source[start : start + size, head * rows : (head + 1) * rows, :]
    mine = mine.reshape(size * rows, mine.shape[2])
    theirs = head_rows_of(halo_qkv, first, rows)
    return tn(mine[:, :HALO], theirs[:, :HALO]), tn(mine[:, HALO:], theirs[:, HALO:])


def early_kernel(heads, flm, flo, frm, fro, wp, qkv, cot, halo_qkv, partial, token):
    token[...] = jnp.zeros_like(token)
    project_halo(0, [(flm, flo, frm, fro)], wp, halo_qkv)
    for quantity in range(2 * heads):
        left, right = halo_scores(heads, quantity, 0, qkv, cot, halo_qkv)
        partial[quantity, 0] = left
        partial[quantity, 1] = right


def edge_kernel(heads, score_scale, start, late, *refs):
    chunks = [refs[at : at + 4] for at in range(0, 4 * late, 4)]
    (wp, qkv, cot, scores, partial, bias, valid, index_rows, index_wide,
     halo_qkv, grad_bias, message_a, message_b) = refs[4 * late :]
    slots = valid.shape[0]
    project_halo(start, chunks, wp, halo_qkv)
    lane = lax.broadcasted_iota(jnp.int32, (HALO, 2 * heads * slots), 1)
    gathered = [jnp.zeros((HALO, 2 * heads * slots), F32) for _ in range(2)]
    for quantity in range(2 * heads):
        left, right = halo_scores(heads, quantity, start, qkv, cot, halo_qkv)
        left, right = left + partial[quantity, 0], right + partial[quantity, 1]
        for half in range(2):
            own = scores[quantity, half * HALO : (half + 1) * HALO, :]
            own = [own[:, :HALO], own[:, HALO:]]
            tiles = [left] + own if half == 0 else own + [right]
            index = index_wide[half * HALO : (half + 1) * HALO, :]
            inner, tile_of = index & (HALO - 1), index >> 7
            values = jnp.where(
                tile_of == 0,
                pick(tiles[0], inner),
                jnp.where(tile_of == 1, pick(tiles[1], inner), pick(tiles[2], inner)),
            )
            gathered[half] = jnp.where(lane // slots == quantity, values, gathered[half])
    for half, message in enumerate((message_a, message_b)):
        span = slice(half * HALO, (half + 1) * HALO)
        edges = gathered[half].T.reshape(2, heads, slots, HALO)
        squashed = jnp.tanh(edges[0] * (score_scale / SOFT_CAP))
        logits = SOFT_CAP * squashed + bias[:, :, span]
        live = valid[:, span][None] > 0
        weight = jnp.where(live, jnp.exp(logits), 0.0)
        attention = weight / jnp.sum(weight, axis=1, keepdims=True)
        grad_attn = edges[1]
        grad_logit = attention * (
            grad_attn - jnp.sum(attention * grad_attn, axis=1, keepdims=True)
        )
        grad_bias[:, :, span] = grad_logit
        grad_raw = score_scale * grad_logit * (1.0 - squashed * squashed)
        index = index_rows[:, span]
        both = jnp.stack([grad_raw, attention]).reshape(2 * heads, slots, HALO)
        merged = jnp.zeros_like(both)
        for slot in range(slots):
            same = (index == index[slot : slot + 1, :])[None]
            merged = merged + jnp.where(same, both[:, slot : slot + 1, :], 0.0)
        atom = lax.broadcasted_iota(jnp.int32, (slots, HALO), 1)
        edge_rows = 2 * heads * slots
        message[:edge_rows, :] = merged.reshape(edge_rows, HALO)
        message[edge_rows : edge_rows + slots, :] = (index - HALO - atom).astype(F32)
        message[edge_rows + slots :, :] = jnp.zeros_like(message[edge_rows + slots :, :])


def joined_rows(early, late, first_row, rows):
    return jnp.concatenate(
        [head_rows_of(early, first_row, rows), head_rows_of(late, first_row, rows)], axis=0
    )


def grads_kernel(heads, slots, pieces, place, fm, fo, *refs):
    chunks = [refs[at : at + 4] for at in range(0, 4 * pieces, 4)]
    (qkv, halo_a, halo_b, cot, slot_own, message_a, message_b, grad_query, own_key, own_value, kept,
     sent_1, sent_2, sent_3, ext, weight_terms) = refs[4 * pieces :]
    places = [(chunk, at) for chunk in chunks for at in range(chunk[0].shape[0])]
    comps, chan_local = fm.shape[0], fm.shape[1]
    rows = chan_local // heads
    atoms = 2 * HALO
    core = place[0]
    empty = jnp.zeros((HALO, HALO), BF16)
    coefs = [message[: 2 * heads * slots, :].T for message in (message_a, message_b)]
    for head in range(heads):
        tables = []
        for quantity in (head, heads + head):
            halves = []
            for half in range(2):
                tiles = [spread(slot_own[half, t], coefs[half], quantity, slots) for t in range(3)]
                tiles = tiles + [empty] if half == 0 else [empty] + tiles
                halves.append(jnp.concatenate(tiles, axis=1))
            tables.append(jnp.concatenate(halves, axis=0))
        raw_table, attn_table = tables
        query = head_rows_of(qkv, head * rows, rows)
        key = head_rows_of(qkv, chan_local + head * rows, rows)
        halo_key = joined_rows(halo_a, halo_b, chan_local + head * rows, rows)
        key_ext = jnp.concatenate([halo_key[:, :HALO], key, halo_key[:, HALO:]], axis=1)
        span = slice(head * rows, (head + 1) * rows)
        value_span = slice(chan_local + head * rows, chan_local + (head + 1) * rows)
        grad_query[:, span, :] = nt(key_ext, raw_table).astype(BF16).reshape(comps, rows, atoms)
        key_sums = nn(query, raw_table)
        own_key[:, span, :] = key_sums[:, HALO : HALO + atoms].reshape(comps, rows, atoms)
        ext[:, span, :] = key_sums.astype(BF16).reshape(comps, rows, atoms + 2 * HALO)
        value_sums = nn(head_rows_of(cot, head * rows, rows), attn_table)
        own_value[:, span, :] = value_sums[:, HALO : HALO + atoms].reshape(comps, rows, atoms)
        ext[:, value_span, :] = value_sums.astype(BF16).reshape(comps, rows, atoms + 2 * HALO)
    for degree in range(LMAX + 1):
        query_total = jnp.zeros((chan_local, 2 * chan_local), F32)
        keyval_total = jnp.zeros((2 * chan_local, 2 * chan_local), F32)
        for comp in range(degree * degree, (degree + 1) * (degree + 1)):
            own = jnp.concatenate([fm[comp], fo[comp]], axis=0)
            (flm, flo, frm, fro), at = places[comp]
            wide = jnp.concatenate(
                [
                    jnp.concatenate([flm[at], fm[comp], frm[at]], axis=1),
                    jnp.concatenate([flo[at], fo[comp], fro[at]], axis=1),
                ],
                axis=0,
            )
            query_total = query_total + nt(grad_query[comp], own)
            keyval_total = keyval_total + nt(ext[comp], wide)
        total = jnp.concatenate([query_total, keyval_total], axis=0)
        total = jnp.where(core == 0, total, pltpu.roll(total, chan_local, 1))
        for g in range(3):
            weight_terms[g * (LMAX + 1) + degree] = total[g * chan_local : (g + 1) * chan_local]
    piece = chan_local // 4
    spot = place[2]
    for delta, part in enumerate((kept, sent_1, sent_2, sent_3)):
        first = pl.multiple_of((spot ^ delta) * piece, piece)
        part[...] = weight_terms[:, pl.ds(first, piece), :].astype(part.dtype)


def halo_slots(message_left, message_right, quantities, slots):
    coefs, tables = [], []
    for message, tile in ((message_left, 2), (message_right, 0)):
        coefs.append(message[: quantities * slots, :].T)
        offset = message[quantities * slots : (quantities + 1) * slots, :].astype(jnp.int32)
        atom = lax.broadcasted_iota(jnp.int32, offset.shape, 1)
        tables.append(slot_tile(wide_transpose(offset + HALO + atom)[:, :slots], tile))
    return coefs, tables


def final_kernel(heads, slots, start, grad_query, own_key, own_value, halo_qkv, cl, cr,
                 message_left, message_right, wc, mine, theirs, token, grad):
    token[...] = jnp.zeros_like(token)
    comps, chan_local = halo_qkv.shape[0], cl.shape[1]
    rows = chan_local // heads
    stop = start + comps
    grad[:, :chan_local, :] = grad_query[start:stop]
    coefs, tables = halo_slots(message_left, message_right, 2 * heads, slots)
    for head in range(heads):
        span = slice(head * rows, (head + 1) * rows)
        query = head_rows_of(halo_qkv, head * rows, rows)
        sides = (
            (own_key, chan_local, head, (query[:, :HALO], query[:, HALO:])),
            (
                own_value,
                2 * chan_local,
                heads + head,
                tuple(side[start:stop, span, :].reshape(comps * rows, HALO) for side in (cl, cr)),
            ),
        )
        for own, first, quantity, outer in sides:
            rim = [
                nn(outer[at], spread(tables[at], coefs[at], quantity, slots)) for at in range(2)
            ]
            total = own[start:stop, span, :].reshape(comps * rows, 2 * HALO)
            total = total + jnp.concatenate(rim, axis=1)
            grad[:, first + head * rows : first + (head + 1) * rows, :] = (
                total.astype(BF16).reshape(comps, rows, 2 * HALO)
            )
    for comp in range(comps):
        total = nn(wc[degree_of(start + comp)], grad[comp])
        mine[comp] = total[:chan_local]
        theirs[comp] = total[chan_local:].astype(BF16)


def finish_kernel(*refs):
    out, start = refs[-1], 0
    for mine, theirs in zip(refs[:-1:2], refs[1:-1:2]):
        stop = start + mine.shape[0]
        out[start:stop] = (mine[...] + theirs[...].astype(F32)).astype(BF16)
        start = stop


def gather_kernel(place, part_0, part_1, part_2, part_3, out):
    piece = part_0.shape[1]
    spot = place[2]
    for delta, part in enumerate((part_0, part_1, part_2, part_3)):
        first = pl.multiple_of((spot ^ delta) * piece, piece)
        out[:, pl.ds(first, piece), :] = part[...].astype(F32)


def call(kernel, args, outs, scratch=(), scalars=0, limit=24, stay=(), tokens=(), flops=0):
    whole = pl.BlockSpec(memory_space=pltpu.VMEM)
    small = pl.BlockSpec(memory_space=pltpu.SMEM)
    args = [
        pltpu.with_memory_space_constraint(a, pltpu.VMEM) if at in stay else a
        for at, a in enumerate(args)
    ]
    count = len(args)

    def body(*refs):
        kernel(*refs[:count], *refs[count + len(tokens) :])

    return pl.pallas_call(
        body,
        out_shape=tuple(outs),
        in_specs=[small] * scalars
        + [whole] * (count - scalars)
        + [pl.BlockSpec(memory_space=pl.ANY)] * len(tokens),
        out_specs=tuple([whole] * len(outs)),
        scratch_shapes=list(scratch),
        compiler_params=pltpu.CompilerParams(vmem_limit_bytes=limit * 1024 * 1024),
        cost_estimate=pl.CostEstimate(flops=flops, bytes_accessed=1024, transcendentals=0),
    )(*args, *tokens)


def after(values, tokens):
    anywhere = pl.BlockSpec(memory_space=pl.ANY)
    count = len(values)

    def kernel(*refs):
        pass

    return pl.pallas_call(
        kernel,
        out_shape=tuple(jax.ShapeDtypeStruct(v.shape, v.dtype) for v in values),
        in_specs=[anywhere] * (count + len(tokens)),
        out_specs=tuple([anywhere] * count),
        input_output_aliases={i: i for i in range(count)},
        compiler_params=pltpu.CompilerParams(vmem_limit_bytes=1024 * 1024),
        cost_estimate=pl.CostEstimate(flops=0, bytes_accessed=1024, transcendentals=0),
    )(*values, *tokens)


def shifted(value, axis, steps):
    count = lax.axis_size(axis)
    pairs = [(source, (source + steps) % count) for source in range(count)]
    return lax.ppermute(value, axis, pairs)


def exchanged(value, axis, offset):
    count = lax.axis_size(axis)
    return lax.ppermute(value, axis, [(source, source ^ offset) for source in range(count)])


def on_device(features, weights, cotangent, edge_bias, neighbours, valid_mask):
    chan_local, comps, atoms_dev = features.shape
    heads, slots = edge_bias.shape[0], edge_bias.shape[1]
    channels = weights.shape[2]
    assert atoms_dev == 2 * HALO and channels == 2 * chan_local
    score_scale = 1.0 / math.sqrt(chan_local // heads * comps)
    total_atoms = atoms_dev * lax.axis_size("atom")
    count = lax.axis_size("atom")
    assert count >= 4 and count & (count - 1) == 0
    atom_place = lax.axis_index("atom")
    cut_bits = (1, 2) if count >= 8 else (0, 1)
    spot = (atom_place >> cut_bits[0]) & 3
    place = jnp.stack([lax.axis_index("chan"), atom_place * atoms_dev, spot])
    place = place.astype(jnp.int32)
    feature_cut = comps // 2
    feature_cuts = ((0, feature_cut), (feature_cut, comps))

    def held(*dims, dtype=F32):
        return pltpu.VMEM(dims, dtype)

    def plain(*dims, dtype=F32):
        return jax.ShapeDtypeStruct(dims, dtype)

    fm = jnp.transpose(features, (1, 0, 2))
    cot = jnp.transpose(cotangent, (1, 0, 2))
    mix = jnp.transpose(weights, (0, 1, 3, 2))
    anywhere = pl.BlockSpec(memory_space=pl.ANY)
    rim_count = 2 * len(feature_cuts)
    feature_rims = pl.pallas_call(
        functools.partial(split_kernel, feature_cuts),
        out_shape=tuple(
            held(stop - start, chan_local, HALO, dtype=BF16)
            for start, stop in feature_cuts
            for _ in range(2)
        ),
        in_specs=[anywhere],
        out_specs=(pl.BlockSpec(memory_space=pltpu.VMEM),) * rim_count,
        scratch_shapes=[pltpu.SemaphoreType.DMA((rim_count,))],
        compiler_params=pltpu.CompilerParams(vmem_limit_bytes=4 * 1024 * 1024),
    )(pltpu.with_memory_space_constraint(fm, pltpu.HBM))
    from_sides = [
        shifted(rim, "atom", 1 if at % 2 == 0 else -1) for at, rim in enumerate(feature_rims)
    ]
    fo = shifted(fm, "chan", 1)

    qkv, scores, slot_own, index_rows, index_wide, wp, wc, token, *rims = call(
        functools.partial(own_kernel, heads, total_atoms),
        (place, fm, fo, cot, mix, neighbours),
        (
            held(comps, 3 * chan_local, atoms_dev, dtype=BF16),
            held(2 * heads, atoms_dev, atoms_dev),
            held(2, 3, HALO, HALO, dtype=jnp.int32),
            held(slots, atoms_dev, dtype=jnp.int32),
            held(atoms_dev, HALO, dtype=jnp.int32),
            held(LMAX + 1, 3 * chan_local, channels, dtype=BF16),
            held(LMAX + 1, channels, 3 * chan_local, dtype=BF16),
            plain(8, HALO),
            *(
                plain(comps, chan_local, HALO, dtype=BF16) for _ in range(2)
            ),
        ),
        scalars=1,
        stay=(1, 2, 3),
        flops=12 * 10**9,
    )
    flm, frm = after(from_sides[:2], (token,))
    early_chunk = (flm, shifted(flm, "chan", 1), frm, shifted(frm, "chan", 1))
    halo_a, partial, token = call(
        functools.partial(early_kernel, heads),
        (*early_chunk, wp, qkv, cot),
        (
            held(feature_cut, 3 * chan_local, atoms_dev, dtype=BF16),
            held(2 * heads, 2, HALO, HALO),
            plain(8, HALO),
        ),
        stay=tuple(range(7)),
    )
    rims = after(rims, (token,))
    late_sides = after(from_sides[2:], (token,))
    late_chunks = []
    for flm, frm in zip(late_sides[::2], late_sides[1::2]):
        late_chunks += [flm, shifted(flm, "chan", 1), frm, shifted(frm, "chan", 1)]
    from_left, from_right = shifted(rims[0], "atom", 1), shifted(rims[1], "atom", -1)
    halo_b, grad_bias, message_a, message_b = call(
        functools.partial(edge_kernel, heads, score_scale, feature_cut, len(late_chunks) // 4),
        (*late_chunks, wp, qkv, cot, scores, partial, edge_bias, valid_mask, index_rows, index_wide),
        (
            held(comps - feature_cut, 3 * chan_local, atoms_dev, dtype=BF16),
            plain(heads, slots, atoms_dev),
            held((2 * heads + 3) * slots, HALO),
            held((2 * heads + 3) * slots, HALO),
        ),
        stay=(*range(len(late_chunks) + 5), len(late_chunks) + 7, len(late_chunks) + 8),
    )
    message_left = shifted(message_b, "atom", 1)
    message_right = shifted(message_a, "atom", -1)
    piece = (3 * (LMAX + 1), chan_local // 4, channels)
    grad_query, own_key, own_value, kept, *sent = call(
        functools.partial(grads_kernel, heads, slots, len(feature_cuts)),
        (place, fm, fo, *early_chunk, *late_chunks, qkv, halo_a, halo_b, cot, slot_own, message_a,
         message_b),
        (
            held(comps, chan_local, atoms_dev, dtype=BF16),
            held(comps, chan_local, atoms_dev),
            held(comps, chan_local, atoms_dev),
            held(*piece),
            plain(*piece, dtype=BF16),
            plain(*piece, dtype=BF16),
            plain(*piece, dtype=BF16),
        ),
        scratch=[
            pltpu.VMEM((comps, 2 * chan_local, 2 * atoms_dev), BF16),
            pltpu.VMEM((3 * (LMAX + 1), chan_local, channels), F32),
        ],
        scalars=1,
        stay=tuple(range(1, 10 + 4 * len(feature_cuts))),
    )
    for delta, part in enumerate(sent, 1):
        kept = kept + exchanged(part, "atom", delta << cut_bits[0]).astype(F32)
    rest = [bit for bit in reversed(range(count.bit_length() - 1)) if bit not in cut_bits]
    for at, bit in enumerate(rest):
        also = 1 << rest[at - 1] if 0 < at == len(rest) - 1 else 0
        arrived = exchanged(kept.astype(BF16), "atom", 1 << bit | also)
        if bit == rest[-1]:
            from_left, from_right, message_left, message_right, arrived = after(
                (from_left, from_right, message_left, message_right, arrived), ()
            )
        kept = kept + arrived.astype(F32)
    rounded = kept.astype(BF16)
    pieces = [rounded] + [exchanged(rounded, "atom", d << cut_bits[0]) for d in range(1, 4)]
    (grad_weights,) = call(
        gather_kernel,
        (place, *pieces),
        (plain(3 * (LMAX + 1), chan_local, channels),),
        scalars=1,
        limit=8,
        flops=20 * 10**9,
    )
    parts, tokens = [], ()
    for (start, stop), halo_qkv in zip(feature_cuts, (halo_a, halo_b)):
        size = stop - start
        mine, theirs, token = call(
            functools.partial(final_kernel, heads, slots, start),
            (grad_query, own_key, own_value, halo_qkv, from_left, from_right, message_left,
             message_right, wc),
            (
                held(size, chan_local, atoms_dev),
                held(size, chan_local, atoms_dev, dtype=BF16),
                plain(8, HALO),
            ),
            scratch=[pltpu.VMEM((size, 3 * chan_local, atoms_dev), BF16)],
            limit=16,
            stay=(0, 1, 2, 3, 4, 5, 8),
            tokens=tokens,
        )
        parts += [mine, shifted(theirs, "chan", 1)]
        tokens = (token, pieces[2])
    (out,) = call(
        finish_kernel,
        parts,
        (plain(comps, chan_local, atoms_dev, dtype=BF16),),
        limit=8,
        stay=tuple(range(len(parts))),
    )
    grad_features = jnp.transpose(out, (1, 0, 2))
    grad_weights = grad_weights.reshape(3, LMAX + 1, chan_local, channels)
    grad_weights = jnp.transpose(grad_weights, (0, 1, 3, 2))
    return grad_features, grad_weights, grad_bias


def solution(mesh):
    in_specs = (
        P("chan", None, "atom"),
        P(None, None, None, "chan"),
        P("chan", None, "atom"),
        P("chan", None, "atom"),
        P(None, "atom"),
        P(None, "atom"),
    )
    out_specs = (P("chan", None, "atom"), P(None, None, None, "chan"), P("chan", None, "atom"))
    return jax.shard_map(
        on_device, mesh=mesh, in_specs=in_specs, out_specs=out_specs, check_vma=False
    )
```

```python
import functools
import math

import jax
import jax.numpy as jnp
from jax import lax
from jax.experimental import pallas as pl
from jax.experimental.pallas import tpu as pltpu
from jax.sharding import PartitionSpec as P

LMAX = 6
HALO = 128
SOFT_CAP = 10.0
F32 = jnp.float32
BF16 = jnp.bfloat16


def degree_of(comp):
    return math.isqrt(comp)


def nn(lhs, rhs):
    return lax.dot_general(lhs, rhs, (((1,), (0,)), ((), ())), preferred_element_type=F32)


def nt(lhs, rhs):
    return lax.dot_general(lhs, rhs, (((1,), (1,)), ((), ())), preferred_element_type=F32)


def tn(lhs, rhs):
    return lax.dot_general(lhs, rhs, (((0,), (0,)), ((), ())), preferred_element_type=F32)


def pick(table, index):
    return jnp.take_along_axis(table, index, axis=1, mode="promise_in_bounds")


def head_rows_of(ref, first_row, rows):
    block = ref[:, first_row : first_row + rows, :]
    return block.reshape(block.shape[0] * rows, block.shape[2])


def slot_tile(window_index, tile):
    atoms, slots = window_index.shape
    lane = lax.broadcasted_iota(jnp.int32, (atoms, HALO), 1) + tile * HALO
    found = jnp.full((atoms, HALO), -1, jnp.int32)
    for slot in range(slots):
        found = jnp.where(window_index[:, slot : slot + 1] == lane, slot, found)
    return found


def spread(slot, coef, quantity, slots):
    values = pick(coef, jnp.maximum(slot, 0) + quantity * slots)
    return jnp.where(slot >= 0, values, 0.0).astype(BF16)


def wide_transpose(rows):
    return jnp.concatenate([rows] * (HALO // rows.shape[0]), axis=0).T


def split_kernel(cuts, fm, *refs):
    *parts, sems = refs
    copies = []
    for at, part in enumerate(parts):
        start, stop = cuts[at // 2]
        atom = HALO if at % 2 == 0 else 0
        copies.append(
            pltpu.make_async_copy(
                fm.at[pl.ds(start, stop - start), :, pl.ds(atom, HALO)], part, sems.at[at]
            )
        )
    for copy in copies:
        copy.start()
    for copy in copies:
        copy.wait()


def own_kernel(heads, total_atoms, place, fm, fo, cot, weights, neighbours,
               qkv, scores, slot_own, index_rows, index_wide, wp, wc, token, *rims):
    token[...] = jnp.zeros_like(token)
    rims[0][...] = cot[:, :, HALO:]
    rims[1][...] = cot[:, :, :HALO]
    comps, chan_local = fm.shape[0], fm.shape[1]
    channels = weights.shape[3]
    rows = chan_local // heads
    slots = neighbours.shape[0]
    core, first_atom = place[0], place[1]
    for degree in range(LMAX + 1):
        mix = jnp.concatenate([weights[g, degree] for g in range(3)], axis=0).astype(F32)
        mix = jnp.where(core == 0, mix, pltpu.roll(mix, chan_local, 1))
        wp[degree] = mix.astype(BF16)
        padded = jnp.concatenate([mix, jnp.zeros((chan_local, channels), F32)], axis=0)
        wc[degree] = padded.T[:, : 3 * chan_local].astype(BF16)
    for comp in range(comps):
        feats = jnp.concatenate([fm[comp], fo[comp]], axis=0)
        qkv[comp] = nn(wp[degree_of(comp)], feats).astype(BF16)
    for head in range(heads):
        query = head_rows_of(qkv, head * rows, rows)
        key = head_rows_of(qkv, chan_local + head * rows, rows)
        value = head_rows_of(qkv, 2 * chan_local + head * rows, rows)
        scores[head] = tn(query, key)
        scores[heads + head] = tn(head_rows_of(cot, head * rows, rows), value)
    for half in range(2):
        span = slice(half * HALO, (half + 1) * HALO)
        index = neighbours[:, span] - (first_atom + (half - 1) * HALO)
        index = jnp.where(index < 0, index + total_atoms, index)
        index = jnp.where(index >= total_atoms, index - total_atoms, index)
        index_rows[:, span] = index
        wide = wide_transpose(index)
        index_wide[span, :] = wide
        for tile in range(3):
            slot_own[half, tile] = slot_tile(wide[:, :slots], tile)


def project_halo(start, chunks, wp, halo_qkv):
    at = 0
    for flm, flo, frm, fro in chunks:
        for comp in range(flm.shape[0]):
            feats = jnp.concatenate(
                [
                    jnp.concatenate([flm[comp], frm[comp]], axis=1),
                    jnp.concatenate([flo[comp], fro[comp]], axis=1),
                ],
                axis=0,
            )
            halo_qkv[at] = nn(wp[degree_of(start + at)], feats).astype(BF16)
            at += 1


def halo_scores(heads, quantity, start, qkv, cot, halo_qkv):
    size, chan_local = halo_qkv.shape[0], cot.shape[1]
    rows = chan_local // heads
    head = quantity % heads
    first = (1 if quantity < heads else 2) * chan_local + head * rows
    source = qkv if quantity < heads else cot
    mine = source[start : start + size, head * rows : (head + 1) * rows, :]
    mine = mine.reshape(size * rows, mine.shape[2])
    theirs = head_rows_of(halo_qkv, first, rows)
    return tn(mine[:, :HALO], theirs[:, :HALO]), tn(mine[:, HALO:], theirs[:, HALO:])


def early_kernel(heads, flm, flo, frm, fro, wp, qkv, cot, halo_qkv, partial, token):
    token[...] = jnp.zeros_like(token)
    project_halo(0, [(flm, flo, frm, fro)], wp, halo_qkv)
    for quantity in range(2 * heads):
        left, right = halo_scores(heads, quantity, 0, qkv, cot, halo_qkv)
        partial[quantity, 0] = left
        partial[quantity, 1] = right


def edge_kernel(heads, score_scale, start, late, *refs):
    chunks = [refs[at : at + 4] for at in range(0, 4 * late, 4)]
    (wp, qkv, cot, scores, partial, bias, valid, index_rows, index_wide,
     halo_qkv, grad_bias, message_a, message_b) = refs[4 * late :]
    slots = valid.shape[0]
    project_halo(start, chunks, wp, halo_qkv)
    lane = lax.broadcasted_iota(jnp.int32, (HALO, 2 * heads * slots), 1)
    gathered = [jnp.zeros((HALO, 2 * heads * slots), F32) for _ in range(2)]
    for quantity in range(2 * heads):
        left, right = halo_scores(heads, quantity, start, qkv, cot, halo_qkv)
        left, right = left + partial[quantity, 0], right + partial[quantity, 1]
        for half in range(2):
            own = scores[quantity, half * HALO : (half + 1) * HALO, :]
            own = [own[:, :HALO], own[:, HALO:]]
            tiles = [left] + own if half == 0 else own + [right]
            index = index_wide[half * HALO : (half + 1) * HALO, :]
            inner, tile_of = index & (HALO - 1), index >> 7
            values = jnp.where(
                tile_of == 0,
                pick(tiles[0], inner),
                jnp.where(tile_of == 1, pick(tiles[1], inner), pick(tiles[2], inner)),
            )
            gathered[half] = jnp.where(lane // slots == quantity, values, gathered[half])
    for half, message in enumerate((message_a, message_b)):
        span = slice(half * HALO, (half + 1) * HALO)
        edges = gathered[half].T.reshape(2, heads, slots, HALO)
        squashed = jnp.tanh(edges[0] * (score_scale / SOFT_CAP))
        logits = SOFT_CAP * squashed + bias[:, :, span]
        live = valid[:, span][None] > 0
        weight = jnp.where(live, jnp.exp(logits), 0.0)
        attention = weight / jnp.sum(weight, axis=1, keepdims=True)
        grad_attn = edges[1]
        grad_logit = attention * (
            grad_attn - jnp.sum(attention * grad_attn, axis=1, keepdims=True)
        )
        grad_bias[:, :, span] = grad_logit
        grad_raw = score_scale * grad_logit * (1.0 - squashed * squashed)
        index = index_rows[:, span]
        both = jnp.stack([grad_raw, attention]).reshape(2 * heads, slots, HALO)
        merged = jnp.zeros_like(both)
        for slot in range(slots):
            same = (index == index[slot : slot + 1, :])[None]
            merged = merged + jnp.where(same, both[:, slot : slot + 1, :], 0.0)
        atom = lax.broadcasted_iota(jnp.int32, (slots, HALO), 1)
        edge_rows = 2 * heads * slots
        message[:edge_rows, :] = merged.reshape(edge_rows, HALO)
        message[edge_rows : edge_rows + slots, :] = (index - HALO - atom).astype(F32)
        message[edge_rows + slots :, :] = jnp.zeros_like(message[edge_rows + slots :, :])


def joined_rows(early, late, first_row, rows):
    return jnp.concatenate(
        [head_rows_of(early, first_row, rows), head_rows_of(late, first_row, rows)], axis=0
    )


def grads_kernel(heads, slots, pieces, place, fm, fo, *refs):
    chunks = [refs[at : at + 4] for at in range(0, 4 * pieces, 4)]
    (qkv, halo_a, halo_b, cot, slot_own, message_a, message_b, grad_query, own_key, own_value, kept,
     sent_1, sent_2, sent_3, ext, weight_terms) = refs[4 * pieces :]
    places = [(chunk, at) for chunk in chunks for at in range(chunk[0].shape[0])]
    comps, chan_local = fm.shape[0], fm.shape[1]
    rows = chan_local // heads
    atoms = 2 * HALO
    core = place[0]
    empty = jnp.zeros((HALO, HALO), BF16)
    coefs = [message[: 2 * heads * slots, :].T for message in (message_a, message_b)]
    for head in range(heads):
        tables = []
        for quantity in (head, heads + head):
            halves = []
            for half in range(2):
                tiles = [spread(slot_own[half, t], coefs[half], quantity, slots) for t in range(3)]
                tiles = tiles + [empty] if half == 0 else [empty] + tiles
                halves.append(jnp.concatenate(tiles, axis=1))
            tables.append(jnp.concatenate(halves, axis=0))
        raw_table, attn_table = tables
        query = head_rows_of(qkv, head * rows, rows)
        key = head_rows_of(qkv, chan_local + head * rows, rows)
        halo_key = joined_rows(halo_a, halo_b, chan_local + head * rows, rows)
        key_ext = jnp.concatenate([halo_key[:, :HALO], key, halo_key[:, HALO:]], axis=1)
        span = slice(head * rows, (head + 1) * rows)
        value_span = slice(chan_local + head * rows, chan_local + (head + 1) * rows)
        grad_query[:, span, :] = nt(key_ext, raw_table).astype(BF16).reshape(comps, rows, atoms)
        key_sums = nn(query, raw_table)
        own_key[:, span, :] = key_sums[:, HALO : HALO + atoms].reshape(comps, rows, atoms)
        ext[:, span, :] = key_sums.astype(BF16).reshape(comps, rows, atoms + 2 * HALO)
        value_sums = nn(head_rows_of(cot, head * rows, rows), attn_table)
        own_value[:, span, :] = value_sums[:, HALO : HALO + atoms].reshape(comps, rows, atoms)
        ext[:, value_span, :] = value_sums.astype(BF16).reshape(comps, rows, atoms + 2 * HALO)
    for degree in range(LMAX + 1):
        query_total = jnp.zeros((chan_local, 2 * chan_local), F32)
        keyval_total = jnp.zeros((2 * chan_local, 2 * chan_local), F32)
        for comp in range(degree * degree, (degree + 1) * (degree + 1)):
            own = jnp.concatenate([fm[comp], fo[comp]], axis=0)
            (flm, flo, frm, fro), at = places[comp]
            wide = jnp.concatenate(
                [
                    jnp.concatenate([flm[at], fm[comp], frm[at]], axis=1),
                    jnp.concatenate([flo[at], fo[comp], fro[at]], axis=1),
                ],
                axis=0,
            )
            query_total = query_total + nt(grad_query[comp], own)
            keyval_total = keyval_total + nt(ext[comp], wide)
        total = jnp.concatenate([query_total, keyval_total], axis=0)
        total = jnp.where(core == 0, total, pltpu.roll(total, chan_local, 1))
        for g in range(3):
            weight_terms[g * (LMAX + 1) + degree] = total[g * chan_local : (g + 1) * chan_local]
    piece = chan_local // 4
    spot = place[2]
    for delta, part in enumerate((kept, sent_1, sent_2, sent_3)):
        first = pl.multiple_of((spot ^ delta) * piece, piece)
        part[...] = weight_terms[:, pl.ds(first, piece), :].astype(part.dtype)


def halo_slots(message_left, message_right, quantities, slots):
    coefs, tables = [], []
    for message, tile in ((message_left, 2), (message_right, 0)):
        coefs.append(message[: quantities * slots, :].T)
        offset = message[quantities * slots : (quantities + 1) * slots, :].astype(jnp.int32)
        atom = lax.broadcasted_iota(jnp.int32, offset.shape, 1)
        tables.append(slot_tile(wide_transpose(offset + HALO + atom)[:, :slots], tile))
    return coefs, tables


def final_kernel(heads, slots, start, grad_query, own_key, own_value, halo_qkv, cl, cr,
                 message_left, message_right, wc, mine, theirs, token, grad):
    token[...] = jnp.zeros_like(token)
    comps, chan_local = halo_qkv.shape[0], cl.shape[1]
    rows = chan_local // heads
    stop = start + comps
    grad[:, :chan_local, :] = grad_query[start:stop]
    coefs, tables = halo_slots(message_left, message_right, 2 * heads, slots)
    for head in range(heads):
        span = slice(head * rows, (head + 1) * rows)
        query = head_rows_of(halo_qkv, head * rows, rows)
        sides = (
            (own_key, chan_local, head, (query[:, :HALO], query[:, HALO:])),
            (
                own_value,
                2 * chan_local,
                heads + head,
                tuple(side[start:stop, span, :].reshape(comps * rows, HALO) for side in (cl, cr)),
            ),
        )
        for own, first, quantity, outer in sides:
            rim = [
                nn(outer[at], spread(tables[at], coefs[at], quantity, slots)) for at in range(2)
            ]
            total = own[start:stop, span, :].reshape(comps * rows, 2 * HALO)
            total = total + jnp.concatenate(rim, axis=1)
            grad[:, first + head * rows : first + (head + 1) * rows, :] = (
                total.astype(BF16).reshape(comps, rows, 2 * HALO)
            )
    for comp in range(comps):
        total = nn(wc[degree_of(start + comp)], grad[comp])
        mine[comp] = total[:chan_local]
        theirs[comp] = total[chan_local:].astype(BF16)


def finish_kernel(*refs):
    out, start = refs[-1], 0
    for mine, theirs in zip(refs[:-1:2], refs[1:-1:2]):
        stop = start + mine.shape[0]
        out[start:stop] = (mine[...] + theirs[...].astype(F32)).astype(BF16)
        start = stop


def gather_kernel(place, part_0, part_1, part_2, part_3, out):
    piece = part_0.shape[1]
    spot = place[2]
    for delta, part in enumerate((part_0, part_1, part_2, part_3)):
        first = pl.multiple_of((spot ^ delta) * piece, piece)
        out[:, pl.ds(first, piece), :] = part[...].astype(F32)


def add_kernel(*refs):
    *parts, total, rounded = refs
    value = parts[0][...]
    for part in parts[1:]:
        value = value + part[...].astype(F32)
    total[...] = value
    rounded[...] = value.astype(BF16)


def call(kernel, args, outs, scratch=(), scalars=0, limit=24, stay=(), tokens=(), flops=0):
    whole = pl.BlockSpec(memory_space=pltpu.VMEM)
    small = pl.BlockSpec(memory_space=pltpu.SMEM)
    args = [
        pltpu.with_memory_space_constraint(a, pltpu.VMEM) if at in stay else a
        for at, a in enumerate(args)
    ]
    count = len(args)

    def body(*refs):
        kernel(*refs[:count], *refs[count + len(tokens) :])

    return pl.pallas_call(
        body,
        out_shape=tuple(outs),
        in_specs=[small] * scalars
        + [whole] * (count - scalars)
        + [pl.BlockSpec(memory_space=pl.ANY)] * len(tokens),
        out_specs=tuple([whole] * len(outs)),
        scratch_shapes=list(scratch),
        compiler_params=pltpu.CompilerParams(vmem_limit_bytes=limit * 1024 * 1024),
        cost_estimate=pl.CostEstimate(flops=flops, bytes_accessed=1024, transcendentals=0),
    )(*args, *tokens)


def after(values, tokens):
    anywhere = pl.BlockSpec(memory_space=pl.ANY)
    count = len(values)

    def kernel(*refs):
        pass

    return pl.pallas_call(
        kernel,
        out_shape=tuple(jax.ShapeDtypeStruct(v.shape, v.dtype) for v in values),
        in_specs=[anywhere] * (count + len(tokens)),
        out_specs=tuple([anywhere] * count),
        input_output_aliases={i: i for i in range(count)},
        compiler_params=pltpu.CompilerParams(vmem_limit_bytes=1024 * 1024),
        cost_estimate=pl.CostEstimate(flops=0, bytes_accessed=1024, transcendentals=0),
    )(*values, *tokens)


def shifted(value, axis, steps):
    count = lax.axis_size(axis)
    pairs = [(source, (source + steps) % count) for source in range(count)]
    return lax.ppermute(value, axis, pairs)


def exchanged(value, axis, offset):
    count = lax.axis_size(axis)
    return lax.ppermute(value, axis, [(source, source ^ offset) for source in range(count)])


def on_device(features, weights, cotangent, edge_bias, neighbours, valid_mask):
    chan_local, comps, atoms_dev = features.shape
    heads, slots = edge_bias.shape[0], edge_bias.shape[1]
    channels = weights.shape[2]
    assert atoms_dev == 2 * HALO and channels == 2 * chan_local
    score_scale = 1.0 / math.sqrt(chan_local // heads * comps)
    total_atoms = atoms_dev * lax.axis_size("atom")
    count = lax.axis_size("atom")
    assert count >= 4 and count & (count - 1) == 0
    atom_place = lax.axis_index("atom")
    cut_bits = (1, 2) if count >= 8 else (0, 1)
    spot = (atom_place >> cut_bits[0]) & 3
    place = jnp.stack([lax.axis_index("chan"), atom_place * atoms_dev, spot])
    place = place.astype(jnp.int32)
    feature_cut = comps // 2
    feature_cuts = ((0, feature_cut), (feature_cut, comps))

    def held(*dims, dtype=F32):
        return pltpu.VMEM(dims, dtype)

    def plain(*dims, dtype=F32):
        return jax.ShapeDtypeStruct(dims, dtype)

    fm = jnp.transpose(features, (1, 0, 2))
    cot = jnp.transpose(cotangent, (1, 0, 2))
    mix = jnp.transpose(weights, (0, 1, 3, 2))
    anywhere = pl.BlockSpec(memory_space=pl.ANY)
    rim_count = 2 * len(feature_cuts)
    feature_rims = pl.pallas_call(
        functools.partial(split_kernel, feature_cuts),
        out_shape=tuple(
            held(stop - start, chan_local, HALO, dtype=BF16)
            for start, stop in feature_cuts
            for _ in range(2)
        ),
        in_specs=[anywhere],
        out_specs=(pl.BlockSpec(memory_space=pltpu.VMEM),) * rim_count,
        scratch_shapes=[pltpu.SemaphoreType.DMA((rim_count,))],
        compiler_params=pltpu.CompilerParams(vmem_limit_bytes=4 * 1024 * 1024),
    )(pltpu.with_memory_space_constraint(fm, pltpu.HBM))
    from_sides = [
        shifted(rim, "atom", 1 if at % 2 == 0 else -1) for at, rim in enumerate(feature_rims)
    ]
    fo = shifted(fm, "chan", 1)

    qkv, scores, slot_own, index_rows, index_wide, wp, wc, token, *rims = call(
        functools.partial(own_kernel, heads, total_atoms),
        (place, fm, fo, cot, mix, neighbours),
        (
            held(comps, 3 * chan_local, atoms_dev, dtype=BF16),
            held(2 * heads, atoms_dev, atoms_dev),
            held(2, 3, HALO, HALO, dtype=jnp.int32),
            held(slots, atoms_dev, dtype=jnp.int32),
            held(atoms_dev, HALO, dtype=jnp.int32),
            held(LMAX + 1, 3 * chan_local, channels, dtype=BF16),
            held(LMAX + 1, channels, 3 * chan_local, dtype=BF16),
            plain(8, HALO),
            *(
                plain(comps, chan_local, HALO, dtype=BF16) for _ in range(2)
            ),
        ),
        scalars=1,
        stay=(1, 2, 3),
        flops=12 * 10**9,
    )
    flm, frm = after(from_sides[:2], (token,))
    early_chunk = (flm, shifted(flm, "chan", 1), frm, shifted(frm, "chan", 1))
    halo_a, partial, token = call(
        functools.partial(early_kernel, heads),
        (*early_chunk, wp, qkv, cot),
        (
            held(feature_cut, 3 * chan_local, atoms_dev, dtype=BF16),
            held(2 * heads, 2, HALO, HALO),
            plain(8, HALO),
        ),
        stay=tuple(range(7)),
    )
    rims = after(rims, (token,))
    late_sides = after(from_sides[2:], (token,))
    late_chunks = []
    for flm, frm in zip(late_sides[::2], late_sides[1::2]):
        late_chunks += [flm, shifted(flm, "chan", 1), frm, shifted(frm, "chan", 1)]
    from_left, from_right = shifted(rims[0], "atom", 1), shifted(rims[1], "atom", -1)
    halo_b, grad_bias, message_a, message_b = call(
        functools.partial(edge_kernel, heads, score_scale, feature_cut, len(late_chunks) // 4),
        (*late_chunks, wp, qkv, cot, scores, partial, edge_bias, valid_mask, index_rows, index_wide),
        (
            held(comps - feature_cut, 3 * chan_local, atoms_dev, dtype=BF16),
            plain(heads, slots, atoms_dev),
            held((2 * heads + 3) * slots, HALO),
            held((2 * heads + 3) * slots, HALO),
        ),
        stay=(*range(len(late_chunks) + 5), len(late_chunks) + 7, len(late_chunks) + 8),
    )
    message_left = shifted(message_b, "atom", 1)
    message_right = shifted(message_a, "atom", -1)
    piece = (3 * (LMAX + 1), chan_local // 4, channels)
    grad_query, own_key, own_value, kept, *sent = call(
        functools.partial(grads_kernel, heads, slots, len(feature_cuts)),
        (place, fm, fo, *early_chunk, *late_chunks, qkv, halo_a, halo_b, cot, slot_own, message_a,
         message_b),
        (
            held(comps, chan_local, atoms_dev, dtype=BF16),
            held(comps, chan_local, atoms_dev),
            held(comps, chan_local, atoms_dev),
            held(*piece),
            plain(*piece, dtype=BF16),
            plain(*piece, dtype=BF16),
            plain(*piece, dtype=BF16),
        ),
        scratch=[
            pltpu.VMEM((comps, 2 * chan_local, 2 * atoms_dev), BF16),
            pltpu.VMEM((3 * (LMAX + 1), chan_local, channels), F32),
        ],
        scalars=1,
        stay=tuple(range(1, 10 + 4 * len(feature_cuts))),
    )
    def summed(kept, parts):
        return call(
            add_kernel, (kept, *parts), (held(*piece), plain(*piece, dtype=BF16)), limit=8, stay=(0,)
        )

    def plainly(kept, parts):
        kept = functools.reduce(lambda total, part: total + part.astype(F32), parts, kept)
        return kept, kept.astype(BF16)

    arrived = [exchanged(part, "atom", delta << cut_bits[0]) for delta, part in enumerate(sent, 1)]
    kept, rounded = summed(kept, arrived)
    rest = [bit for bit in reversed(range(count.bit_length() - 1)) if bit not in cut_bits]
    for at, bit in enumerate(rest):
        final = 0 < at == len(rest) - 1
        also = 1 << rest[at - 1] if final else 0
        arrived = [exchanged(rounded, "atom", 1 << bit | also)]
        kept, rounded = (summed if final else plainly)(kept, arrived)
    pieces = [rounded] + [exchanged(rounded, "atom", d << cut_bits[0]) for d in range(1, 4)]
    (grad_weights,) = call(
        gather_kernel,
        (place, *pieces),
        (plain(3 * (LMAX + 1), chan_local, channels),),
        scalars=1,
        limit=8,
        flops=20 * 10**9,
    )
    parts, tokens = [], (rounded,)
    for (start, stop), halo_qkv in zip(feature_cuts, (halo_a, halo_b)):
        size = stop - start
        mine, theirs, token = call(
            functools.partial(final_kernel, heads, slots, start),
            (grad_query, own_key, own_value, halo_qkv, from_left, from_right, message_left,
             message_right, wc),
            (
                held(size, chan_local, atoms_dev),
                held(size, chan_local, atoms_dev, dtype=BF16),
                plain(8, HALO),
            ),
            scratch=[pltpu.VMEM((size, 3 * chan_local, atoms_dev), BF16)],
            limit=16,
            stay=(0, 1, 2, 3, 4, 5, 8),
            tokens=tokens,
        )
        parts += [mine, shifted(theirs, "chan", 1)]
        tokens = (token, pieces[2])
    (out,) = call(
        finish_kernel,
        parts,
        (plain(comps, chan_local, atoms_dev, dtype=BF16),),
        limit=8,
        stay=tuple(range(len(parts))),
    )
    grad_features = jnp.transpose(out, (1, 0, 2))
    grad_weights = grad_weights.reshape(3, LMAX + 1, chan_local, channels)
    grad_weights = jnp.transpose(grad_weights, (0, 1, 3, 2))
    return grad_features, grad_weights, grad_bias


def solution(mesh):
    in_specs = (
        P("chan", None, "atom"),
        P(None, None, None, "chan"),
        P("chan", None, "atom"),
        P("chan", None, "atom"),
        P(None, "atom"),
        P(None, "atom"),
    )
    out_specs = (P("chan", None, "atom"), P(None, None, None, "chan"), P("chan", None, "atom"))
    return jax.shard_map(
        on_device, mesh=mesh, in_specs=in_specs, out_specs=out_specs, check_vma=False
    )
```

```python
import functools
import math

import jax
import jax.numpy as jnp
from jax import lax
from jax.experimental import pallas as pl
from jax.experimental.pallas import tpu as pltpu
from jax.sharding import PartitionSpec as P

LMAX = 6
HALO = 128
SOFT_CAP = 10.0
F32 = jnp.float32
BF16 = jnp.bfloat16


def degree_of(comp):
    return math.isqrt(comp)


def nn(lhs, rhs):
    return lax.dot_general(lhs, rhs, (((1,), (0,)), ((), ())), preferred_element_type=F32)


def nt(lhs, rhs):
    return lax.dot_general(lhs, rhs, (((1,), (1,)), ((), ())), preferred_element_type=F32)


def tn(lhs, rhs):
    return lax.dot_general(lhs, rhs, (((0,), (0,)), ((), ())), preferred_element_type=F32)


def pick(table, index):
    return jnp.take_along_axis(table, index, axis=1, mode="promise_in_bounds")


def head_rows_of(ref, first_row, rows):
    block = ref[:, first_row : first_row + rows, :]
    return block.reshape(block.shape[0] * rows, block.shape[2])


def slot_tile(window_index, tile):
    atoms, slots = window_index.shape
    lane = lax.broadcasted_iota(jnp.int32, (atoms, HALO), 1) + tile * HALO
    found = jnp.full((atoms, HALO), -1, jnp.int32)
    for slot in range(slots):
        found = jnp.where(window_index[:, slot : slot + 1] == lane, slot, found)
    return found


def spread(slot, coef, quantity, slots):
    values = pick(coef, jnp.maximum(slot, 0) + quantity * slots)
    return jnp.where(slot >= 0, values, 0.0).astype(BF16)


def wide_transpose(rows):
    return jnp.concatenate([rows] * (HALO // rows.shape[0]), axis=0).T


def split_kernel(cuts, fm, *refs):
    *parts, sems = refs
    copies = []
    for at, part in enumerate(parts):
        start, stop = cuts[at // 2]
        atom = HALO if at % 2 == 0 else 0
        copies.append(
            pltpu.make_async_copy(
                fm.at[pl.ds(start, stop - start), :, pl.ds(atom, HALO)], part, sems.at[at]
            )
        )
    for copy in copies:
        copy.start()
    for copy in copies:
        copy.wait()


def own_kernel(heads, total_atoms, place, fm, fo, cot, weights, neighbours,
               qkv, scores, slot_own, index_rows, index_wide, wp, wc, token, *rims):
    token[...] = jnp.zeros_like(token)
    rims[0][...] = cot[:, :, HALO:]
    rims[1][...] = cot[:, :, :HALO]
    comps, chan_local = fm.shape[0], fm.shape[1]
    channels = weights.shape[3]
    rows = chan_local // heads
    slots = neighbours.shape[0]
    core, first_atom = place[0], place[1]
    for degree in range(LMAX + 1):
        mix = jnp.concatenate([weights[g, degree] for g in range(3)], axis=0).astype(F32)
        mix = jnp.where(core == 0, mix, pltpu.roll(mix, chan_local, 1))
        wp[degree] = mix.astype(BF16)
        padded = jnp.concatenate([mix, jnp.zeros((chan_local, channels), F32)], axis=0)
        wc[degree] = padded.T[:, : 3 * chan_local].astype(BF16)
    for comp in range(comps):
        feats = jnp.concatenate([fm[comp], fo[comp]], axis=0)
        qkv[comp] = nn(wp[degree_of(comp)], feats).astype(BF16)
    for head in range(heads):
        query = head_rows_of(qkv, head * rows, rows)
        key = head_rows_of(qkv, chan_local + head * rows, rows)
        value = head_rows_of(qkv, 2 * chan_local + head * rows, rows)
        scores[head] = tn(query, key)
        scores[heads + head] = tn(head_rows_of(cot, head * rows, rows), value)
    for half in range(2):
        span = slice(half * HALO, (half + 1) * HALO)
        index = neighbours[:, span] - (first_atom + (half - 1) * HALO)
        index = jnp.where(index < 0, index + total_atoms, index)
        index = jnp.where(index >= total_atoms, index - total_atoms, index)
        index_rows[:, span] = index
        wide = wide_transpose(index)
        index_wide[span, :] = wide
        for tile in range(3):
            slot_own[half, tile] = slot_tile(wide[:, :slots], tile)


def project_halo(start, chunks, wp, halo_qkv):
    at = 0
    for flm, flo, frm, fro in chunks:
        for comp in range(flm.shape[0]):
            feats = jnp.concatenate(
                [
                    jnp.concatenate([flm[comp], frm[comp]], axis=1),
                    jnp.concatenate([flo[comp], fro[comp]], axis=1),
                ],
                axis=0,
            )
            halo_qkv[at] = nn(wp[degree_of(start + at)], feats).astype(BF16)
            at += 1


def halo_scores(heads, quantity, start, qkv, cot, halo_qkv):
    size, chan_local = halo_qkv.shape[0], cot.shape[1]
    rows = chan_local // heads
    head = quantity % heads
    first = (1 if quantity < heads else 2) * chan_local + head * rows
    source = qkv if quantity < heads else cot
    mine = source[start : start + size, head * rows : (head + 1) * rows, :]
    mine = mine.reshape(size * rows, mine.shape[2])
    theirs = head_rows_of(halo_qkv, first, rows)
    return tn(mine[:, :HALO], theirs[:, :HALO]), tn(mine[:, HALO:], theirs[:, HALO:])


def early_kernel(heads, flm, flo, frm, fro, wp, qkv, cot, halo_qkv, partial, token):
    token[...] = jnp.zeros_like(token)
    project_halo(0, [(flm, flo, frm, fro)], wp, halo_qkv)
    for quantity in range(2 * heads):
        left, right = halo_scores(heads, quantity, 0, qkv, cot, halo_qkv)
        partial[quantity, 0] = left
        partial[quantity, 1] = right


def edge_kernel(heads, score_scale, start, late, *refs):
    chunks = [refs[at : at + 4] for at in range(0, 4 * late, 4)]
    (wp, qkv, cot, scores, partial, bias, valid, index_rows, index_wide,
     halo_qkv, grad_bias, message_a, message_b) = refs[4 * late :]
    slots = valid.shape[0]
    project_halo(start, chunks, wp, halo_qkv)
    lane = lax.broadcasted_iota(jnp.int32, (HALO, 2 * heads * slots), 1)
    gathered = [jnp.zeros((HALO, 2 * heads * slots), F32) for _ in range(2)]
    for quantity in range(2 * heads):
        left, right = halo_scores(heads, quantity, start, qkv, cot, halo_qkv)
        left, right = left + partial[quantity, 0], right + partial[quantity, 1]
        for half in range(2):
            own = scores[quantity, half * HALO : (half + 1) * HALO, :]
            own = [own[:, :HALO], own[:, HALO:]]
            tiles = [left] + own if half == 0 else own + [right]
            index = index_wide[half * HALO : (half + 1) * HALO, :]
            inner, tile_of = index & (HALO - 1), index >> 7
            values = jnp.where(
                tile_of == 0,
                pick(tiles[0], inner),
                jnp.where(tile_of == 1, pick(tiles[1], inner), pick(tiles[2], inner)),
            )
            gathered[half] = jnp.where(lane // slots == quantity, values, gathered[half])
    for half, message in enumerate((message_a, message_b)):
        span = slice(half * HALO, (half + 1) * HALO)
        edges = gathered[half].T.reshape(2, heads, slots, HALO)
        squashed = jnp.tanh(edges[0] * (score_scale / SOFT_CAP))
        logits = SOFT_CAP * squashed + bias[:, :, span]
        live = valid[:, span][None] > 0
        weight = jnp.where(live, jnp.exp(logits), 0.0)
        attention = weight / jnp.sum(weight, axis=1, keepdims=True)
        grad_attn = edges[1]
        grad_logit = attention * (
            grad_attn - jnp.sum(attention * grad_attn, axis=1, keepdims=True)
        )
        grad_bias[:, :, span] = grad_logit
        grad_raw = score_scale * grad_logit * (1.0 - squashed * squashed)
        index = index_rows[:, span]
        both = jnp.stack([grad_raw, attention]).reshape(2 * heads, slots, HALO)
        merged = jnp.zeros_like(both)
        for slot in range(slots):
            same = (index == index[slot : slot + 1, :])[None]
            merged = merged + jnp.where(same, both[:, slot : slot + 1, :], 0.0)
        atom = lax.broadcasted_iota(jnp.int32, (slots, HALO), 1)
        edge_rows = 2 * heads * slots
        message[:edge_rows, :] = merged.reshape(edge_rows, HALO)
        message[edge_rows : edge_rows + slots, :] = (index - HALO - atom).astype(F32)
        message[edge_rows + slots :, :] = jnp.zeros_like(message[edge_rows + slots :, :])


def joined_rows(early, late, first_row, rows):
    return jnp.concatenate(
        [head_rows_of(early, first_row, rows), head_rows_of(late, first_row, rows)], axis=0
    )


def grads_kernel(heads, slots, pieces, place, fm, fo, *refs):
    chunks = [refs[at : at + 4] for at in range(0, 4 * pieces, 4)]
    (qkv, halo_a, halo_b, cot, slot_own, message_a, message_b, grad_query, own_key, own_value, kept,
     sent_1, sent_2, sent_3, ext, weight_terms) = refs[4 * pieces :]
    places = [(chunk, at) for chunk in chunks for at in range(chunk[0].shape[0])]
    comps, chan_local = fm.shape[0], fm.shape[1]
    rows = chan_local // heads
    atoms = 2 * HALO
    core = place[0]
    empty = jnp.zeros((HALO, HALO), BF16)
    coefs = [message[: 2 * heads * slots, :].T for message in (message_a, message_b)]
    for head in range(heads):
        tables = []
        for quantity in (head, heads + head):
            halves = []
            for half in range(2):
                tiles = [spread(slot_own[half, t], coefs[half], quantity, slots) for t in range(3)]
                tiles = tiles + [empty] if half == 0 else [empty] + tiles
                halves.append(jnp.concatenate(tiles, axis=1))
            tables.append(jnp.concatenate(halves, axis=0))
        raw_table, attn_table = tables
        query = head_rows_of(qkv, head * rows, rows)
        key = head_rows_of(qkv, chan_local + head * rows, rows)
        halo_key = joined_rows(halo_a, halo_b, chan_local + head * rows, rows)
        key_ext = jnp.concatenate([halo_key[:, :HALO], key, halo_key[:, HALO:]], axis=1)
        span = slice(head * rows, (head + 1) * rows)
        value_span = slice(chan_local + head * rows, chan_local + (head + 1) * rows)
        grad_query[:, span, :] = nt(key_ext, raw_table).astype(BF16).reshape(comps, rows, atoms)
        key_sums = nn(query, raw_table)
        own_key[:, span, :] = key_sums[:, HALO : HALO + atoms].reshape(comps, rows, atoms)
        ext[:, span, :] = key_sums.astype(BF16).reshape(comps, rows, atoms + 2 * HALO)
        value_sums = nn(head_rows_of(cot, head * rows, rows), attn_table)
        own_value[:, span, :] = value_sums[:, HALO : HALO + atoms].reshape(comps, rows, atoms)
        ext[:, value_span, :] = value_sums.astype(BF16).reshape(comps, rows, atoms + 2 * HALO)
    for degree in range(LMAX + 1):
        query_total = jnp.zeros((chan_local, 2 * chan_local), F32)
        keyval_total = jnp.zeros((2 * chan_local, 2 * chan_local), F32)
        for comp in range(degree * degree, (degree + 1) * (degree + 1)):
            own = jnp.concatenate([fm[comp], fo[comp]], axis=0)
            (flm, flo, frm, fro), at = places[comp]
            wide = jnp.concatenate(
                [
                    jnp.concatenate([flm[at], fm[comp], frm[at]], axis=1),
                    jnp.concatenate([flo[at], fo[comp], fro[at]], axis=1),
                ],
                axis=0,
            )
            query_total = query_total + nt(grad_query[comp], own)
            keyval_total = keyval_total + nt(ext[comp], wide)
        total = jnp.concatenate([query_total, keyval_total], axis=0)
        total = jnp.where(core == 0, total, pltpu.roll(total, chan_local, 1))
        for g in range(3):
            weight_terms[g * (LMAX + 1) + degree] = total[g * chan_local : (g + 1) * chan_local]
    piece = chan_local // 4
    spot = place[2]
    for delta, part in enumerate((kept, sent_1, sent_2, sent_3)):
        first = pl.multiple_of((spot ^ delta) * piece, piece)
        part[...] = weight_terms[:, pl.ds(first, piece), :].astype(part.dtype)


def halo_slots(message_left, message_right, quantities, slots):
    coefs, tables = [], []
    for message, tile in ((message_left, 2), (message_right, 0)):
        coefs.append(message[: quantities * slots, :].T)
        offset = message[quantities * slots : (quantities + 1) * slots, :].astype(jnp.int32)
        atom = lax.broadcasted_iota(jnp.int32, offset.shape, 1)
        tables.append(slot_tile(wide_transpose(offset + HALO + atom)[:, :slots], tile))
    return coefs, tables


def final_kernel(heads, slots, start, grad_query, own_key, own_value, halo_qkv, cl, cr,
                 message_left, message_right, wc, mine, theirs, token, grad):
    token[...] = jnp.zeros_like(token)
    comps, chan_local = halo_qkv.shape[0], cl.shape[1]
    rows = chan_local // heads
    stop = start + comps
    grad[:, :chan_local, :] = grad_query[start:stop]
    coefs, tables = halo_slots(message_left, message_right, 2 * heads, slots)
    for head in range(heads):
        span = slice(head * rows, (head + 1) * rows)
        query = head_rows_of(halo_qkv, head * rows, rows)
        sides = (
            (own_key, chan_local, head, (query[:, :HALO], query[:, HALO:])),
            (
                own_value,
                2 * chan_local,
                heads + head,
                tuple(side[start:stop, span, :].reshape(comps * rows, HALO) for side in (cl, cr)),
            ),
        )
        for own, first, quantity, outer in sides:
            rim = [
                nn(outer[at], spread(tables[at], coefs[at], quantity, slots)) for at in range(2)
            ]
            total = own[start:stop, span, :].reshape(comps * rows, 2 * HALO)
            total = total + jnp.concatenate(rim, axis=1)
            grad[:, first + head * rows : first + (head + 1) * rows, :] = (
                total.astype(BF16).reshape(comps, rows, 2 * HALO)
            )
    for comp in range(comps):
        total = nn(wc[degree_of(start + comp)], grad[comp])
        mine[comp] = total[:chan_local]
        theirs[comp] = total[chan_local:].astype(BF16)


def finish_kernel(place, part_0, part_1, part_2, part_3, *refs):
    *sides, out, weight_out = refs
    piece = part_0.shape[1]
    for delta, part in enumerate((part_0, part_1, part_2, part_3)):
        first = pl.multiple_of((place[2] ^ delta) * piece, piece)
        weight_out[:, pl.ds(first, piece), :] = part[...].astype(F32)
    start = 0
    for mine, theirs in zip(sides[::2], sides[1::2]):
        stop = start + mine.shape[0]
        out[start:stop] = (mine[...] + theirs[...].astype(F32)).astype(BF16)
        start = stop


def add_kernel(*refs):
    *parts, total, rounded = refs
    value = parts[0][...]
    for part in parts[1:]:
        value = value + part[...].astype(F32)
    total[...] = value
    rounded[...] = value.astype(BF16)


def call(kernel, args, outs, scratch=(), scalars=0, limit=24, stay=(), tokens=(), flops=0):
    whole = pl.BlockSpec(memory_space=pltpu.VMEM)
    small = pl.BlockSpec(memory_space=pltpu.SMEM)
    args = [
        pltpu.with_memory_space_constraint(a, pltpu.VMEM) if at in stay else a
        for at, a in enumerate(args)
    ]
    count = len(args)

    def body(*refs):
        kernel(*refs[:count], *refs[count + len(tokens) :])

    return pl.pallas_call(
        body,
        out_shape=tuple(outs),
        in_specs=[small] * scalars
        + [whole] * (count - scalars)
        + [pl.BlockSpec(memory_space=pl.ANY)] * len(tokens),
        out_specs=tuple([whole] * len(outs)),
        scratch_shapes=list(scratch),
        compiler_params=pltpu.CompilerParams(vmem_limit_bytes=limit * 1024 * 1024),
        cost_estimate=pl.CostEstimate(flops=flops, bytes_accessed=1024, transcendentals=0),
    )(*args, *tokens)


def after(values, tokens):
    anywhere = pl.BlockSpec(memory_space=pl.ANY)
    count = len(values)

    def kernel(*refs):
        pass

    return pl.pallas_call(
        kernel,
        out_shape=tuple(jax.ShapeDtypeStruct(v.shape, v.dtype) for v in values),
        in_specs=[anywhere] * (count + len(tokens)),
        out_specs=tuple([anywhere] * count),
        input_output_aliases={i: i for i in range(count)},
        compiler_params=pltpu.CompilerParams(vmem_limit_bytes=1024 * 1024),
        cost_estimate=pl.CostEstimate(flops=0, bytes_accessed=1024, transcendentals=0),
    )(*values, *tokens)


def shifted(value, axis, steps):
    count = lax.axis_size(axis)
    pairs = [(source, (source + steps) % count) for source in range(count)]
    return lax.ppermute(value, axis, pairs)


def exchanged(value, axis, offset):
    count = lax.axis_size(axis)
    return lax.ppermute(value, axis, [(source, source ^ offset) for source in range(count)])


def on_device(features, weights, cotangent, edge_bias, neighbours, valid_mask):
    chan_local, comps, atoms_dev = features.shape
    heads, slots = edge_bias.shape[0], edge_bias.shape[1]
    channels = weights.shape[2]
    assert atoms_dev == 2 * HALO and channels == 2 * chan_local
    score_scale = 1.0 / math.sqrt(chan_local // heads * comps)
    total_atoms = atoms_dev * lax.axis_size("atom")
    count = lax.axis_size("atom")
    assert count >= 4 and count & (count - 1) == 0
    atom_place = lax.axis_index("atom")
    cut_bits = (1, 2) if count >= 8 else (0, 1)
    spot = (atom_place >> cut_bits[0]) & 3
    place = jnp.stack([lax.axis_index("chan"), atom_place * atoms_dev, spot])
    place = place.astype(jnp.int32)
    feature_cut = comps // 2
    feature_cuts = ((0, feature_cut), (feature_cut, comps))

    def held(*dims, dtype=F32):
        return pltpu.VMEM(dims, dtype)

    def plain(*dims, dtype=F32):
        return jax.ShapeDtypeStruct(dims, dtype)

    fm = jnp.transpose(features, (1, 0, 2))
    cot = jnp.transpose(cotangent, (1, 0, 2))
    mix = jnp.transpose(weights, (0, 1, 3, 2))
    anywhere = pl.BlockSpec(memory_space=pl.ANY)
    rim_count = 2 * len(feature_cuts)
    feature_rims = pl.pallas_call(
        functools.partial(split_kernel, feature_cuts),
        out_shape=tuple(
            held(stop - start, chan_local, HALO, dtype=BF16)
            for start, stop in feature_cuts
            for _ in range(2)
        ),
        in_specs=[anywhere],
        out_specs=(pl.BlockSpec(memory_space=pltpu.VMEM),) * rim_count,
        scratch_shapes=[pltpu.SemaphoreType.DMA((rim_count,))],
        compiler_params=pltpu.CompilerParams(vmem_limit_bytes=4 * 1024 * 1024),
    )(pltpu.with_memory_space_constraint(fm, pltpu.HBM))
    from_sides = [
        shifted(rim, "atom", 1 if at % 2 == 0 else -1) for at, rim in enumerate(feature_rims)
    ]
    fo = shifted(fm, "chan", 1)

    qkv, scores, slot_own, index_rows, index_wide, wp, wc, token, *rims = call(
        functools.partial(own_kernel, heads, total_atoms),
        (place, fm, fo, cot, mix, neighbours),
        (
            held(comps, 3 * chan_local, atoms_dev, dtype=BF16),
            held(2 * heads, atoms_dev, atoms_dev),
            held(2, 3, HALO, HALO, dtype=jnp.int32),
            held(slots, atoms_dev, dtype=jnp.int32),
            held(atoms_dev, HALO, dtype=jnp.int32),
            held(LMAX + 1, 3 * chan_local, channels, dtype=BF16),
            held(LMAX + 1, channels, 3 * chan_local, dtype=BF16),
            plain(8, HALO),
            *(
                plain(comps, chan_local, HALO, dtype=BF16) for _ in range(2)
            ),
        ),
        scalars=1,
        stay=(1, 2, 3),
        flops=12 * 10**9,
    )
    flm, frm = after(from_sides[:2], (token,))
    early_chunk = (flm, shifted(flm, "chan", 1), frm, shifted(frm, "chan", 1))
    halo_a, partial, token = call(
        functools.partial(early_kernel, heads),
        (*early_chunk, wp, qkv, cot),
        (
            held(feature_cut, 3 * chan_local, atoms_dev, dtype=BF16),
            held(2 * heads, 2, HALO, HALO),
            plain(8, HALO),
        ),
        stay=tuple(range(7)),
    )
    rims = after(rims, (token,))
    late_sides = after(from_sides[2:], (token,))
    late_chunks = []
    for flm, frm in zip(late_sides[::2], late_sides[1::2]):
        late_chunks += [flm, shifted(flm, "chan", 1), frm, shifted(frm, "chan", 1)]
    from_left, from_right = shifted(rims[0], "atom", 1), shifted(rims[1], "atom", -1)
    halo_b, grad_bias, message_a, message_b = call(
        functools.partial(edge_kernel, heads, score_scale, feature_cut, len(late_chunks) // 4),
        (*late_chunks, wp, qkv, cot, scores, partial, edge_bias, valid_mask, index_rows, index_wide),
        (
            held(comps - feature_cut, 3 * chan_local, atoms_dev, dtype=BF16),
            plain(heads, slots, atoms_dev),
            held((2 * heads + 3) * slots, HALO),
            held((2 * heads + 3) * slots, HALO),
        ),
        stay=(*range(len(late_chunks) + 5), len(late_chunks) + 7, len(late_chunks) + 8),
    )
    message_left = shifted(message_b, "atom", 1)
    message_right = shifted(message_a, "atom", -1)
    piece = (3 * (LMAX + 1), chan_local // 4, channels)
    grad_query, own_key, own_value, kept, *sent = call(
        functools.partial(grads_kernel, heads, slots, len(feature_cuts)),
        (place, fm, fo, *early_chunk, *late_chunks, qkv, halo_a, halo_b, cot, slot_own, message_a,
         message_b),
        (
            held(comps, chan_local, atoms_dev, dtype=BF16),
            held(comps, chan_local, atoms_dev),
            held(comps, chan_local, atoms_dev),
            held(*piece),
            plain(*piece, dtype=BF16),
            plain(*piece, dtype=BF16),
            plain(*piece, dtype=BF16),
        ),
        scratch=[
            pltpu.VMEM((comps, 2 * chan_local, 2 * atoms_dev), BF16),
            pltpu.VMEM((3 * (LMAX + 1), chan_local, channels), F32),
        ],
        scalars=1,
        stay=tuple(range(1, 10 + 4 * len(feature_cuts))),
    )
    def summed(kept, parts):
        return call(
            add_kernel, (kept, *parts), (held(*piece), plain(*piece, dtype=BF16)), limit=8, stay=(0,)
        )

    def plainly(kept, parts):
        kept = functools.reduce(lambda total, part: total + part.astype(F32), parts, kept)
        return kept, kept.astype(BF16)

    arrived = [exchanged(part, "atom", delta << cut_bits[0]) for delta, part in enumerate(sent, 1)]
    kept, rounded = summed(kept, arrived)
    rest = [bit for bit in reversed(range(count.bit_length() - 1)) if bit not in cut_bits]
    for at, bit in enumerate(rest):
        final = 0 < at == len(rest) - 1
        also = 1 << rest[at - 1] if final else 0
        arrived = [exchanged(rounded, "atom", 1 << bit | also)]
        kept, rounded = (summed if final else plainly)(kept, arrived)
    pieces = [rounded] + [exchanged(rounded, "atom", d << cut_bits[0]) for d in range(1, 4)]
    parts, tokens = [], (rounded,)
    for (start, stop), halo_qkv in zip(feature_cuts, (halo_a, halo_b)):
        size = stop - start
        mine, theirs, token = call(
            functools.partial(final_kernel, heads, slots, start),
            (grad_query, own_key, own_value, halo_qkv, from_left, from_right, message_left,
             message_right, wc),
            (
                held(size, chan_local, atoms_dev),
                held(size, chan_local, atoms_dev, dtype=BF16),
                plain(8, HALO),
            ),
            scratch=[pltpu.VMEM((size, 3 * chan_local, atoms_dev), BF16)],
            limit=16,
            stay=(0, 1, 2, 3, 4, 5, 8),
            tokens=tokens,
        )
        parts += [mine, shifted(theirs, "chan", 1)]
        tokens = (token, *pieces[1:])
    out, grad_weights = call(
        finish_kernel,
        (place, *pieces, *parts),
        (
            plain(comps, chan_local, atoms_dev, dtype=BF16),
            plain(3 * (LMAX + 1), chan_local, channels),
        ),
        scalars=1,
        limit=8,
        stay=tuple(range(5, 5 + len(parts))),
        flops=0,
    )
    grad_features = jnp.transpose(out, (1, 0, 2))
    grad_weights = grad_weights.reshape(3, LMAX + 1, chan_local, channels)
    grad_weights = jnp.transpose(grad_weights, (0, 1, 3, 2))
    return grad_features, grad_weights, grad_bias


def solution(mesh):
    in_specs = (
        P("chan", None, "atom"),
        P(None, None, None, "chan"),
        P("chan", None, "atom"),
        P("chan", None, "atom"),
        P(None, "atom"),
        P(None, "atom"),
    )
    out_specs = (P("chan", None, "atom"), P(None, None, None, "chan"), P("chan", None, "atom"))
    return jax.shard_map(
        on_device, mesh=mesh, in_specs=in_specs, out_specs=out_specs, check_vma=False
    )
```
